32 devices in a mesh: replica: 2 (over y), shard: 16 (over z, x, core).
Axes of the slice: x: 2, y: 2, z: 4, core: 2. Of those that a mesh axis runs over, the one named last changes fastest.
Arguments:
- tokens: bfloat16 [4096, 1024], P(('replica', 'shard')), may hold values from -6 to 6
- norm_gain: bfloat16 [1024], P('shard'), may hold values from 0.5 to 1.5
- w_inner: bfloat16 [1024, 2048], P(None, 'shard'), may hold values from -0.1875 to 0.1875
- w_gate: bfloat16 [1024, 2048], P(None, 'shard'), may hold values from -0.1875 to 0.1875
- conv_weight: bfloat16 [4, 2048], P(None, 'shard'), may hold values from -3 to 3
- conv_bias: bfloat16 [2048], P('shard'), may hold values from -3 to 3
- w_proj: bfloat16 [2048, 96], P('shard'), may hold values from -0.125 to 0.125
- w_step: bfloat16 [64, 2048], P(None, 'shard'), may hold values from -0.75 to 0.75
- step_bias: bfloat16 [2048], P('shard'), may hold values from -6.5 to -2.296875
- a_log: bfloat16 [16, 2048], P(None, 'shard'), may hold values from 0 to 2.765625
- skip_gain: bfloat16 [2048], P('shard'), may hold values from 0.5 to 1.5
- w_out: bfloat16 [2048, 1024], P('shard'), may hold values from -0.125 to 0.125
- cotangent: bfloat16 [4096, 1024], P(('replica', 'shard')), may hold values from -6 to 6
- lengths: int32 [32], P(('replica', 'shard')), may hold values from 32 to 128, as said below
Outputs:
- output: bfloat16 [4096, 1024], P(('replica', 'shard'))
- grad_tokens: float32 [4096, 1024], P(('replica', 'shard'))
- grad_norm_gain: float32 [1024], P('shard')
- grad_w_inner: float32 [1024, 2048], P(None, 'shard')
- grad_w_gate: float32 [1024, 2048], P(None, 'shard')
- grad_conv_weight: float32 [4, 2048], P(None, 'shard')
- grad_conv_bias: float32 [2048], P('shard')
- grad_w_proj: float32 [2048, 96], P('shard')
- grad_w_step: float32 [64, 2048], P(None, 'shard')
- grad_step_bias: float32 [2048], P('shard')
- grad_a_log: float32 [16, 2048], P(None, 'shard')
- grad_skip_gain: float32 [2048], P('shard')
- grad_w_out: float32 [2048, 1024], P('shard')
The draws below stay inside these ranges and needn't reach their ends.
Inputs may be any that keep to these rules, and one draw needn't show every extreme that they name: lengths[i] is the number of valid positions at the start of slot i, the rest of the slot being padding; some slot has exactly 128 and some other exactly 32.
All inputs are finite; a program needn't handle non-finite values.
Results may differ from the reference program's by a relative error of at most 0.02.
Values may be sent and summed in bfloat16 or wider, within the bound.
A program may use at most 192 MiB of HBM per device.

```python
from functools import partial
import jax
import jax.numpy as jnp
from jax import lax

D = 1024
E = 2048
RANK = 64
STATE = 16
CONV = 4
SLOT = 128
BLOCK = 64
SLOTS = 32
TOKENS = 4096


def draw_lengths(key, part):
    key = jax.random.fold_in(key, 7)
    key_fill, key_long, key_hop = jax.random.split(key, 3)
    lengths_all = jax.random.randint(key_fill, (SLOTS,), SLOT // 4, SLOT + 1, dtype=jnp.int32)
    longest = jax.random.randint(key_long, (), 0, SLOTS, dtype=jnp.int32)
    distance = jax.random.randint(key_hop, (), 1, SLOTS, dtype=jnp.int32)
    shortest = (longest + distance) % SLOTS
    positions = jnp.arange(SLOTS, dtype=jnp.int32)
    lengths_all = jnp.where(positions == longest, SLOT, lengths_all)
    lengths_all = jnp.where(positions == shortest, SLOT // 4, lengths_all)
    return lengths_all.astype(jnp.int32)


def block_levels(rng, shape, cuts, least, top_value):
    def one(axis_at, blocks):
        steps = jax.random.uniform(jax.random.fold_in(jax.random.fold_in(rng, 6), axis_at), (blocks,), jnp.float32, least / len(cuts), top_value / len(cuts))
        return jnp.repeat(jnp.exp(steps), shape[axis_at] // blocks).reshape((-1,) + (1,) * (len(shape) - axis_at - 1))

    gain = one(*cuts[0])
    for cut in cuts[1:]:
        gain = gain * one(*cut)
    return gain


def centred(own_key, shape, width, bound, cuts=(), kind=jnp.bfloat16):
    array = width * jax.random.normal(own_key, shape, jnp.float32)
    if cuts:
        array = array * block_levels(own_key, shape, cuts, -0.22, 0.18)
    return jnp.clip(array, -bound, bound).astype(kind)


def setup_inputs(seed: int = 0) -> dict:
    key_of = jax.random.split(jax.random.key(seed), 15)
    tokens = centred(key_of[0], (TOKENS, D), 1.0, 6.0, ((0, 32),))
    norm_gain = jnp.clip(1.0 + 0.1 * jax.random.normal(key_of[1], (D,), jnp.float32), 0.5, 1.5).astype(jnp.bfloat16)
    w_inner = centred(key_of[2], (D, E), D ** -0.5, 0.1875, ((1, 16),))
    w_gate = centred(key_of[3], (D, E), D ** -0.5, 0.1875, ((1, 16),))
    conv_weight = centred(key_of[4], (CONV, E), CONV ** -0.5, 3.0, ((1, 16),))
    conv_bias = centred(key_of[5], (E,), 0.5, 3.0, ((0, 16),))
    w_proj = centred(key_of[6], (E, RANK + 2 * STATE), E ** -0.5, 0.125, ((0, 16),))
    w_step = centred(key_of[7], (RANK, E), RANK ** -0.5, 0.75, ((1, 16),))
    step_bias = jnp.clip(-6.5 + 4.203125 * jax.random.uniform(key_of[8], (E,), jnp.float32) ** block_levels(key_of[8], (E,), ((0, 16),), -0.2, 0.2), -6.5, -2.296875).astype(jnp.bfloat16)
    a_log = jnp.clip(2.765625 * jax.random.uniform(key_of[9], (STATE, E), jnp.float32) ** block_levels(key_of[9], (STATE, E), ((1, 16),), -0.2, 0.2), 0.0, 2.765625).astype(jnp.bfloat16)
    skip_gain = jnp.clip(0.5 + 1.0 * jax.random.uniform(key_of[10], (E,), jnp.float32) ** block_levels(key_of[10], (E,), ((0, 16),), -0.2, 0.2), 0.5, 1.5).astype(jnp.bfloat16)
    w_out = centred(key_of[11], (E, D), E ** -0.5, 0.125, ((0, 16),))
    cotangent = centred(key_of[12], (TOKENS, D), 1.0, 6.0, ((0, 32),))
    lengths = draw_lengths(jax.random.fold_in(key_of[14], 71), 0)
    return dict(tokens=tokens, norm_gain=norm_gain, w_inner=w_inner, w_gate=w_gate, conv_weight=conv_weight, conv_bias=conv_bias, w_proj=w_proj, w_step=w_step, step_bias=step_bias, a_log=a_log, skip_gain=skip_gain, w_out=w_out, cotangent=cotangent, lengths=lengths)


EPS = 1e-05
HIGH = lax.Precision.HIGHEST

@jax.custom_vjp
def low(v):
    return lax.optimization_barrier(v.astype(jnp.bfloat16)).astype(jnp.float32)

@jax.custom_vjp
def low_back(v):
    return v

def low_keep(v):
    return (low(v), None)

def low_pass(kept, grad):
    return (grad,)

def back_keep(v):
    return (v, None)

def back_low(kept, grad):
    return (low(grad),)
low.defvjp(low_keep, low_pass)
low_back.defvjp(back_keep, back_low)

def matmul(left, right):
    return jnp.dot(left, right, precision=HIGH, preferred_element_type=jnp.float32)

def combine(earlier, later):
    return (earlier[0] * later[0], later[0] * earlier[1] + later[1])

def scan_block(start_state, pieces, decay_rates):
    step_size, in_map, out_map, conv_out = pieces
    decays = jnp.exp(step_size[:, None, :] * decay_rates[None, :, :])
    driven = step_size[:, None, :] * in_map[:, :, None] * conv_out[:, None, :]
    driven = driven.at[0].add(decays[0] * start_state)
    states = lax.associative_scan(combine, (decays, driven), axis=0)[1]
    mixed_out = jnp.einsum('tn,tne->te', out_map, states, precision=HIGH)
    return (states[-1], mixed_out)

def selective_scan(step_size, in_map, out_map, conv_out, decay_rates):
    blocks = step_size.shape[0] // BLOCK
    pieces = tuple((tensor.reshape(blocks, BLOCK, tensor.shape[1]) for tensor in (step_size, in_map, out_map, conv_out)))
    stepper = jax.checkpoint(partial(scan_block, decay_rates=decay_rates))
    initial = jnp.zeros((STATE, conv_out.shape[1]), jnp.float32)
    _, outputs = lax.scan(stepper, initial, pieces)
    return outputs.reshape(step_size.shape[0], conv_out.shape[1])

def slot_forward(residual, valid_mask, norm_gain, w_inner, w_gate, conv_weight, conv_bias, w_proj, w_step, step_bias, a_log, skip_gain, w_out):
    inv_rms = lax.rsqrt(lax.optimization_barrier(jnp.mean(residual * residual, axis=-1, keepdims=True)) + EPS)
    normed = low(residual * inv_rms * norm_gain)
    inner_pre = low_back(matmul(normed, w_inner))
    gate_pre = low_back(matmul(normed, w_gate))
    padded = jnp.pad(inner_pre, ((CONV - 1, 0), (0, 0)))
    conv_pre = jnp.broadcast_to(conv_bias, inner_pre.shape)
    for offset in range(CONV):
        conv_pre = conv_pre + conv_weight[offset] * padded[offset:offset + SLOT]
    conv_out = jax.nn.silu(conv_pre)
    conv_low = low(conv_out)
    projected = low_back(matmul(conv_low, w_proj))
    step_low = low(projected[:, :RANK])
    in_map = projected[:, RANK:RANK + STATE]
    out_map = projected[:, RANK + STATE:]
    step_size = jax.nn.softplus(low_back(matmul(step_low, w_step)) + step_bias)
    decay_rates = -jnp.exp(a_log)
    scanned = selective_scan(step_size, in_map, out_map, conv_out, decay_rates)
    mixed_out = scanned + skip_gain * conv_out
    gated_out = low(mixed_out * jax.nn.silu(gate_pre))
    branch = low_back(matmul(gated_out, w_out))
    return residual + valid_mask[:, None] * branch

def reference(tokens, norm_gain, w_inner, w_gate, conv_weight, conv_bias, w_proj, w_step, step_bias, a_log, skip_gain, w_out, cotangent, lengths):
    positions = jnp.arange(SLOT, dtype=jnp.int32)
    slot_masks = (positions[None, :] < lengths[:, None].astype(jnp.int32)).astype(jnp.float32)
    params = tuple((tensor.astype(jnp.float32) for tensor in (norm_gain, w_inner, w_gate, conv_weight, conv_bias, w_proj, w_step, step_bias, a_log, skip_gain, w_out)))
    inputs = tokens.astype(jnp.float32).reshape(SLOTS, SLOT, D)

    def whole_layer(inputs, *params):
        slot_step = jax.checkpoint(slot_forward)
        return lax.map(lambda pieces: slot_step(pieces[0], pieces[1], *params), (inputs, slot_masks))
    outputs, pullback = jax.vjp(whole_layer, inputs, *params)
    gradients = pullback(cotangent.astype(jnp.float32).reshape(SLOTS, SLOT, D))
    return (outputs.reshape(TOKENS, D).astype(jnp.bfloat16), gradients[0].reshape(TOKENS, D), gradients[1], gradients[2], gradients[3], gradients[4], gradients[5], gradients[6], gradients[7], gradients[8], gradients[9], gradients[10], gradients[11])
```

```python
import functools
import math
from types import SimpleNamespace

import jax
import jax.numpy as jnp
from jax import lax
from jax.experimental import pallas as pl
from jax.experimental.pallas import tpu as pltpu
from jax.sharding import PartitionSpec as P

RANK = 64
STATE = 16
CONV = 4
SLOT = 128
EPS = 1e-05
LN2 = math.log(2.0)
PACK = 96
MESH = pl.DeviceIdType.MESH
F32 = jnp.float32
BF16 = jnp.bfloat16


def nt(left, right):
    return lax.dot_general(left, right, (((1,), (1,)), ((), ())), preferred_element_type=F32)


def nn(left, right):
    return lax.dot_general(left, right, (((1,), (0,)), ((), ())), preferred_element_type=F32)


def tn(left, right):
    return lax.dot_general(left, right, (((0,), (0,)), ((), ())), preferred_element_type=F32)


def buffers(depth, hl, width, shards, piece):
    cols = depth * hl
    rows = 8 * SLOT
    reduce_small = dict(
        s1=((4, SLOT, 128), BF16),
        l1=((4, SLOT, 128), BF16),
        s2=((4, SLOT, 128), BF16),
        l2=((4, SLOT, 128), BF16),
        s3=((4, SLOT, 128), BF16),
        l3=((4, SLOT, 128), BF16),
        own=((4, SLOT, 128), F32),
        oth=((4, SLOT, 128), F32),
    )
    reduce_large = dict(
        s1=((4, SLOT, width), BF16),
        l1=((4, SLOT, width), BF16),
        sx=((2, SLOT // 2, width), BF16),
        sy=((2, SLOT // 2, width), BF16),
        lx=((2, SLOT // 2, width), BF16),
        ly=((2, SLOT // 2, width), BF16),
        tx=((SLOT // 2, width), BF16),
        ty=((SLOT // 2, width), BF16),
        mx=((SLOT // 2, width), BF16),
        my=((SLOT // 2, width), BF16),
    )
    shapes = dict(
        wt=((3, depth, hl, width), BF16),
        ws=((2, cols, width), BF16),
        pka=((depth, PACK, 128), BF16),
        wpa=((depth, hl, 128), BF16),
        gb=((depth, 2, 2, 8, 128), F32),
        gl=((1, width), F32),
        nb=((4, 2, SLOT, width), BF16),
        db=((4, 2, SLOT, width), BF16),
        pkl=((PACK, cols), F32),
        wst=((128, cols), BF16),
        rate=((STATE, 2, 8, 128), F32),
        ip=((8, SLOT + 8, cols), F32),
        dcp=((SLOT + 8, cols), F32),
        tm=((rows, 128), F32),
        spread=((rows, 256), BF16),
        sel=((256, 2 * STATE * 128), BF16),
        bc=((SLOT, 2 * STATE, 8, 128), F32),
        sall=((SLOT + 2, STATE, 16, 128), BF16),
        cl=((8, SLOT, cols), BF16),
        xc=((2, rows, 128), F32),
        pp=((4, 2, SLOT, 128), F32),
        slow=((rows, 128), BF16),
        dpj=((rows, 128), BF16),
        dt=((2, rows, 128), F32),
        ys=((2, rows, 128), F32),
        dm=((2, rows, 128), F32),
        ga=((STATE, 2, 8, 128), F32),
        go=((4, 2, SLOT, cols), BF16),
        dg=((4, 2, SLOT, cols), BF16),
        di=((4, 2, SLOT, cols), BF16),
        dsl=((8, SLOT, cols), BF16),
        tt=((cols, rows), BF16),
        gws=((3, depth, hl, width), BF16),
        gwl=((3, depth - 1, hl, width), BF16),
        gys=((3, hl, width), BF16),
        gyl=((3, hl, width), BF16),
        sg=((PACK, cols), F32),
        sgs=((depth, PACK, 128), BF16),
        sgl=((depth - 1, PACK, 128), BF16),
        sgt=((PACK, 128), BF16),
        sgy=((PACK, 128), BF16),
        gps=((depth, hl, 128), BF16),
        gpl=((depth - 1, hl, 128), BF16),
        gpt=((hl, 128), BF16),
        gpy=((hl, 128), BF16),
        vv=((1, width), F32),
        sum=((4, SLOT, width), F32),
        vs=((4, 8, 128), F32),
        vl=((3, 8, 128), F32),
        vz=((depth - 1, 8, 128), F32),
    )
    return [shapes, reduce_small, reduce_small, reduce_large]


def main_kernel(names, depth, hl, piece, nsem, *refs):
    (tok, cot, win, wg, wo, wp, pk, gain, lens, bsum, dsc, gout, sout, pout, vout) = refs[:15]
    send_sems, recv_sems = refs[-2:]
    sets, at = [], 15
    for group in names:
        sets.append(SimpleNamespace(**dict(zip(group, refs[at:]))))
        at += len(group)
    b = sets[0]
    width = tok.shape[1]
    cols = depth * hl
    el = 2 * hl

    r = lax.axis_index("replica")
    s = lax.axis_index("shard")
    y = lax.rem(r, 2)
    f = s // 4
    x = lax.rem(s // 2, 2)
    c = lax.rem(s, 2)
    core = (r, s + 1 - 2 * c)
    xpeer = (r, s + 2 - 4 * x)
    ypeer = (r + 1 - 2 * y, s)
    zpos = [lax.rem(f + k, depth) for k in range(1, depth)]
    zpeers = [(r, s + 4 * (q - f)) for q in zpos]
    q0 = y * 2 + x
    qx = y * 2 + 1 - x
    qy = (1 - y) * 2 + x
    qd = (1 - y) * 2 + 1 - x
    oc = 1 - c
    half = SLOT // 2

    counter = [0]
    started = []

    def rcopy(src, dst, dev):
        i = counter[0]
        counter[0] += 1
        assert i < nsem
        cp = pltpu.make_async_remote_copy(
            src_ref=src,
            dst_ref=dst,
            send_sem=send_sems.at[i],
            recv_sem=recv_sems.at[i],
            device_id=dev,
            device_id_type=MESH,
        )
        cp.start()
        started.append(cp)
        return cp

    def settle(cps):
        for cp in cps:
            cp.wait_send()
            started[:] = [other for other in started if other is not cp]

    barrier = pltpu.get_barrier_semaphore()
    for dev in [core, xpeer, ypeer] + zpeers:
        pl.semaphore_signal(barrier, inc=1, device_id=dev, device_id_type=MESH)

    b.gb[f, x, c] = gain[...]
    b.pka[f] = pk[...]
    wpv = wp[pl.ds(y * hl, hl), :].astype(F32)
    b.wpa[f] = jnp.concatenate([wpv, jnp.zeros((hl, 128 - wpv.shape[1]), F32)], axis=1).astype(BF16)
    wint = win[...].T
    b.wt[0, f] = jnp.where(y == 0, wint[:hl], wint[hl:])
    t32 = tok[...].astype(F32)
    inv = lax.rsqrt(jnp.mean(t32 * t32, axis=1, keepdims=True) + EPS)
    b.nb[q0, c] = (t32 * inv).astype(BF16)

    pl.semaphore_wait(barrier, 2 + depth)

    gcore = rcopy(b.gb.at[f, x, c], b.gb.at[f, x, c], core)

    def plane_start(buf):
        ax = rcopy(buf.at[q0, c, pl.ds(0, half)], buf.at[q0, c, pl.ds(0, half)], xpeer)
        by = rcopy(buf.at[q0, c, pl.ds(half, half)], buf.at[q0, c, pl.ds(half, half)], ypeer)
        bx = rcopy(buf.at[q0, c, pl.ds(half, half)], buf.at[q0, c, pl.ds(half, half)], xpeer)
        ay = rcopy(buf.at[q0, c, pl.ds(0, half)], buf.at[q0, c, pl.ds(0, half)], ypeer)
        oo = rcopy(buf.at[q0, c], buf.at[q0, c], core)
        return ax, by, bx, ay, oo

    def plane_forward(buf, cps):
        ax, by, bx, ay, oo = cps
        ax.wait_recv()
        fa = rcopy(buf.at[qx, c, pl.ds(0, half)], buf.at[qx, c, pl.ds(0, half)], ypeer)
        by.wait_recv()
        fb = rcopy(buf.at[qy, c, pl.ds(half, half)], buf.at[qy, c, pl.ds(half, half)], xpeer)
        bx.wait_recv()
        ox = rcopy(buf.at[qx, c], buf.at[qx, c], core)
        ay.wait_recv()
        oy = rcopy(buf.at[qy, c], buf.at[qy, c], core)
        return oo, ox, oy, fa, fb

    def plane_finish(buf, cps):
        oo, ox, oy, fa, fb = cps
        fa.wait_recv()
        fb.wait_recv()
        od = rcopy(buf.at[qd, c], buf.at[qd, c], core)
        oo.wait_recv()
        ox.wait_recv()
        oy.wait_recv()
        od.wait_recv()

    nstart = plane_start(b.nb)
    zsmall = [rcopy(b.pka.at[f], b.pka.at[f], dev) for dev in zpeers]
    zsmall += [rcopy(b.wpa.at[f], b.wpa.at[f], dev) for dev in zpeers]
    zin = [rcopy(b.wt.at[0, f], b.wt.at[0, f], dev) for dev in zpeers]

    gcore.wait_recv()
    gx = rcopy(b.gb.at[f, x], b.gb.at[f, x], xpeer)
    wgt = wg[...].T
    b.wt[1, f] = jnp.where(y == 0, wgt[:hl], wgt[hl:])
    b.wt[2, f] = wo[pl.ds(y * hl, hl), :]
    rowid = lax.broadcasted_iota(jnp.int32, (SLOT, 1), 0)
    b.db[q0, c] = jnp.where(rowid < lens[0], cot[...].astype(F32), 0.0).astype(BF16)
    b.ip[:, 0:8, :] = jnp.zeros((8, 8, cols), F32)
    b.dcp[SLOT : SLOT + 8, :] = jnp.zeros((8, cols), F32)
    b.ga[...] = jnp.zeros((STATE, 2, 8, 128), F32)
    b.sall[1] = jnp.zeros((STATE, 16, 128), BF16)
    source = lax.broadcasted_iota(jnp.int32, (256, 2 * STATE * 128), 0)
    target = lax.broadcasted_iota(jnp.int32, (256, 2 * STATE * 128), 1)
    b.sel[...] = jnp.where(lax.rem(source, 128) == RANK + target // 128, 1.0, 0.0).astype(BF16)
    gx.wait_recv()
    gz = [rcopy(b.gb.at[f], b.gb.at[f], dev) for dev in zpeers]

    nmid = plane_forward(b.nb, nstart)
    for cp in gz + zsmall:
        cp.wait_recv()
    pieces = []
    for i in range(depth):
        for j in range(2):
            for k in range(2):
                pieces.append(b.gb[i, j, k][0:1, :piece])
    gl = jnp.concatenate(pieces, axis=1)
    b.gl[...] = gl
    locs = []
    for i in range(depth):
        full = b.pka[i].astype(F32)
        locs.append(jnp.where(y == 0, full[:, :hl], full[:, hl:el]))
    pkl = jnp.concatenate(locs, axis=1)
    b.pkl[...] = pkl
    b.wst[...] = jnp.concatenate([pkl[:RANK], jnp.zeros((128 - RANK, cols), F32)], axis=0).astype(BF16)
    for n in range(STATE):
        row = -jnp.exp(pkl[RANK + n : RANK + n + 1]) * (1.0 / LN2)
        for et in range(2):
            b.rate[n, et] = jnp.broadcast_to(row[:, et * 128 : et * 128 + 128], (8, 128))
    plane_finish(b.nb, nmid)
    dstart = plane_start(b.db)
    for cp in zin:
        cp.wait_recv()
    zgate = [rcopy(b.wt.at[1, f], b.wt.at[1, f], dev) for dev in zpeers]
    zout = [rcopy(b.wt.at[2, f], b.wt.at[2, f], dev) for dev in zpeers]

    def scaled(w):
        full = b.wt[w].reshape(cols, width).astype(F32)
        b.ws[w] = (full * b.gl[...]).astype(BF16)

    scaled(0)
    o = RANK + STATE
    taps = [b.pkl[o + k : o + k + 1, :] for k in range(CONV)]
    cbias = b.pkl[o + CONV : o + CONV + 1, :]
    sbias = b.pkl[o + CONV + 1 : o + CONV + 2, :]
    skip = b.pkl[o + CONV + 2 : o + CONV + 3, :]

    @pl.loop(0, 4)
    def _(q):
        pre = nt(b.nb[q].reshape(2 * SLOT, width), b.ws[0])
        b.ip[2 * q, 8 : 8 + SLOT, :] = pre[:SLOT]
        b.ip[2 * q + 1, 8 : 8 + SLOT, :] = pre[SLOT:]

    wpl = b.wpa[...].reshape(cols, 128)

    @pl.loop(0, 4)
    def _(q):
        for cc in range(2):
            j = 2 * q + cc
            acc = jnp.broadcast_to(cbias, (SLOT, cols))
            for k in range(CONV):
                acc = acc + taps[k] * b.ip[j, 5 + k : 5 + k + SLOT, :]
            out = acc * jax.nn.sigmoid(acc)
            rows = pl.ds(pl.multiple_of(j * SLOT, SLOT), SLOT)
            b.xc[0, rows, :] = out[:, :128]
            b.xc[1, rows, :] = out[:, 128:]
            low = out.astype(BF16)
            b.cl[j] = low
            b.pp[q, cc] = nn(low, wpl)

    def all_reduce(which, between):
        g = sets[which]
        g.s1[...] = b.pp[:, oc].astype(BF16)
        one = rcopy(g.s1, g.l1, core)
        between(0)
        one.wait_recv()
        total = b.pp[:, c] + g.l1[...].astype(F32)
        g.s2[...] = total.astype(BF16)
        two = [
            rcopy(g.s2.at[pl.ds(0, 2)], g.l2.at[pl.ds(0, 2)], xpeer),
            rcopy(g.s2.at[pl.ds(2, 2)], g.l2.at[pl.ds(2, 2)], ypeer),
        ]
        g.own[...] = total
        between(1)
        for cp in two:
            cp.wait_recv()
        total = g.own[...] + g.l2[...].astype(F32)
        g.s3[...] = total.astype(BF16)
        three = [
            rcopy(g.s3.at[pl.ds(0, 2)], g.l3.at[pl.ds(0, 2)], ypeer),
            rcopy(g.s3.at[pl.ds(2, 2)], g.l3.at[pl.ds(2, 2)], xpeer),
        ]
        g.own[...] = total
        between(2)
        for cp in three:
            cp.wait_recv()
        g.own[...] = g.own[...] + g.l3[...].astype(F32)
        four = rcopy(g.own, g.oth, core)
        between(3)
        four.wait_recv()

    dstate = [None]

    def pump_first(stage):
        if stage == 1:
            dstate[0] = plane_forward(b.db, dstart)
        if stage == 2:
            plane_finish(b.db, dstate[0])

    all_reduce(1, pump_first)

    @pl.loop(0, 4)
    def _(q):
        for cc, src in ((c, sets[1].own), (oc, sets[1].oth)):
            j = 2 * q + cc
            rows = pl.ds(pl.multiple_of(j * SLOT, SLOT), SLOT)
            proj = src[q]
            b.tm[pl.ds(j, SLOT, stride=8), :] = proj
            low = proj.astype(BF16)
            b.slow[rows, :] = low
            pre = nn(low, b.wst[...]) + sbias
            size = jnp.maximum(pre, 0.0) + jnp.log1p(jnp.exp(-jnp.abs(pre)))
            b.dt[0, rows, :] = size[:, :128]
            b.dt[1, rows, :] = size[:, 128:]

    tm = b.tm[...]
    high = tm.astype(BF16)
    spread = jnp.concatenate([high, (tm - high.astype(F32)).astype(BF16)], axis=1)
    b.spread[...] = spread

    @pl.loop(0, STATE)
    def _(i):
        chunk = pl.ds(pl.multiple_of(i * 256, 256), 256)
        both = nn(b.spread[...], b.sel[:, chunk])
        b.bc[:, 2 * i] = both[:, :128].reshape(SLOT, 8, 128)
        b.bc[:, 2 * i + 1] = both[:, 128:].reshape(SLOT, 8, 128)

    def forward_step(t, carry):
        at = pl.ds(t, 8, stride=SLOT)
        size = [b.dt[e, at, :] for e in range(2)]
        push = [size[e] * b.xc[e, at, :] for e in range(2)]
        out = [jnp.zeros((8, 128), F32) for _ in range(2)]
        new = []
        for n in range(STATE):
            inm = b.bc[t, n]
            outm = b.bc[t, STATE + n]
            for e in range(2):
                decay = jnp.exp2(size[e] * b.rate[n, e])
                state = decay * carry[2 * n + e] + push[e] * inm
                out[e] = out[e] + outm * state
                new.append(state)
            b.sall[t + 2, n] = jnp.concatenate(new[-2:], axis=0).astype(BF16)
        for e in range(2):
            b.ys[e, at, :] = out[e]
        return tuple(new)

    zero = jnp.zeros((8, 128), F32)
    lax.fori_loop(0, SLOT, forward_step, tuple(zero for _ in range(2 * STATE)))

    for cp in zgate:
        cp.wait_recv()
    scaled(1)
    for cp in zout:
        cp.wait_recv()
    wout = b.wt.at[2]
    b.sg[...] = jnp.zeros((PACK, cols), F32)
    skip_row = o + CONV + 2

    @pl.loop(0, 4)
    def _(q):
        gpre = nt(b.nb[q].reshape(2 * SLOT, width), b.ws[1])
        dgat = nt(b.db[q].reshape(2 * SLOT, width), wout[...].reshape(cols, width))
        rows = pl.ds(pl.multiple_of(q * 2 * SLOT, 2 * SLOT), 2 * SLOT)
        conv = jnp.concatenate([b.xc[0, rows, :], b.xc[1, rows, :]], axis=1)
        mixed = jnp.concatenate([b.ys[0, rows, :], b.ys[1, rows, :]], axis=1) + skip * conv
        sig = jax.nn.sigmoid(gpre)
        act = gpre * sig
        b.go[q] = (mixed * act).astype(BF16).reshape(2, SLOT, cols)
        dmix = dgat * act
        b.dm[0, rows, :] = dmix[:, :128]
        b.dm[1, rows, :] = dmix[:, 128:]
        slope = sig * (1.0 + gpre * (1.0 - sig))
        b.dg[q] = (dgat * mixed * slope).astype(BF16).reshape(2, SLOT, cols)
        b.sg[skip_row : skip_row + 1, :] += jnp.sum(dmix * conv, axis=0, keepdims=True)

    def reduce_begin(which, dots):
        g = sets[which]

        @pl.loop(0, width // 256)
        def _(i):
            chunk = pl.ds(pl.multiple_of(i * 256, 256), 256)
            g.s1[:, :, chunk] = dots(oc, chunk).astype(BF16).reshape(4, SLOT, 256)

        one = rcopy(g.s1, g.l1, core)

        @pl.loop(0, width // 256)
        def _(i):
            chunk = pl.ds(pl.multiple_of(i * 256, 256), 256)
            b.sum[:, :, chunk] = dots(c, chunk).reshape(4, SLOT, 256)

        return one

    def reduce_second(which, one):
        g = sets[which]
        one.wait_recv()
        top, low = slice(0, half), slice(half, SLOT)
        for k, q in ((0, qx), (1, qd)):
            g.sx[k] = (b.sum[q, top, :] + g.l1[q, top, :].astype(F32)).astype(BF16)
        cx = rcopy(g.sx, g.lx, xpeer)
        for k, q in ((0, qy), (1, qd)):
            g.sy[k] = (b.sum[q, low, :] + g.l1[q, low, :].astype(F32)).astype(BF16)
        cy = rcopy(g.sy, g.ly, ypeer)
        return cx, cy

    def reduce_third(which, cps):
        g = sets[which]
        cx, cy = cps
        top, low = slice(0, half), slice(half, SLOT)
        cx.wait_recv()
        g.ty[...] = (
            b.sum[qy, top, :] + g.l1[qy, top, :].astype(F32) + g.lx[1].astype(F32)
        ).astype(BF16)
        c1 = rcopy(g.ty, g.my, ypeer)
        cy.wait_recv()
        g.tx[...] = (
            b.sum[qx, low, :] + g.l1[qx, low, :].astype(F32) + g.ly[1].astype(F32)
        ).astype(BF16)
        c2 = rcopy(g.tx, g.mx, xpeer)
        return c1, c2

    def reduce_end(which, cps, out):
        g = sets[which]
        top, low = slice(0, half), slice(half, SLOT)
        for cp in cps:
            cp.wait_recv()
        out[top, :] = (
            b.sum[q0, top, :]
            + g.l1[q0, top, :].astype(F32)
            + g.lx[0].astype(F32)
            + g.my[...].astype(F32)
        )
        out[low, :] = (
            b.sum[q0, low, :]
            + g.l1[q0, low, :].astype(F32)
            + g.ly[0].astype(F32)
            + g.mx[...].astype(F32)
        )

    def weight_grad(w, lhs, rhs, gained, first):
        b.tt[...] = lhs[...].reshape(8 * SLOT, cols).T

        @pl.loop(0, width // 256)
        def _(i):
            chunk = pl.ds(pl.multiple_of(i * 256, 256), 256)
            grad = nn(b.tt[...], rhs[:, :, :, chunk].reshape(8 * SLOT, 256))
            if gained:
                part = jnp.sum(
                    grad * b.wt[w, :, :, chunk].reshape(cols, 256).astype(F32), axis=0, keepdims=True
                )
                if first:
                    b.vv[:, chunk] = part
                else:
                    b.vv[:, chunk] += part
                grad = grad * b.gl[:, chunk]
            b.gws[w, :, :, chunk] = grad.astype(BF16).reshape(depth, hl, 256)

        return [rcopy(b.gws.at[w, q], b.gwl.at[w, k], dev) for k, (q, dev) in enumerate(zip(zpos, zpeers))]

    def weight_sum(w, cps):
        total = b.gws[w, f].astype(F32)
        for k, cp in enumerate(cps):
            cp.wait_recv()
            total = total + b.gwl[w, k].astype(F32)
        gout[w, y] = total
        b.gys[w] = total.astype(BF16)
        return rcopy(b.gys.at[w], b.gyl.at[w], ypeer)

    bone = reduce_begin(
        3,
        lambda cc, chunk: nn(
            b.go[:, cc].reshape(4 * SLOT, cols), b.wt[2, :, :, chunk].reshape(cols, 256)
        ),
    )
    zgo = weight_grad(2, b.go, b.db, False, False)
    btwo = reduce_second(3, bone)
    zgg = weight_grad(1, b.dg, b.nb, True, True)

    def backward_one(t, carry):
        at = pl.ds(t, 8, stride=SLOT)
        size = [b.dt[e, at, :] for e in range(2)]
        conv = [b.xc[e, at, :] for e in range(2)]
        dmix = [b.dm[e, at, :] for e in range(2)]
        push = [size[e] * conv[e] for e in range(2)]
        rate_sum = [zero, zero]
        weighted = [zero, zero]
        new, dins, douts = [], [], []
        for n in range(STATE):
            inm = b.bc[t, n]
            outm = b.bc[t, STATE + n]
            before = b.sall[t + 1, n].astype(F32)
            after = b.sall[t + 2, n].astype(F32)
            din = zero
            dout = zero
            for e in range(2):
                rate = b.rate[n, e]
                decay = jnp.exp2(size[e] * rate)
                lam = outm * dmix[e] + carry[2 * n + e]
                back = decay * lam
                grad = back * before[8 * e : 8 * e + 8]
                rate_sum[e] = rate_sum[e] + grad * rate
                weighted[e] = weighted[e] + lam * inm
                b.ga[n, e] += grad * size[e]
                din = din + lam * push[e]
                dout = dout + dmix[e] * after[8 * e : 8 * e + 8]
                new.append(back)
            dins.append(din)
            douts.append(dout)
        for e in range(2):
            b.ys[e, at, :] = rate_sum[e] * LN2 + conv[e] * weighted[e]
            b.xc[e, at, :] = size[e] * weighted[e]
        return tuple(new), dins, douts

    def backward_step(i, carry):
        t = SLOT - 2 - 2 * i
        carry, din1, dout1 = backward_one(t + 1, carry)
        carry, din0, dout0 = backward_one(t, carry)
        for n in range(STATE):
            b.sall[t + 2, n] = jnp.concatenate([din0[n], din1[n]], axis=0).astype(BF16)
            b.sall[t + 3, n] = jnp.concatenate([dout0[n], dout1[n]], axis=0).astype(BF16)
        return carry

    carry = tuple(zero for _ in range(2 * STATE))
    carry = lax.fori_loop(0, SLOT // 4, backward_step, carry)
    bthree = reduce_third(3, btwo)
    carry = lax.fori_loop(SLOT // 4, SLOT // 2, backward_step, carry)
    reduce_end(3, bthree, bsum)
    for n in range(STATE):
        row = jnp.concatenate(
            [jnp.sum(b.ga[n, e] * b.rate[n, e], axis=0, keepdims=True) for e in range(2)], axis=1
        )
        b.sg[RANK + n : RANK + n + 1, :] = row * LN2

    bias_row = o + CONV + 1
    trow = lax.broadcasted_iota(jnp.int32, (256, 128), 0)
    tcol = lax.broadcasted_iota(jnp.int32, (256, 128), 1)
    maps = jnp.zeros((8 * SLOT, 128), F32)
    for k in range(2):
        for n in range(0, STATE, 2):
            left = b.sall[2:, n].reshape(SLOT // 2, 2, 16, 128)[:, k].reshape(8 * SLOT, 128)
            right = b.sall[2:, n + 1].reshape(SLOT // 2, 2, 16, 128)[:, k].reshape(8 * SLOT, 128)
            ones = jnp.where(tcol == RANK + k * STATE + n + trow // 128, 1.0, 0.0).astype(BF16)
            maps = maps + nn(jnp.concatenate([left, right], axis=1), ones)
    b.tm[...] = maps


    @pl.loop(0, 4)
    def _(q):
        for cc in range(2):
            j = 2 * q + cc
            rows = pl.ds(pl.multiple_of(j * SLOT, SLOT), SLOT)
            step_pre = nn(b.slow[rows, :], b.wst[...]) + sbias
            dstep = jnp.concatenate([b.ys[0, rows, :], b.ys[1, rows, :]], axis=1)
            dpre = dstep * jax.nn.sigmoid(step_pre)
            b.sg[bias_row : bias_row + 1, :] += jnp.sum(dpre, axis=0, keepdims=True)
            low = dpre.astype(BF16)
            b.dsl[j] = low
            b.pp[q, cc] = nt(low, b.wst[...]) + b.tm[pl.ds(j, SLOT, stride=8), :]

    ystate = [None, None]

    def pump_second(stage):
        if stage == 0:
            grad = tn(b.slow[...], b.dsl[...].reshape(8 * SLOT, cols))
            b.sg[0:RANK, :] = grad[:RANK]
        if stage == 1:
            ystate[0] = weight_sum(2, zgo)
        if stage == 2:
            ystate[1] = weight_sum(1, zgg)

    all_reduce(2, pump_second)

    tap_row = o

    @pl.loop(0, 4)
    def _(q):
        for cc, src in ((c, sets[2].own), (oc, sets[2].oth)):
            j = 2 * q + cc
            rows = pl.ds(pl.multiple_of(j * SLOT, SLOT), SLOT)
            dproj = src[q].astype(BF16)
            b.dpj[rows, :] = dproj
            dmix = jnp.concatenate([b.dm[0, rows, :], b.dm[1, rows, :]], axis=1)
            dconv = jnp.concatenate([b.xc[0, rows, :], b.xc[1, rows, :]], axis=1) + dmix * skip
            dconv = dconv + nt(dproj, wpl)
            cpre = jnp.broadcast_to(cbias, (SLOT, cols))
            for k in range(CONV):
                cpre = cpre + taps[k] * b.ip[j, 5 + k : 5 + k + SLOT, :]
            sig = jax.nn.sigmoid(cpre)
            dpre = dconv * (sig * (1.0 + cpre * (1.0 - sig)))
            b.dcp[0:SLOT, :] = dpre
            sums = [jnp.sum(dpre * b.ip[j, 5 + k : 5 + k + SLOT, :], axis=0, keepdims=True) for k in range(CONV)]
            sums.append(jnp.sum(dpre, axis=0, keepdims=True))
            b.sg[tap_row : tap_row + CONV + 1, :] += jnp.concatenate(sums, axis=0)
            dinner = taps[CONV - 1] * dpre
            for k in range(CONV - 1):
                dinner = dinner + taps[k] * b.dcp[CONV - 1 - k : CONV - 1 - k + SLOT, :]
            b.di[q, cc] = dinner.astype(BF16)

    zgi = weight_grad(0, b.di, b.nb, True, False)
    for i in range(8):
        b.vs[0, i : i + 1, :] = b.vv[:, i * 128 : i * 128 + 128]
    v1 = rcopy(b.vs.at[0], b.vl.at[0], core)

    gproj = tn(b.cl[...].reshape(8 * SLOT, cols), b.dpj[...])
    b.gps[...] = gproj.reshape(depth, hl, 128).astype(BF16)
    for i in range(depth):
        cut = b.sg[:, i * hl : (i + 1) * hl]
        b.sgs[i] = jnp.concatenate([cut, jnp.zeros((PACK, 128 - hl), F32)], axis=1).astype(BF16)
    zgs = [rcopy(b.sgs.at[q], b.sgl.at[k], dev) for k, (q, dev) in enumerate(zip(zpos, zpeers))]
    zgp = [rcopy(b.gps.at[q], b.gpl.at[k], dev) for k, (q, dev) in enumerate(zip(zpos, zpeers))]

    settle([bone, *btwo, *bthree])
    done = reduce_begin(
        3,
        lambda cc, chunk: nn(b.di[:, cc].reshape(4 * SLOT, cols), b.ws[0, :, chunk])
        + nn(b.dg[:, cc].reshape(4 * SLOT, cols), b.ws[1, :, chunk]),
    )
    dtwo = reduce_second(3, done)
    v1.wait_recv()
    b.vs[1] = b.vs[0] + b.vl[0]
    v2 = rcopy(b.vs.at[1], b.vl.at[1], xpeer)
    dthree = reduce_third(3, dtwo)
    v2.wait_recv()
    b.vs[2] = b.vs[1] + b.vl[1]
    v3 = rcopy(b.vs.at[2], b.vl.at[2], ypeer)
    for w in (2, 1):
        ystate[2 - w].wait_recv()
        gout[w, 1 - y] = b.gyl[w].astype(F32)
    yin = weight_sum(0, zgi)

    total = b.sgs[f].astype(F32)
    for k, cp in enumerate(zgs):
        cp.wait_recv()
        total = total + b.sgl[k].astype(F32)
    sout[y] = total
    b.sgt[...] = total.astype(BF16)
    ys1 = rcopy(b.sgt, b.sgy, ypeer)
    total = b.gps[f].astype(F32)
    for k, cp in enumerate(zgp):
        cp.wait_recv()
        total = total + b.gpl[k].astype(F32)
    pout[y] = total
    b.gpt[...] = total.astype(BF16)
    ys2 = rcopy(b.gpt, b.gpy, ypeer)
    v3.wait_recv()
    b.vs[3] = b.vs[2] + b.vl[2]
    v4 = [rcopy(b.vs.at[3], b.vz.at[k], dev) for k, dev in enumerate(zpeers)]
    reduce_end(3, dthree, dsc)
    total = b.vs[3]
    for k, cp in enumerate(v4):
        cp.wait_recv()
        total = total + b.vz[k]
    vout[...] = total
    yin.wait_recv()
    gout[0, 1 - y] = b.gyl[0].astype(F32)
    ys1.wait_recv()
    sout[1 - y] = b.sgy[...].astype(F32)
    ys2.wait_recv()
    pout[1 - y] = b.gpy[...].astype(F32)
    for cp in started:
        cp.wait_send()


def last_kernel(hl, piece, tok, cot, lens, bsum, dsc, gout, sout, pout, vout, *outs):
    (out, dtok, ggain, ginner, ggate, gconv, gcb, gproj, gstep, gsb, glog, gskip, gwout) = outs
    s = lax.axis_index("shard")
    t32 = tok[...].astype(F32)
    rowid = lax.broadcasted_iota(jnp.int32, (SLOT, 1), 0)
    out[...] = (t32 + jnp.where(rowid < lens[0], bsum[...], 0.0)).astype(BF16)
    inv = lax.rsqrt(jnp.mean(t32 * t32, axis=1, keepdims=True) + EPS)
    ds = dsc[...]
    mean = jnp.mean(ds * t32, axis=1, keepdims=True)
    dtok[...] = cot[...].astype(F32) + inv * ds - t32 * (inv * inv * inv * mean)
    width = tok.shape[1]
    el = 2 * hl
    ginner[...] = gout[0].reshape(el, width).T
    ggate[...] = gout[1].reshape(el, width).T
    gwout[...] = gout[2].reshape(el, width)
    gproj[...] = pout[...].reshape(el, 128)[:, : RANK + 2 * STATE]
    both = jnp.concatenate([sout[0][:, :hl], sout[1][:, :hl]], axis=1)
    o = RANK + STATE
    gstep[...] = both[:RANK]
    glog[...] = both[RANK:o]
    gconv[...] = both[o : o + CONV]
    gcb[...] = both[o + CONV : o + CONV + 1]
    gsb[...] = both[o + CONV + 1 : o + CONV + 2]
    gskip[...] = both[o + CONV + 2 : o + CONV + 3]
    per = 128 // piece
    vec = vout[...]
    rows = lax.broadcasted_iota(jnp.int32, (8, 128), 0)
    row = jnp.sum(jnp.where(rows == s // per, vec, 0.0), axis=0, keepdims=True)
    pick = jnp.zeros((1, piece), F32)
    for i in range(per):
        pick = jnp.where(lax.rem(s, per) == i, row[:, i * piece : (i + 1) * piece], pick)
    ggain[...] = pick


def make_local(replicas, shards):
    depth = shards // 4

    def local(
        tokens, norm_gain, w_inner, w_gate, conv_weight, conv_bias, w_proj, w_step, step_bias, a_log, skip_gain,
        w_out, cotangent, lengths,
    ):
        width = tokens.shape[1]
        el = w_inner.shape[1]
        hl = el // 2
        piece = norm_gain.shape[0]
        pack = jnp.concatenate(
            [w_step, a_log, conv_weight, conv_bias[None], step_bias[None], skip_gain[None]], axis=0
        )
        pack = jnp.pad(pack, ((0, PACK - pack.shape[0]), (0, 128 - el)))
        gain = jnp.pad(
            jnp.broadcast_to(norm_gain.astype(F32)[None], (8, piece)), ((0, 0), (0, 128 - piece))
        )
        spec = buffers(depth, hl, width, shards, piece)
        nsem = 96 + 16 * depth
        vm = pl.BlockSpec(memory_space=pltpu.VMEM)
        sm = pl.BlockSpec(memory_space=pltpu.SMEM)
        sds = jax.ShapeDtypeStruct
        mid = pl.pallas_call(
            functools.partial(main_kernel, [tuple(group) for group in spec], depth, hl, piece, nsem),
            out_shape=(
                sds((SLOT, width), F32),
                sds((SLOT, width), F32),
                sds((3, 2, hl, width), F32),
                sds((2, PACK, 128), F32),
                sds((2, hl, 128), F32),
                sds((8, 128), F32),
            ),
            in_specs=[vm] * 8 + [sm],
            out_specs=(vm,) * 6,
            scratch_shapes=[pltpu.VMEM(shape, kind) for group in spec for shape, kind in group.values()]
            + [pltpu.SemaphoreType.DMA((nsem,)), pltpu.SemaphoreType.DMA((nsem,))],
            compiler_params=pltpu.CompilerParams(
                collective_id=0, has_side_effects=True, vmem_limit_bytes=61 << 20
            ),
            name="layer",
        )(tokens, cotangent, w_inner, w_gate, w_out, w_proj, pack, gain, lengths)
        bsum, dsc, gout, sout, pout, vout = mid
        if replicas > 2:
            groups = [[r for r in range(replicas) if r % 2 == k] for k in range(2)]
            gout, sout, pout, vout = (
                lax.psum(v, "replica", axis_index_groups=groups) for v in (gout, sout, pout, vout)
            )
        outs = pl.pallas_call(
            functools.partial(last_kernel, hl, piece),
            out_shape=(
                sds((SLOT, width), BF16),
                sds((SLOT, width), F32),
                sds((1, piece), F32),
                sds((width, el), F32),
                sds((width, el), F32),
                sds((CONV, el), F32),
                sds((1, el), F32),
                sds((el, RANK + 2 * STATE), F32),
                sds((RANK, el), F32),
                sds((1, el), F32),
                sds((STATE, el), F32),
                sds((1, el), F32),
                sds((el, width), F32),
            ),
            in_specs=[vm, vm, sm] + [vm] * 6,
            out_specs=(vm,) * 13,
            name="results",
        )(tokens, cotangent, lengths, bsum, dsc, gout, sout, pout, vout)
        return tuple(v.reshape(-1) if v.shape[0] == 1 else v for v in outs)

    return local


def solution(mesh):
    return jax.shard_map(
        make_local(mesh.shape["replica"], mesh.shape["shard"]),
        mesh=mesh,
        in_specs=(
            P(("replica", "shard"), None),
            P("shard"),
            P(None, "shard"),
            P(None, "shard"),
            P(None, "shard"),
            P("shard"),
            P("shard", None),
            P(None, "shard"),
            P("shard"),
            P(None, "shard"),
            P("shard"),
            P("shard", None),
            P(("replica", "shard"), None),
            P(("replica", "shard")),
        ),
        out_specs=(
            P(("replica", "shard"), None),
            P(("replica", "shard"), None),
            P("shard"),
            P(None, "shard"),
            P(None, "shard"),
            P(None, "shard"),
            P("shard"),
            P("shard", None),
            P(None, "shard"),
            P("shard"),
            P(None, "shard"),
            P("shard"),
            P("shard", None),
        ),
        check_vma=False,
    )
```

```python
import functools
import math
from types import SimpleNamespace

import jax
import jax.numpy as jnp
from jax import lax
from jax.experimental import pallas as pl
from jax.experimental.pallas import tpu as pltpu
from jax.sharding import PartitionSpec as P

RANK = 64
STATE = 16
CONV = 4
SLOT = 128
EPS = 1e-05
LN2 = math.log(2.0)
PROJ = RANK + 2 * STATE
PACK = 192
STEP_ROW = PROJ
LOG_ROW = STEP_ROW + RANK
TAP_ROW = LOG_ROW + STATE
CONV_ROW = TAP_ROW + CONV
BIAS_ROW = CONV_ROW + 1
SKIP_ROW = BIAS_ROW + 1
GAIN_ROW = SKIP_ROW + 1
MESH = pl.DeviceIdType.MESH
F32 = jnp.float32
BF16 = jnp.bfloat16


def sigmoid(value):
    return 0.5 * jnp.tanh(0.5 * value) + 0.5


def nt(left, right):
    return lax.dot_general(left, right, (((1,), (1,)), ((), ())), preferred_element_type=F32)


def nn(left, right):
    return lax.dot_general(left, right, (((1,), (0,)), ((), ())), preferred_element_type=F32)


def tn(left, right):
    return lax.dot_general(left, right, (((0,), (0,)), ((), ())), preferred_element_type=F32)


def buffers(depth, hl, width, shards, piece):
    cols = depth * hl
    rows = 8 * SLOT
    reduce_small = dict(
        s1=((4, SLOT, 128), BF16),
        l1=((4, SLOT, 128), BF16),
        s2=((4, SLOT, 128), BF16),
        l2=((4, SLOT, 128), BF16),
        s3=((4, SLOT, 128), BF16),
        l3=((4, SLOT, 128), BF16),
        own=((4, SLOT, 128), F32),
        oth=((4, SLOT, 128), F32),
    )
    reduce_large = dict(
        s1=((4, SLOT, width), BF16),
        l1=((4, SLOT, width), BF16),
        sx=((2, SLOT // 2, width), BF16),
        sy=((2, SLOT // 2, width), BF16),
        lx=((2, SLOT // 2, width), BF16),
        ly=((2, SLOT // 2, width), BF16),
        tx=((SLOT // 2, width), BF16),
        ty=((SLOT // 2, width), BF16),
        mx=((SLOT // 2, width), BF16),
        my=((SLOT // 2, width), BF16),
    )
    shapes = dict(
        wt=((3, depth, hl, width), BF16),
        ws=((2, cols, width), BF16),
        pka=((depth, PACK // 2, 128), BF16),
        wpt=((128, cols), BF16),
        gb=((2, 2, 8, cols), F32),
        t1=((rows, cols), F32),
        t2=((rows, cols), F32),
        gl=((1, width), F32),
        nb=((4, 2, SLOT, width), BF16),
        db=((4, 2, SLOT, width), BF16),
        pkl=((PACK, cols), F32),
        wst=((128, cols), BF16),
        rate=((STATE, 2, 8, 128), F32),
        ip=((8, SLOT + 8, cols), F32),
        dcp=((SLOT + 8, cols), F32),
        tm=((rows, 128), F32),
        sel=((256, 2 * STATE * 128), BF16),
        bc=((SLOT, 2 * STATE, 8, 128), F32),
        sall=((SLOT // 2 + 1, STATE, 2, 16, 128), BF16),
        cl=((8, SLOT, cols), BF16),
        xc=((2, rows, 128), F32),
        pp=((4, 2, SLOT, 128), F32),
        slow=((rows, 128), BF16),
        dpj=((rows, 128), BF16),
        dt=((2, rows, 128), F32),
        ys=((2, rows, 128), F32),
        dm=((2, rows, 128), F32),
        ga=((STATE, 2, 8, 128), F32),
        go=((4, 2, SLOT, cols), BF16),
        dg=((4, 2, SLOT, cols), BF16),
        di=((4, 2, SLOT, cols), BF16),
        dsl=((8, SLOT, cols), BF16),
        gws=((3, depth, hl, width), BF16),
        gwl=((3, depth - 1, hl, width), BF16),
        gwx=((3, hl, width), BF16),
        sg=((PACK, cols), F32),
        sgs=((depth, PACK // 2, 128), BF16),
        sgl=((depth - 1, PACK // 2, 128), BF16),
        sgx=((PACK // 2, 128), BF16),
        vv=((1, width), F32),
        sum=((4, SLOT, width), F32),
        vs=((4, 8, 128), F32),
        vl=((3, 8, 128), F32),
        vz=((depth, 8, 128), F32),
    )
    return [shapes, reduce_small, reduce_small, reduce_large]


def main_kernel(names, depth, hl, piece, nsem, *refs):
    (tok, cot, win, wg, wo, wproj, wstep, alog, convw, convb, stepb, skipg, gain, lens) = refs[:14]
    (bsum, dsc, gout, sout, vout) = refs[14:19]
    send_sems, recv_sems = refs[-2:]
    sets, at = [], 19
    for group in names:
        sets.append(SimpleNamespace(**dict(zip(group, refs[at:]))))
        at += len(group)
    b = sets[0]
    width = tok.shape[1]
    cols = depth * hl
    el = 2 * hl
    count = 8 * SLOT
    half = SLOT // 2

    r = lax.axis_index("replica")
    s = lax.axis_index("shard")
    y = lax.rem(r, 2)
    f = s // 4
    x = lax.rem(s // 2, 2)
    c = lax.rem(s, 2)
    core = (r, s + 1 - 2 * c)
    xpeer = (r, s + 2 - 4 * x)
    ypeer = (r + 1 - 2 * y, s)
    zpos = [lax.rem(f + k, depth) for k in range(1, depth)]
    zpeers = [(r, s + 4 * (q - f)) for q in zpos]
    q0 = y * 2 + x
    qx = y * 2 + 1 - x
    qy = (1 - y) * 2 + x
    qd = (1 - y) * 2 + 1 - x
    oc = 1 - c
    top, low = slice(0, half), slice(half, SLOT)

    counter = [0]
    started = []
    line = depth == 4
    ends = (f == 0) | (f == 3)
    inner = (f == 1) | (f == 2)

    def ticket():
        counter[0] += 1
        assert counter[0] <= nsem
        return counter[0] - 1

    def remote(src, dst, dev, send, recv):
        return pltpu.make_async_remote_copy(
            src_ref=src,
            dst_ref=dst,
            send_sem=send_sems.at[send],
            recv_sem=recv_sems.at[recv],
            device_id=dev,
            device_id_type=MESH,
        )

    def rcopy(src, dst, dev):
        i = ticket()
        cp = remote(src, dst, dev, i, i)
        cp.start()
        started.append(cp)
        return cp

    def same(ref, dev):
        return rcopy(ref, ref, dev)

    def settle(cps):
        for cp in cps:
            cp.wait_send()
            started[:] = [other for other in started if other is not cp]

    def arrive(cps):
        for cp in cps:
            cp.wait_recv()

    def only(when, cp):
        @pl.when(when)
        def _():
            cp.start()

        def wait_send():
            @pl.when(when)
            def _():
                cp.wait_send()

        started.append(SimpleNamespace(wait_send=wait_send))

    def far(k):
        return ((f == 0) & (k == 3)) | ((f == 3) & (k == 1))

    def far_from(k):
        return ((f == 0) & (k == 1)) | ((f == 3) & (k == 3))

    def z_gather(piece):
        ids = [ticket() for _ in range(depth)]
        cps = {}
        for k in sorted(range(1, depth), key=lambda k: k != 2):
            cps[k] = remote(piece(f), piece(f), zpeers[k - 1], ids[k], ids[k])
            if line and k != 2:
                only(jnp.logical_not(far(k)), cps[k])
            else:
                cps[k].start()
                started.append(cps[k])
        return SimpleNamespace(piece=piece, ids=ids, cps=cps)

    def z_relay(st):
        if line:
            st.cps[2].wait_recv()
            q = 3 * (2 - jnp.where(inner, f, 1))
            near = jnp.where(inner, 2 * f - 1, 1)
            only(inner, remote(st.piece(q), st.piece(q), (r, s + 4 * (3 - q - f)), st.ids[0], st.ids[1] + near - 1))

    def z_arrive(st):
        for k in range(1, depth):
            if not (line and k == 2):
                st.cps[k].wait_recv()

    def z_scatter(send, land, extra):
        ids = [ticket() for _ in range(depth)]
        cps = {k: remote(send(zpos[k - 1]), land(k - 1), zpeers[k - 1], ids[k], ids[k]) for k in range(1, depth)}
        st = SimpleNamespace(send=send, land=land, extra=extra, cps=cps)
        if not line:
            for cp in cps.values():
                cp.start()
                started.append(cp)
            return st
        st.cross = remote(send(3 - f), extra, (r, s + 4 - 8 * (f // 3)), ids[0], ids[0])
        only(ends, st.cross)
        return st

    def z_direct(st):
        if line:
            only(ends, st.cps[2])
            for k in (1, 3):
                only(jnp.logical_not(far(k)), st.cps[k])
        return st

    def z_absorb(st):
        if line:

            @pl.when(inner)
            def _():
                st.cross.wait_recv()
                target = st.send(zpos[1])
                target[...] = (target[...].astype(F32) + st.extra[...].astype(F32)).astype(BF16)

            only(inner, st.cps[2])

    def z_sum(st, own):
        total = own
        for k in range(1, depth):
            if line and k != 2:

                @pl.when(jnp.logical_not(far_from(k)))
                def _():
                    st.cps[k].wait_recv()

            else:
                st.cps[k].wait_recv()
        for k in range(1, depth):
            value = st.land(k - 1)[...].astype(F32)
            total = total + (jnp.where(far_from(k), 0.0, value) if line and k != 2 else value)
        return total

    barrier = pltpu.get_barrier_semaphore()
    reach = [core, xpeer, ypeer]
    for dev in reach:
        pl.semaphore_signal(barrier, inc=1, device_id=dev, device_id_type=MESH)
    for k in range(1, depth):

        def hello():
            pl.semaphore_signal(barrier, inc=1, device_id=zpeers[k - 1], device_id_type=MESH)

        if line and k != 2:
            pl.when(jnp.logical_not(far(k)))(hello)
        else:
            hello()

    def lanes(value, n):
        value = value.astype(F32)
        if value.shape[1] == n:
            return value
        return jnp.concatenate([value, jnp.zeros((value.shape[0], n - value.shape[1]), F32)], axis=1)

    def folded(value, n):
        both = jnp.concatenate([value[: PACK // 2], value[PACK // 2 :]], axis=1)
        return lanes(both, 128).astype(BF16)

    def unfolded(value, n):
        return jnp.concatenate([value[:, :n], value[:, n : 2 * n]], axis=0)

    rows = [wproj[...], wstep[...], alog[...], convw[...]]
    rows += [v[...].reshape(1, el) for v in (convb, stepb, skipg)]
    rows = [v.astype(F32) for v in rows]
    rows.append(jnp.zeros((PACK - GAIN_ROW, el), F32))
    pack = jnp.concatenate(rows, axis=0)
    mine = jnp.where(y == 0, pack[:, :hl], pack[:, hl:])
    own_gain = gain[...].reshape(1, piece).astype(F32)
    rowid = lax.broadcasted_iota(jnp.int32, (PACK, 1), 0)
    b.pka[f] = folded(jnp.where(rowid == GAIN_ROW, own_gain, mine), hl)
    wint = win[...].T
    b.wt[0, f] = jnp.where(y == 0, wint[:hl], wint[hl:])
    t32 = tok[...].astype(F32)
    inv = lax.rsqrt(jnp.mean(t32 * t32, axis=1, keepdims=True) + EPS)
    b.nb[q0, c] = (t32 * inv).astype(BF16)

    if line:
        for w in range(3):
            for k in (1, 3):

                @pl.when(far_from(k))
                def _():
                    b.gwl[w, k - 1] = jnp.zeros((hl, width), BF16)

        for k in (1, 3):

            @pl.when(far_from(k))
            def _():
                b.sgl[k - 1] = jnp.zeros((PACK // 2, 128), BF16)

        pl.semaphore_wait(barrier, jnp.where(ends, 5, 6))
    else:
        pl.semaphore_wait(barrier, 2 + depth)

    def plane_start(buf):
        upper, lower = buf.at[q0, c, pl.ds(0, half)], buf.at[q0, c, pl.ds(half, half)]
        ax = same(upper, xpeer)
        by = same(lower, ypeer)
        bx = same(lower, xpeer)
        ay = same(upper, ypeer)
        oo = same(buf.at[q0, c], core)
        return ax, by, bx, ay, oo

    def plane_forward(buf, cps):
        ax, by, bx, ay, oo = cps
        ax.wait_recv()
        fa = same(buf.at[qx, c, pl.ds(0, half)], ypeer)
        by.wait_recv()
        fb = same(buf.at[qy, c, pl.ds(half, half)], xpeer)
        return bx, ay, oo, fa, fb

    def plane_core(buf, cps):
        bx, ay, oo, fa, fb = cps
        bx.wait_recv()
        ox = same(buf.at[qx, c], core)
        ay.wait_recv()
        oy = same(buf.at[qy, c], core)
        return oo, ox, oy, fa, fb

    def plane_last(buf, cps):
        oo, ox, oy, fa, fb = cps
        arrive([fa, fb])
        return oo, ox, oy, same(buf.at[qd, c], core)

    zsmall = z_gather(lambda q: b.pka.at[q])
    zin = z_gather(lambda q: b.wt.at[0, q])
    nstate = plane_start(b.nb)

    wgt = wg[...].T
    b.wt[1, f] = jnp.where(y == 0, wgt[:hl], wgt[hl:])
    b.wt[2, f] = wo[pl.ds(y * hl, hl), :]
    rowid = lax.broadcasted_iota(jnp.int32, (SLOT, 1), 0)
    b.db[q0, c] = jnp.where(rowid < lens[0], cot[...].astype(F32), 0.0).astype(BF16)
    z_relay(zsmall)
    nstate = plane_forward(b.nb, nstate)
    z_relay(zin)
    zgate = z_gather(lambda q: b.wt.at[1, q])
    zout = z_gather(lambda q: b.wt.at[2, q])
    z_arrive(zsmall)
    locs = [unfolded(b.pka[i].astype(F32), hl) for i in range(depth)]
    pkl = jnp.concatenate(locs, axis=1)
    b.pkl[...] = pkl
    b.gb[c, x] = jnp.broadcast_to(pkl[GAIN_ROW : GAIN_ROW + 1], (8, cols))
    gx = same(b.gb.at[c, x], xpeer)
    dstate = plane_start(b.db)
    b.wst[...] = jnp.concatenate(
        [pkl[STEP_ROW:LOG_ROW], jnp.zeros((128 - RANK, cols), F32)], axis=0
    ).astype(BF16)
    b.wpt[...] = jnp.concatenate([pkl[:PROJ], jnp.zeros((128 - PROJ, cols), F32)], axis=0).astype(BF16)
    for n in range(STATE):
        row = -jnp.exp(pkl[LOG_ROW + n : LOG_ROW + n + 1]) * (1.0 / LN2)
        for et in range(2):
            b.rate[n, et] = jnp.broadcast_to(row[:, et * 128 : et * 128 + 128], (8, 128))
    nstate = plane_core(b.nb, nstate)
    b.ip[:, 0:8, :] = jnp.zeros((8, 8, cols), F32)
    b.dcp[SLOT : SLOT + 8, :] = jnp.zeros((8, cols), F32)
    b.ga[...] = jnp.zeros((STATE, 2, 8, 128), F32)
    b.sall[0] = jnp.zeros((STATE, 2, 16, 128), BF16)
    b.sg[...] = jnp.zeros((PACK, cols), F32)
    source = lax.broadcasted_iota(jnp.int32, (256, 2 * STATE * 128), 0)
    target = lax.broadcasted_iota(jnp.int32, (256, 2 * STATE * 128), 1)
    b.sel[...] = jnp.where(lax.rem(source, 128) == RANK + target // 128, 1.0, 0.0).astype(BF16)
    gx.wait_recv()
    gc = same(b.gb.at[c], core)
    gc.wait_recv()
    pieces = []
    for i in range(depth):
        for j in range(2):
            for k in range(2):
                pieces.append(b.gb[k, j, 0:1, i * piece : (i + 1) * piece])
    b.gl[...] = jnp.concatenate(pieces, axis=1)

    z_arrive(zin)
    z_relay(zgate)

    def scaled(w):
        full = b.wt[w].reshape(cols, width).astype(F32)
        b.ws[w] = (full * b.gl[...]).astype(BF16)

    scaled(0)
    arrive(plane_last(b.nb, nstate))

    def row_of(i):
        return b.pkl[i : i + 1, :]

    taps = [row_of(TAP_ROW + k) for k in range(CONV)]
    cbias = row_of(CONV_ROW)
    sbias = row_of(BIAS_ROW)
    skip = row_of(SKIP_ROW)

    def slot_rows(j):
        return pl.ds(pl.multiple_of(j * SLOT, SLOT), SLOT)

    def pair(ref, at):
        return jnp.concatenate([ref[0, at, :], ref[1, at, :]], axis=1)

    def unpair(ref, at, value):
        ref[0, at, :] = value[:, :128]
        ref[1, at, :] = value[:, 128:]

    def convolved(j):
        acc = jnp.broadcast_to(cbias, (SLOT, cols))
        for k in range(CONV):
            acc = acc + taps[k] * b.ip[j, 5 + k : 5 + k + SLOT, :]
        return acc

    b.ip[:, 8 : 8 + SLOT, :] = nt(b.nb[...].reshape(count, width), b.ws[0]).reshape(8, SLOT, cols)

    @pl.loop(0, 8)
    def _(j):
        acc = convolved(j)
        out = acc * sigmoid(acc)
        unpair(b.xc, slot_rows(j), out)
        b.cl[j] = out.astype(BF16)

    b.pp[...] = nt(b.cl[...].reshape(count, cols), b.wpt[...]).reshape(4, 2, SLOT, 128)

    def all_reduce(which, between):
        g = sets[which]
        g.s1[...] = b.pp[:, oc].astype(BF16)
        one = rcopy(g.s1, g.l1, core)
        between(0)
        one.wait_recv()
        total = b.pp[:, c] + g.l1[...].astype(F32)
        g.s2[...] = total.astype(BF16)
        two = [
            rcopy(g.s2.at[pl.ds(0, 2)], g.l2.at[pl.ds(0, 2)], xpeer),
            rcopy(g.s2.at[pl.ds(2, 2)], g.l2.at[pl.ds(2, 2)], ypeer),
        ]
        g.own[...] = total
        between(1)
        arrive(two)
        total = g.own[...] + g.l2[...].astype(F32)
        g.s3[...] = total.astype(BF16)
        three = [
            rcopy(g.s3.at[pl.ds(0, 2)], g.l3.at[pl.ds(0, 2)], ypeer),
            rcopy(g.s3.at[pl.ds(2, 2)], g.l3.at[pl.ds(2, 2)], xpeer),
        ]
        g.own[...] = total
        between(2)
        arrive(three)
        g.own[...] = g.own[...] + g.l3[...].astype(F32)
        four = rcopy(g.own, g.oth, core)
        between(3)
        four.wait_recv()

    dhold = [dstate]

    def pump_first(stage):
        if stage == 1:
            z_relay(zout)
        if stage == 2:
            dhold[0] = plane_forward(b.db, dhold[0])
        if stage == 3:
            dhold[0] = plane_core(b.db, dhold[0])

    all_reduce(1, pump_first)

    @pl.loop(0, 4)
    def _(q):
        for cc, src in ((c, sets[1].own), (oc, sets[1].oth)):
            j = 2 * q + cc
            proj = src[q]
            b.tm[pl.ds(j, SLOT, stride=8), :] = proj
            b.slow[slot_rows(j), :] = proj.astype(BF16)

    b.t1[...] = nn(b.slow[...], b.wst[...])

    @pl.loop(0, 8)
    def _(j):
        at = slot_rows(j)
        pre = b.t1[at, :] + sbias
        unpair(b.dt, at, jnp.maximum(pre, 0.0) + jnp.log1p(jnp.exp(-jnp.abs(pre))))

    tm = b.tm[...]
    high = tm.astype(BF16)
    spread = jnp.concatenate([high, (tm - high.astype(F32)).astype(BF16)], axis=1)
    both = nn(spread, b.sel[...])
    for i in range(2 * STATE):
        b.bc[:, i] = both[:, i * 128 : i * 128 + 128].reshape(SLOT, 8, 128)

    dstate = plane_last(b.db, dhold[0])
    zero = jnp.zeros((8, 128), F32)

    def forward_pair(k, carry):
        ats = [pl.ds(2 * k + i, 8, stride=SLOT) for i in range(2)]
        size = [[b.dt[e, at, :] for e in range(2)] for at in ats]
        push = [[size[i][e] * b.xc[e, ats[i], :] for e in range(2)] for i in range(2)]
        out = [[zero, zero], [zero, zero]]
        new = []
        for n in range(STATE):
            inm = [b.bc[2 * k + i, n] for i in range(2)]
            outm = [b.bc[2 * k + i, STATE + n] for i in range(2)]
            for e in range(2):
                rate = b.rate[n, e]
                state = carry[2 * n + e]
                kept = []
                for i in range(2):
                    state = jnp.exp2(size[i][e] * rate) * state + push[i][e] * inm[i]
                    out[i][e] = out[i][e] + outm[i] * state
                    kept.append(state)
                b.sall[k + 1, n, e] = jnp.concatenate(kept, axis=0).astype(BF16)
                new.append(state)
        for i in range(2):
            for e in range(2):
                b.ys[e, ats[i], :] = out[i][e]
        return tuple(new)

    lax.fori_loop(0, SLOT // 2, forward_pair, tuple(zero for _ in range(2 * STATE)))

    arrive(dstate)
    z_arrive(zgate)
    scaled(1)
    b.t1[...] = nt(b.nb[...].reshape(count, width), b.ws[1])
    z_arrive(zout)
    b.t2[...] = nt(b.db[...].reshape(count, width), b.wt[2].reshape(cols, width))

    @pl.loop(0, 4)
    def _(q):
        for cc in range(2):
            at = slot_rows(2 * q + cc)
            gpre = b.t1[at, :]
            dgat = b.t2[at, :]
            conv = pair(b.xc, at)
            mixed = pair(b.ys, at) + skip * conv
            sig = sigmoid(gpre)
            act = gpre * sig
            b.go[q, cc] = (mixed * act).astype(BF16)
            dmix = dgat * act
            unpair(b.dm, at, dmix)
            slope = sig * (1.0 + gpre * (1.0 - sig))
            b.dg[q, cc] = (dgat * mixed * slope).astype(BF16)
            b.sg[SKIP_ROW : SKIP_ROW + 1, :] += jnp.sum(dmix * conv, axis=0, keepdims=True)

    def reduce_begin(dots):
        g = sets[3]
        g.s1[qd] = dots(lambda ref: ref[qd, oc]).astype(BF16)
        cores = [rcopy(g.s1.at[qd], g.l1.at[qd], core)]
        others = (qx, qy, q0)
        rest = dots(lambda ref: jnp.concatenate([ref[q, oc] for q in others], axis=0)).astype(BF16)
        for k, q in enumerate(others):
            g.s1[q] = rest[k * SLOT : (k + 1) * SLOT]
            cores.append(rcopy(g.s1.at[q], g.l1.at[q], core))
        b.sum[...] = dots(lambda ref: ref[:, c].reshape(4 * SLOT, cols)).reshape(4, SLOT, width)
        return cores

    def reduce_second(cores):
        g = sets[3]

        def chip(q, rows):
            return (b.sum[q, rows, :] + g.l1[q, rows, :].astype(F32)).astype(BF16)

        cores[0].wait_recv()
        g.sx[1] = chip(qd, top)
        x1 = rcopy(g.sx.at[1], g.lx.at[1], xpeer)
        g.sy[1] = chip(qd, low)
        y1 = rcopy(g.sy.at[1], g.ly.at[1], ypeer)
        cores[1].wait_recv()
        g.sx[0] = chip(qx, top)
        x0 = rcopy(g.sx.at[0], g.lx.at[0], xpeer)
        cores[2].wait_recv()
        g.sy[0] = chip(qy, low)
        y0 = rcopy(g.sy.at[0], g.ly.at[0], ypeer)
        return x1, y1, x0, y0

    def reduce_third(cps):
        g = sets[3]
        x1, y1, x0, y0 = cps
        x1.wait_recv()
        g.ty[...] = (b.sum[qy, top, :] + g.l1[qy, top, :].astype(F32) + g.lx[1].astype(F32)).astype(BF16)
        c1 = rcopy(g.ty, g.my, ypeer)
        y1.wait_recv()
        g.tx[...] = (b.sum[qx, low, :] + g.l1[qx, low, :].astype(F32) + g.ly[1].astype(F32)).astype(BF16)
        c2 = rcopy(g.tx, g.mx, xpeer)
        return x0, y0, c1, c2

    def reduce_end(cores, cps, out):
        g = sets[3]
        cores[3].wait_recv()
        arrive(cps)
        for rows, near, far_ref in ((top, g.lx, g.my), (low, g.ly, g.mx)):
            out[rows, :] = (
                b.sum[q0, rows, :]
                + g.l1[q0, rows, :].astype(F32)
                + near[0].astype(F32)
                + far_ref[...].astype(F32)
            ).astype(BF16)

    def weight_grad(w, lhs, rhs, gained, first):
        grad = tn(lhs[...].reshape(count, cols), rhs[...].reshape(count, width))
        if gained:
            part = jnp.sum(grad * b.wt[w].reshape(cols, width).astype(F32), axis=0, keepdims=True)
            b.vv[...] = part if first else b.vv[...] + part
            grad = grad * b.gl[...]
        b.gws[w] = grad.astype(BF16).reshape(depth, hl, width)

    def weight_send(w, at):
        return z_scatter(
            lambda q: b.gws.at[w, q, at], lambda k: b.gwl.at[w, k, at], b.gwx.at[w, at]
        )

    def weight_sum(w, st, at):
        gout[w, y, at, :] = z_sum(st, b.gws[w, f, at, :].astype(F32)).astype(BF16)
        return same(gout.at[w, y, at], ypeer)

    every = pl.ds(0, hl)

    weight_grad(2, b.go, b.db, False, False)
    zgo = z_direct(weight_send(2, every))
    weight_grad(1, b.dg, b.nb, True, True)
    zgg = z_direct(weight_send(1, every))
    bone = reduce_begin(lambda pick: nn(pick(b.go), b.wt[2].reshape(cols, width)))

    def backward_pair(j, carry):
        k = SLOT // 2 - 1 - j
        ats = [pl.ds(2 * k + i, 8, stride=SLOT) for i in range(2)]
        size = [[b.dt[e, at, :] for e in range(2)] for at in ats]
        conv = [[b.xc[e, at, :] for e in range(2)] for at in ats]
        dmix = [[b.dm[e, at, :] for e in range(2)] for at in ats]
        push = [jnp.concatenate([size[i][e] * conv[i][e] for i in range(2)], axis=0).astype(BF16) for e in range(2)]
        dlow = [jnp.concatenate([dmix[i][e] for i in range(2)], axis=0).astype(BF16) for e in range(2)]
        rate_sum = [[zero, zero], [zero, zero]]
        weighted = [[zero, zero], [zero, zero]]
        new = []
        for n in range(STATE):
            inm = [b.bc[2 * k + i, n] for i in range(2)]
            outm = [b.bc[2 * k + i, STATE + n] for i in range(2)]
            dins, douts = [], []
            for e in range(2):
                rate = b.rate[n, e]
                here = b.sall[k + 1, n, e]
                before = [b.sall[k, n, e].astype(F32)[8:16], here.astype(F32)[0:8]]
                back = carry[2 * n + e]
                lams = [None, None]
                acc = b.ga[n, e]
                for i in (1, 0):
                    lam = outm[i] * dmix[i][e] + back
                    back = jnp.exp2(size[i][e] * rate) * lam
                    grad = back * before[i]
                    rate_sum[i][e] = rate_sum[i][e] + grad * rate
                    weighted[i][e] = weighted[i][e] + lam * inm[i]
                    acc = acc + grad * size[i][e]
                    lams[i] = lam
                b.ga[n, e] = acc
                new.append(back)
                dins.append(jnp.concatenate(lams, axis=0).astype(BF16) * push[e])
                douts.append(dlow[e] * here)
            b.sall[k + 1, n, 0] = dins[0] + dins[1]
            b.sall[k + 1, n, 1] = douts[0] + douts[1]
        for i in range(2):
            for e in range(2):
                b.ys[e, ats[i], :] = rate_sum[i][e] * LN2 + conv[i][e] * weighted[i][e]
                b.xc[e, ats[i], :] = size[i][e] * weighted[i][e]
        return tuple(new)

    carry = tuple(zero for _ in range(2 * STATE))
    carry = lax.fori_loop(0, SLOT // 8, backward_pair, carry)
    z_absorb(zgo)
    btwo = reduce_second(bone)
    carry = lax.fori_loop(SLOT // 8, 3 * SLOT // 8, backward_pair, carry)
    z_absorb(zgg)
    bthree = reduce_third(btwo)
    carry = lax.fori_loop(3 * SLOT // 8, SLOT // 2, backward_pair, carry)

    parts = [b.sall[1:, n, k].reshape(count, 128) for k in range(2) for n in range(STATE)]
    b.tm[...] = nt(jnp.concatenate(parts, axis=1), b.sel[0:128, :])

    b.t1[...] = nn(b.slow[...], b.wst[...])

    @pl.loop(0, 8)
    def _(j):
        at = slot_rows(j)
        dpre = pair(b.ys, at) * sigmoid(b.t1[at, :] + sbias)
        b.sg[BIAS_ROW : BIAS_ROW + 1, :] += jnp.sum(dpre, axis=0, keepdims=True)
        b.dsl[j] = dpre.astype(BF16)

    b.pp[...] = nt(b.dsl[...].reshape(count, cols), b.wst[...]).reshape(4, 2, SLOT, 128)

    @pl.loop(0, 4)
    def _(q):
        for cc in range(2):
            b.pp[q, cc] += b.tm[pl.ds(2 * q + cc, SLOT, stride=8), :]

    hold = [None, None]

    def pump_second(stage):
        if stage == 0:
            grad = tn(b.slow[...], b.dsl[...].reshape(count, cols))
            b.sg[STEP_ROW:LOG_ROW, :] = grad[:RANK]
        if stage == 1:
            reduce_end(bone, bthree, bsum)
            for n in range(STATE):
                parts = [jnp.sum(b.ga[n, e] * b.rate[n, e], axis=0, keepdims=True) for e in range(2)]
                b.sg[LOG_ROW + n : LOG_ROW + n + 1, :] = jnp.concatenate(parts, axis=1) * LN2
        if stage == 2:
            hold[0] = weight_sum(2, zgo, every)
        if stage == 3:
            hold[1] = weight_sum(1, zgg, every)

    all_reduce(2, pump_second)

    @pl.loop(0, 4)
    def _(q):
        for cc, src in ((c, sets[2].own), (oc, sets[2].oth)):
            b.dpj[slot_rows(2 * q + cc), :] = src[q].astype(BF16)

    b.t1[...] = nn(b.dpj[...], b.wpt[...])

    @pl.loop(0, 4)
    def _(q):
        for cc in range(2):
            j = 2 * q + cc
            at = slot_rows(j)
            dconv = pair(b.xc, at) + pair(b.dm, at) * skip + b.t1[at, :]
            cpre = convolved(j)
            sig = sigmoid(cpre)
            dpre = dconv * (sig * (1.0 + cpre * (1.0 - sig)))
            b.dcp[0:SLOT, :] = dpre
            sums = [jnp.sum(dpre * b.ip[j, 5 + k : 5 + k + SLOT, :], axis=0, keepdims=True) for k in range(CONV)]
            sums.append(jnp.sum(dpre, axis=0, keepdims=True))
            b.sg[TAP_ROW : CONV_ROW + 1, :] += jnp.concatenate(sums, axis=0)
            dinner = taps[CONV - 1] * dpre
            for k in range(CONV - 1):
                dinner = dinner + taps[k] * b.dcp[CONV - 1 - k : CONV - 1 - k + SLOT, :]
            b.di[q, cc] = dinner.astype(BF16)

    weight_grad(0, b.di, b.nb, True, False)
    first, second = pl.ds(0, hl // 2), pl.ds(hl // 2, hl // 2)
    zgi = [weight_send(0, first), weight_send(0, second)]
    for st in zgi:
        z_direct(st)
    for i in range(8):
        b.vs[0, i : i + 1, :] = b.vv[:, i * 128 : i * 128 + 128]
    v1 = rcopy(b.vs.at[0], b.vl.at[0], xpeer)
    settle([*bone, *btwo, *bthree[2:]])
    done = reduce_begin(lambda pick: nn(pick(b.di), b.ws[0]) + nn(pick(b.dg), b.ws[1]))
    v1.wait_recv()
    b.vs[1] = b.vs[0] + b.vl[0]
    v2 = rcopy(b.vs.at[1], b.vl.at[1], ypeer)
    dtwo = reduce_second(done)
    z_absorb(zgi[0])
    z_absorb(zgi[1])
    grad = tn(b.dpj[...], b.cl[...].reshape(count, cols))
    b.sg[0:PROJ, :] = grad[:PROJ]
    for i in range(depth):
        b.sgs[i] = folded(b.sg[:, i * hl : (i + 1) * hl], hl)
    zgs = z_direct(z_scatter(lambda q: b.sgs.at[q], lambda k: b.sgl.at[k], b.sgx))
    v2.wait_recv()
    b.vs[2] = b.vs[1] + b.vl[1]
    v3 = rcopy(b.vs.at[2], b.vl.at[2], core)
    dthree = reduce_third(dtwo)
    v3.wait_recv()
    b.vz[f] = b.vs[2] + b.vl[2]
    v4 = z_gather(lambda q: b.vz.at[q])
    yin = [weight_sum(0, zgi[0], first)]
    z_absorb(zgs)
    yin.append(weight_sum(0, zgi[1], second))
    sout[y] = z_sum(zgs, b.sgs[f].astype(F32)).astype(BF16)
    ysmall = same(sout.at[y], ypeer)
    z_relay(v4)
    reduce_end(done, dthree, dsc)
    z_arrive(v4)
    total = b.vz[0]
    for k in range(1, depth):
        total = total + b.vz[k]
    vout[...] = total
    arrive(hold + yin + [ysmall])
    for cp in started:
        cp.wait_send()


def last_kernel(hl, piece, tok, cot, lens, bsum, dsc, gout, sout, vout, *outs):
    (out, dtok, ggain, ginner, ggate, gconv, gcb, gproj, gstep, gsb, glog, gskip, gwout) = outs
    s = lax.axis_index("shard")
    t32 = tok[...].astype(F32)
    rowid = lax.broadcasted_iota(jnp.int32, (SLOT, 1), 0)
    out[...] = (t32 + jnp.where(rowid < lens[0], bsum[...].astype(F32), 0.0)).astype(BF16)
    inv = lax.rsqrt(jnp.mean(t32 * t32, axis=1, keepdims=True) + EPS)
    ds = dsc[...].astype(F32)
    mean = jnp.mean(ds * t32, axis=1, keepdims=True)
    dtok[...] = cot[...].astype(F32) + inv * ds - t32 * (inv * inv * inv * mean)
    width = tok.shape[1]
    el = 2 * hl
    ginner[...] = gout[0].reshape(el, width).T.astype(F32)
    ggate[...] = gout[1].reshape(el, width).T.astype(F32)
    gwout[...] = gout[2].reshape(el, width).astype(F32)
    small = sout[...].astype(F32)
    halves = [jnp.concatenate([small[k][:, :hl], small[k][:, hl:el]], axis=0) for k in range(2)]
    both = jnp.concatenate(halves, axis=1)
    gproj[...] = both[:PROJ]
    gstep[...] = both[STEP_ROW:LOG_ROW]
    glog[...] = both[LOG_ROW:TAP_ROW]
    gconv[...] = both[TAP_ROW:CONV_ROW]
    gcb[...] = both[CONV_ROW : CONV_ROW + 1].reshape(el)
    gsb[...] = both[BIAS_ROW : BIAS_ROW + 1].reshape(el)
    gskip[...] = both[SKIP_ROW : SKIP_ROW + 1].reshape(el)
    per = 128 // piece
    vec = vout[...]
    rows = lax.broadcasted_iota(jnp.int32, (8, 128), 0)
    row = jnp.sum(jnp.where(rows == s // per, vec, 0.0), axis=0, keepdims=True)
    pick = jnp.zeros((1, piece), F32)
    for i in range(per):
        pick = jnp.where(lax.rem(s, per) == i, row[:, i * piece : (i + 1) * piece], pick)
    ggain[...] = pick.reshape(piece)


def make_local(replicas, shards):
    depth = shards // 4

    def local(
        tokens, norm_gain, w_inner, w_gate, conv_weight, conv_bias, w_proj, w_step, step_bias, a_log, skip_gain,
        w_out, cotangent, lengths,
    ):
        width = tokens.shape[1]
        el = w_inner.shape[1]
        hl = el // 2
        piece = norm_gain.shape[0]
        spec = buffers(depth, hl, width, shards, piece)
        nsem = 96 + 16 * depth
        vm = pl.BlockSpec(memory_space=pltpu.VMEM)
        sm = pl.BlockSpec(memory_space=pltpu.SMEM)
        sds = jax.ShapeDtypeStruct
        mid = pl.pallas_call(
            functools.partial(main_kernel, [tuple(group) for group in spec], depth, hl, piece, nsem),
            out_shape=(
                pltpu.VMEM((SLOT, width), BF16),
                pltpu.VMEM((SLOT, width), BF16),
                pltpu.VMEM((3, 2, hl, width), BF16),
                pltpu.VMEM((2, PACK // 2, 128), BF16),
                pltpu.VMEM((8, 128), F32),
            ),
            in_specs=[vm] * 13 + [sm],
            out_specs=(vm,) * 5,
            scratch_shapes=[pltpu.VMEM(shape, kind) for group in spec for shape, kind in group.values()]
            + [pltpu.SemaphoreType.DMA((nsem,)), pltpu.SemaphoreType.DMA((nsem,))],
            compiler_params=pltpu.CompilerParams(
                collective_id=0, has_side_effects=True, vmem_limit_bytes=61 << 20
            ),
            name="layer",
        )(
            tokens, cotangent, w_inner, w_gate, w_out, w_proj.T, w_step, a_log, conv_weight, conv_bias, step_bias,
            skip_gain, norm_gain, lengths,
        )
        bsum, dsc, gout, sout, vout = mid
        if replicas > 2:
            groups = [[r for r in range(replicas) if r % 2 == k] for k in range(2)]
            gout, sout, vout = (
                lax.psum(v.astype(F32), "replica", axis_index_groups=groups) for v in (gout, sout, vout)
            )
        outs = pl.pallas_call(
            functools.partial(last_kernel, hl, piece),
            out_shape=(
                sds((SLOT, width), BF16),
                sds((SLOT, width), F32),
                sds((piece,), F32),
                sds((width, el), F32),
                sds((width, el), F32),
                sds((CONV, el), F32),
                sds((el,), F32),
                sds((PROJ, el), F32),
                sds((RANK, el), F32),
                sds((el,), F32),
                sds((STATE, el), F32),
                sds((el,), F32),
                sds((el, width), F32),
            ),
            in_specs=[vm, vm, sm] + [vm] * 5,
            out_specs=(vm,) * 13,
            compiler_params=pltpu.CompilerParams(vmem_limit_bytes=16 << 20),
            name="results",
        )(tokens, cotangent, lengths, bsum, dsc, gout, sout, vout)
        return outs[:7] + (outs[7].T,) + outs[8:]

    return local


def solution(mesh):
    return jax.shard_map(
        make_local(mesh.shape["replica"], mesh.shape["shard"]),
        mesh=mesh,
        in_specs=(
            P(("replica", "shard"), None),
            P("shard"),
            P(None, "shard"),
            P(None, "shard"),
            P(None, "shard"),
            P("shard"),
            P("shard", None),
            P(None, "shard"),
            P("shard"),
            P(None, "shard"),
            P("shard"),
            P("shard", None),
            P(("replica", "shard"), None),
            P(("replica", "shard")),
        ),
        out_specs=(
            P(("replica", "shard"), None),
            P(("replica", "shard"), None),
            P("shard"),
            P(None, "shard"),
            P(None, "shard"),
            P(None, "shard"),
            P("shard"),
            P("shard", None),
            P(None, "shard"),
            P("shard"),
            P(None, "shard"),
            P("shard"),
            P("shard", None),
        ),
        check_vma=False,
    )
```

```python
import functools
import math
from types import SimpleNamespace

import jax
import jax.numpy as jnp
from jax import lax
from jax.experimental import pallas as pl
from jax.experimental.pallas import tpu as pltpu
from jax.sharding import PartitionSpec as P

RANK = 64
STATE = 16
CONV = 4
SLOT = 128
EPS = 1e-05
LN2 = math.log(2.0)
PROJ = RANK + 2 * STATE
PACK = 192
STEP_ROW = PROJ
LOG_ROW = STEP_ROW + RANK
TAP_ROW = LOG_ROW + STATE
CONV_ROW = TAP_ROW + CONV
BIAS_ROW = CONV_ROW + 1
SKIP_ROW = BIAS_ROW + 1
GAIN_ROW = SKIP_ROW + 1
MESH = pl.DeviceIdType.MESH
F32 = jnp.float32
BF16 = jnp.bfloat16


def sigmoid(value):
    return 0.5 * jnp.tanh(0.5 * value) + 0.5


def nt(left, right):
    return lax.dot_general(left, right, (((1,), (1,)), ((), ())), preferred_element_type=F32)


def nn(left, right):
    return lax.dot_general(left, right, (((1,), (0,)), ((), ())), preferred_element_type=F32)


def tn(left, right):
    return lax.dot_general(left, right, (((0,), (0,)), ((), ())), preferred_element_type=F32)


def buffers(depth, hl, width, shards, piece):
    cols = depth * hl
    rows = 8 * SLOT
    reduce_small = dict(
        s1=((4, SLOT, 128), BF16),
        l1=((4, SLOT, 128), BF16),
        s2=((4, SLOT, 128), BF16),
        l2=((4, SLOT, 128), BF16),
        s3=((4, SLOT, 128), BF16),
        l3=((4, SLOT, 128), BF16),
        own=((4, SLOT, 128), F32),
        oth=((4, SLOT, 128), F32),
    )
    reduce_large = dict(
        s1=((4, SLOT, width), BF16),
        l1=((4, SLOT, width), BF16),
        sx=((2, SLOT // 2, width), BF16),
        sy=((2, SLOT // 2, width), BF16),
        lx=((2, SLOT // 2, width), BF16),
        ly=((2, SLOT // 2, width), BF16),
        tx=((SLOT // 2, width), BF16),
        ty=((SLOT // 2, width), BF16),
        mx=((SLOT // 2, width), BF16),
        my=((SLOT // 2, width), BF16),
    )
    shapes = dict(
        wt=((3, depth, hl, width), BF16),
        ws=((2, cols, width), BF16),
        pka=((depth, PACK // 2, 128), BF16),
        wpt=((128, cols), BF16),
        gb=((2, 2, 8, cols), F32),
        t1=((rows, cols), F32),
        t2=((rows, cols), F32),
        gl=((1, width), F32),
        nb=((4, 2, SLOT, width), BF16),
        db=((4, 2, SLOT, width), BF16),
        pkl=((PACK, cols), F32),
        wst=((128, cols), BF16),
        rate=((STATE, 2, 8, 128), F32),
        ip=((8, SLOT + 8, cols), F32),
        dcp=((SLOT + 8, cols), F32),
        tm=((rows, 128), F32),
        sel=((256, 2 * STATE * 128), BF16),
        bc=((SLOT, 2 * STATE, 8, 128), F32),
        sall=((SLOT // 2 + 1, STATE, 2, 16, 128), BF16),
        cl=((8, SLOT, cols), BF16),
        xc=((2, rows, 128), F32),
        pp=((4, 2, SLOT, 128), F32),
        slow=((rows, 128), BF16),
        dpj=((rows, 128), BF16),
        dt=((2, rows, 128), F32),
        ys=((2, rows, 128), F32),
        dm=((2, rows, 128), F32),
        ga=((STATE, 2, 8, 128), F32),
        carried=((STATE, 2, 8, 128), F32),
        go=((4, 2, SLOT, cols), BF16),
        dg=((4, 2, SLOT, cols), BF16),
        di=((4, 2, SLOT, cols), BF16),
        dsl=((8, SLOT, cols), BF16),
        gws=((3, depth, hl, width), BF16),
        gwl=((3, depth - 1, hl, width), BF16),
        gwx=((3, hl, width), BF16),
        sg=((PACK, cols), F32),
        sgs=((depth, PACK // 2, 128), BF16),
        sgl=((depth - 1, PACK // 2, 128), BF16),
        sgx=((PACK // 2, 128), BF16),
        vv=((1, width), F32),
        sum=((4, SLOT, width), F32),
        vs=((4, 8, 128), F32),
        vl=((3, 8, 128), F32),
        vz=((depth, 8, 128), F32),
    )
    return [shapes, reduce_small, reduce_small, reduce_large]


def main_kernel(names, depth, hl, piece, nsem, *refs):
    (tok, cot, win, wg, wo, wproj, wstep, alog, convw, convb, stepb, skipg, gain, lens) = refs[:14]
    (bsum, dsc, gout, sout, vout) = refs[14:19]
    send_sems, recv_sems = refs[-2:]
    sets, at = [], 19
    for group in names:
        sets.append(SimpleNamespace(**dict(zip(group, refs[at:]))))
        at += len(group)
    b = sets[0]
    width = tok.shape[1]
    cols = depth * hl
    el = 2 * hl
    count = 8 * SLOT
    half = SLOT // 2

    r = lax.axis_index("replica")
    s = lax.axis_index("shard")
    y = lax.rem(r, 2)
    f = s // 4
    x = lax.rem(s // 2, 2)
    c = lax.rem(s, 2)
    core = (r, s + 1 - 2 * c)
    xpeer = (r, s + 2 - 4 * x)
    ypeer = (r + 1 - 2 * y, s)
    zpos = [lax.rem(f + k, depth) for k in range(1, depth)]
    zpeers = [(r, s + 4 * (q - f)) for q in zpos]
    q0 = y * 2 + x
    qx = y * 2 + 1 - x
    qy = (1 - y) * 2 + x
    qd = (1 - y) * 2 + 1 - x
    oc = 1 - c
    top, low = slice(0, half), slice(half, SLOT)

    counter = [0]
    started = []
    line = depth == 4
    ends = (f == 0) | (f == 3)
    inner = (f == 1) | (f == 2)

    def ticket():
        counter[0] += 1
        assert counter[0] <= nsem
        return counter[0] - 1

    def remote(src, dst, dev, send, recv):
        return pltpu.make_async_remote_copy(
            src_ref=src,
            dst_ref=dst,
            send_sem=send_sems.at[send],
            recv_sem=recv_sems.at[recv],
            device_id=dev,
            device_id_type=MESH,
        )

    def rcopy(src, dst, dev):
        i = ticket()
        cp = remote(src, dst, dev, i, i)
        cp.start()
        started.append(cp)
        return cp

    def same(ref, dev):
        return rcopy(ref, ref, dev)

    def settle(cps):
        for cp in cps:
            cp.wait_send()
            started[:] = [other for other in started if other is not cp]

    def arrive(cps):
        for cp in cps:
            cp.wait_recv()

    def only(when, cp):
        @pl.when(when)
        def _():
            cp.start()

        def wait_send():
            @pl.when(when)
            def _():
                cp.wait_send()

        started.append(SimpleNamespace(wait_send=wait_send))

    def far(k):
        return ((f == 0) & (k == 3)) | ((f == 3) & (k == 1))

    def far_from(k):
        return ((f == 0) & (k == 1)) | ((f == 3) & (k == 3))

    def z_gather(piece):
        ids = [ticket() for _ in range(depth)]
        cps = {}
        for k in sorted(range(1, depth), key=lambda k: k != 2):
            cps[k] = remote(piece(f), piece(f), zpeers[k - 1], ids[k], ids[k])
            if line and k != 2:
                only(jnp.logical_not(far(k)), cps[k])
            else:
                cps[k].start()
                started.append(cps[k])
        return SimpleNamespace(piece=piece, ids=ids, cps=cps)

    def z_relay(st):
        if line:
            st.cps[2].wait_recv()
            q = 3 * (2 - jnp.where(inner, f, 1))
            near = jnp.where(inner, 2 * f - 1, 1)
            only(inner, remote(st.piece(q), st.piece(q), (r, s + 4 * (3 - q - f)), st.ids[0], st.ids[1] + near - 1))

    def z_arrive(st):
        for k in range(1, depth):
            if not (line and k == 2):
                st.cps[k].wait_recv()

    def z_scatter(send, land, extra):
        ids = [ticket() for _ in range(depth)]
        cps = {k: remote(send(zpos[k - 1]), land(k - 1), zpeers[k - 1], ids[k], ids[k]) for k in range(1, depth)}
        st = SimpleNamespace(send=send, land=land, extra=extra, cps=cps)
        if not line:
            for cp in cps.values():
                cp.start()
                started.append(cp)
            return st
        st.cross = remote(send(3 - f), extra, (r, s + 4 - 8 * (f // 3)), ids[0], ids[0])
        only(ends, st.cross)
        return st

    def z_direct(st):
        if line:
            only(ends, st.cps[2])
            for k in (1, 3):
                only(jnp.logical_not(far(k)), st.cps[k])
        return st

    def z_absorb(st):
        if line:

            @pl.when(inner)
            def _():
                st.cross.wait_recv()
                target = st.send(zpos[1])
                target[...] = (target[...].astype(F32) + st.extra[...].astype(F32)).astype(BF16)

            only(inner, st.cps[2])

    def z_sum(st, own):
        total = own
        for k in range(1, depth):
            if line and k != 2:

                @pl.when(jnp.logical_not(far_from(k)))
                def _():
                    st.cps[k].wait_recv()

            else:
                st.cps[k].wait_recv()
        for k in range(1, depth):
            value = st.land(k - 1)[...].astype(F32)
            total = total + (jnp.where(far_from(k), 0.0, value) if line and k != 2 else value)
        return total

    barrier = pltpu.get_barrier_semaphore()
    reach = [core, xpeer, ypeer]
    for dev in reach:
        pl.semaphore_signal(barrier, inc=1, device_id=dev, device_id_type=MESH)
    for k in range(1, depth):

        def hello():
            pl.semaphore_signal(barrier, inc=1, device_id=zpeers[k - 1], device_id_type=MESH)

        if line and k != 2:
            pl.when(jnp.logical_not(far(k)))(hello)
        else:
            hello()

    def lanes(value, n):
        value = value.astype(F32)
        if value.shape[1] == n:
            return value
        return jnp.concatenate([value, jnp.zeros((value.shape[0], n - value.shape[1]), F32)], axis=1)

    def folded(value, n):
        both = jnp.concatenate([value[: PACK // 2], value[PACK // 2 :]], axis=1)
        return lanes(both, 128).astype(BF16)

    def unfolded(value, n):
        return jnp.concatenate([value[:, :n], value[:, n : 2 * n]], axis=0)

    rows = [wproj[...], wstep[...], alog[...], convw[...]]
    rows += [v[...].reshape(1, el) for v in (convb, stepb, skipg)]
    rows = [v.astype(F32) for v in rows]
    rows.append(jnp.zeros((PACK - GAIN_ROW, el), F32))
    pack = jnp.concatenate(rows, axis=0)
    mine = jnp.where(y == 0, pack[:, :hl], pack[:, hl:])
    own_gain = gain[...].reshape(1, piece).astype(F32)
    rowid = lax.broadcasted_iota(jnp.int32, (PACK, 1), 0)
    b.pka[f] = folded(jnp.where(rowid == GAIN_ROW, own_gain, mine), hl)
    wint = win[...].T
    b.wt[0, f] = jnp.where(y == 0, wint[:hl], wint[hl:])
    t32 = tok[...].astype(F32)
    inv = lax.rsqrt(jnp.mean(t32 * t32, axis=1, keepdims=True) + EPS)
    b.nb[q0, c] = (t32 * inv).astype(BF16)

    if line:
        for w in range(3):
            for k in (1, 3):

                @pl.when(far_from(k))
                def _():
                    b.gwl[w, k - 1] = jnp.zeros((hl, width), BF16)

        for k in (1, 3):

            @pl.when(far_from(k))
            def _():
                b.sgl[k - 1] = jnp.zeros((PACK // 2, 128), BF16)

        pl.semaphore_wait(barrier, jnp.where(ends, 5, 6))
    else:
        pl.semaphore_wait(barrier, 2 + depth)

    def plane_start(buf):
        upper, lower = buf.at[q0, c, pl.ds(0, half)], buf.at[q0, c, pl.ds(half, half)]
        ax = same(upper, xpeer)
        by = same(lower, ypeer)
        bx = same(lower, xpeer)
        ay = same(upper, ypeer)
        oo = same(buf.at[q0, c], core)
        return ax, by, bx, ay, oo

    def plane_forward(buf, cps):
        ax, by, bx, ay, oo = cps
        ax.wait_recv()
        fa = same(buf.at[qx, c, pl.ds(0, half)], ypeer)
        by.wait_recv()
        fb = same(buf.at[qy, c, pl.ds(half, half)], xpeer)
        return bx, ay, oo, fa, fb

    def plane_core(buf, cps):
        bx, ay, oo, fa, fb = cps
        bx.wait_recv()
        ox = same(buf.at[qx, c], core)
        ay.wait_recv()
        oy = same(buf.at[qy, c], core)
        return oo, ox, oy, fa, fb

    def plane_last(buf, cps):
        oo, ox, oy, fa, fb = cps
        arrive([fa, fb])
        return oo, ox, oy, same(buf.at[qd, c], core)

    zsmall = z_gather(lambda q: b.pka.at[q])
    zin = z_gather(lambda q: b.wt.at[0, q])
    nstate = plane_start(b.nb)

    wgt = wg[...].T
    b.wt[1, f] = jnp.where(y == 0, wgt[:hl], wgt[hl:])
    b.wt[2, f] = wo[pl.ds(y * hl, hl), :]
    rowid = lax.broadcasted_iota(jnp.int32, (SLOT, 1), 0)
    b.db[q0, c] = jnp.where(rowid < lens[0], cot[...].astype(F32), 0.0).astype(BF16)
    z_relay(zsmall)
    nstate = plane_forward(b.nb, nstate)
    z_relay(zin)
    z_arrive(zsmall)
    locs = [unfolded(b.pka[i].astype(F32), hl) for i in range(depth)]
    pkl = jnp.concatenate(locs, axis=1)
    b.pkl[...] = pkl
    b.gb[c, x] = jnp.broadcast_to(pkl[GAIN_ROW : GAIN_ROW + 1], (8, cols))
    gx = same(b.gb.at[c, x], xpeer)
    dstate = plane_start(b.db)
    b.wst[...] = jnp.concatenate(
        [pkl[STEP_ROW:LOG_ROW], jnp.zeros((128 - RANK, cols), F32)], axis=0
    ).astype(BF16)
    b.wpt[...] = jnp.concatenate([pkl[:PROJ], jnp.zeros((128 - PROJ, cols), F32)], axis=0).astype(BF16)
    for n in range(STATE):
        row = -jnp.exp(pkl[LOG_ROW + n : LOG_ROW + n + 1]) * (1.0 / LN2)
        for et in range(2):
            b.rate[n, et] = jnp.broadcast_to(row[:, et * 128 : et * 128 + 128], (8, 128))
    nstate = plane_core(b.nb, nstate)
    b.ip[:, 0:8, :] = jnp.zeros((8, 8, cols), F32)
    b.dcp[SLOT : SLOT + 8, :] = jnp.zeros((8, cols), F32)
    b.ga[...] = jnp.zeros((STATE, 2, 8, 128), F32)
    b.sall[0] = jnp.zeros((STATE, 2, 16, 128), BF16)
    b.sg[...] = jnp.zeros((PACK, cols), F32)
    source = lax.broadcasted_iota(jnp.int32, (256, 2 * STATE * 128), 0)
    target = lax.broadcasted_iota(jnp.int32, (256, 2 * STATE * 128), 1)
    b.sel[...] = jnp.where(lax.rem(source, 128) == RANK + target // 128, 1.0, 0.0).astype(BF16)
    gx.wait_recv()
    gc = same(b.gb.at[c], core)
    gc.wait_recv()
    pieces = []
    for i in range(depth):
        for j in range(2):
            for k in range(2):
                pieces.append(b.gb[k, j, 0:1, i * piece : (i + 1) * piece])
    b.gl[...] = jnp.concatenate(pieces, axis=1)

    z_arrive(zin)
    zgate = z_gather(lambda q: b.wt.at[1, q])
    zout = z_gather(lambda q: b.wt.at[2, q])

    def scaled(w):
        full = b.wt[w].reshape(cols, width).astype(F32)
        b.ws[w] = (full * b.gl[...]).astype(BF16)

    scaled(0)
    arrive(plane_last(b.nb, nstate))

    def row_of(i):
        return b.pkl[i : i + 1, :]

    taps = [row_of(TAP_ROW + k) for k in range(CONV)]
    cbias = row_of(CONV_ROW)
    sbias = row_of(BIAS_ROW)
    skip = row_of(SKIP_ROW)

    def slot_rows(j):
        return pl.ds(pl.multiple_of(j * SLOT, SLOT), SLOT)

    def pair(ref, at):
        return jnp.concatenate([ref[0, at, :], ref[1, at, :]], axis=1)

    def unpair(ref, at, value):
        ref[0, at, :] = value[:, :128]
        ref[1, at, :] = value[:, 128:]

    def convolved(j):
        acc = jnp.broadcast_to(cbias, (SLOT, cols))
        for k in range(CONV):
            acc = acc + taps[k] * b.ip[j, 5 + k : 5 + k + SLOT, :]
        return acc

    b.ip[:, 8 : 8 + SLOT, :] = nt(b.nb[...].reshape(count, width), b.ws[0]).reshape(8, SLOT, cols)

    @pl.loop(0, 8)
    def _(j):
        acc = convolved(j)
        out = acc * sigmoid(acc)
        unpair(b.xc, slot_rows(j), out)
        b.cl[j] = out.astype(BF16)

    b.pp[...] = nt(b.cl[...].reshape(count, cols), b.wpt[...]).reshape(4, 2, SLOT, 128)

    def all_reduce(which, between):
        g = sets[which]
        g.s1[...] = b.pp[:, oc].astype(BF16)
        one = rcopy(g.s1, g.l1, core)
        between(0)
        one.wait_recv()
        total = b.pp[:, c] + g.l1[...].astype(F32)
        g.s2[...] = total.astype(BF16)
        two = [
            rcopy(g.s2.at[pl.ds(0, 2)], g.l2.at[pl.ds(0, 2)], xpeer),
            rcopy(g.s2.at[pl.ds(2, 2)], g.l2.at[pl.ds(2, 2)], ypeer),
        ]
        g.own[...] = total
        between(1)
        arrive(two)
        total = g.own[...] + g.l2[...].astype(F32)
        g.s3[...] = total.astype(BF16)
        three = [
            rcopy(g.s3.at[pl.ds(0, 2)], g.l3.at[pl.ds(0, 2)], ypeer),
            rcopy(g.s3.at[pl.ds(2, 2)], g.l3.at[pl.ds(2, 2)], xpeer),
        ]
        g.own[...] = total
        between(2)
        arrive(three)
        g.own[...] = g.own[...] + g.l3[...].astype(F32)
        four = rcopy(g.own, g.oth, core)
        between(3)
        four.wait_recv()

    dhold = [dstate]

    def pump_first(stage):
        if stage == 2:
            dhold[0] = plane_forward(b.db, dhold[0])
            z_relay(zgate)
        if stage == 3:
            dhold[0] = plane_core(b.db, dhold[0])

    all_reduce(1, pump_first)

    @pl.loop(0, 4)
    def _(q):
        for cc, src in ((c, sets[1].own), (oc, sets[1].oth)):
            j = 2 * q + cc
            proj = src[q]
            b.tm[pl.ds(j, SLOT, stride=8), :] = proj
            b.slow[slot_rows(j), :] = proj.astype(BF16)

    b.t1[...] = nn(b.slow[...], b.wst[...])

    @pl.loop(0, 8)
    def _(j):
        at = slot_rows(j)
        pre = b.t1[at, :] + sbias
        unpair(b.dt, at, jnp.maximum(pre, 0.0) + jnp.log1p(jnp.exp(-jnp.abs(pre))))

    tm = b.tm[...]
    high = tm.astype(BF16)
    spread = jnp.concatenate([high, (tm - high.astype(F32)).astype(BF16)], axis=1)
    both = nn(spread, b.sel[...])
    for i in range(2 * STATE):
        b.bc[:, i] = both[:, i * 128 : i * 128 + 128].reshape(SLOT, 8, 128)

    z_relay(zout)
    dstate = plane_last(b.db, dhold[0])
    zero = jnp.zeros((8, 128), F32)

    steps = 4

    def forward_steps(j, carry):
        base = steps * j
        ats = [pl.ds(base + i, 8, stride=SLOT) for i in range(steps)]
        size = [[b.dt[e, at, :] for e in range(2)] for at in ats]
        push = [[size[i][e] * b.xc[e, ats[i], :] for e in range(2)] for i in range(steps)]
        out = [[zero, zero] for _ in range(steps)]
        for n in range(STATE):
            for e in range(2):
                rate = b.rate[n, e]
                state = b.carried[n, e]
                kept = []
                for i in range(steps):
                    state = jnp.exp2(size[i][e] * rate) * state + push[i][e] * b.bc[base + i, n]
                    out[i][e] = out[i][e] + b.bc[base + i, STATE + n] * state
                    kept.append(state)
                b.carried[n, e] = state
                for p in range(steps // 2):
                    both_states = jnp.concatenate(kept[2 * p : 2 * p + 2], axis=0)
                    b.sall[(steps // 2) * j + p + 1, n, e] = both_states.astype(BF16)
        for i in range(steps):
            for e in range(2):
                b.ys[e, ats[i], :] = out[i][e]
        return carry

    b.carried[...] = jnp.zeros((STATE, 2, 8, 128), F32)
    lax.fori_loop(0, SLOT // steps, forward_steps, 0)

    arrive(dstate)
    z_arrive(zgate)
    scaled(1)
    b.t1[...] = nt(b.nb[...].reshape(count, width), b.ws[1])
    z_arrive(zout)
    b.t2[...] = nt(b.db[...].reshape(count, width), b.wt[2].reshape(cols, width))

    @pl.loop(0, 4)
    def _(q):
        for cc in range(2):
            at = slot_rows(2 * q + cc)
            gpre = b.t1[at, :]
            dgat = b.t2[at, :]
            conv = pair(b.xc, at)
            mixed = pair(b.ys, at) + skip * conv
            sig = sigmoid(gpre)
            act = gpre * sig
            b.go[q, cc] = (mixed * act).astype(BF16)
            dmix = dgat * act
            unpair(b.dm, at, dmix)
            slope = sig * (1.0 + gpre * (1.0 - sig))
            b.dg[q, cc] = (dgat * mixed * slope).astype(BF16)
            b.sg[SKIP_ROW : SKIP_ROW + 1, :] += jnp.sum(dmix * conv, axis=0, keepdims=True)

    def reduce_begin(dots, more):
        g = sets[3]

        def low_of(value, q):
            return (value + g.s1[q].astype(F32) if more else value).astype(BF16)

        g.s1[qd] = low_of(dots(lambda ref: ref[qd, oc]), qd)
        cores = [rcopy(g.s1.at[qd], g.l1.at[qd], core)]
        others = (qx, qy, q0)
        rest = dots(lambda ref: jnp.concatenate([ref[q, oc] for q in others], axis=0))
        for k, q in enumerate(others):
            g.s1[q] = low_of(rest[k * SLOT : (k + 1) * SLOT], q)
            cores.append(rcopy(g.s1.at[q], g.l1.at[q], core))
        mine = dots(lambda ref: ref[:, c].reshape(4 * SLOT, cols)).reshape(4, SLOT, width)
        b.sum[...] = b.sum[...] + mine if more else mine
        return cores

    def reduce_second(cores):
        g = sets[3]

        def chip(q, rows):
            return (b.sum[q, rows, :] + g.l1[q, rows, :].astype(F32)).astype(BF16)

        cores[0].wait_recv()
        g.sx[1] = chip(qd, top)
        x1 = rcopy(g.sx.at[1], g.lx.at[1], xpeer)
        g.sy[1] = chip(qd, low)
        y1 = rcopy(g.sy.at[1], g.ly.at[1], ypeer)
        cores[1].wait_recv()
        g.sx[0] = chip(qx, top)
        x0 = rcopy(g.sx.at[0], g.lx.at[0], xpeer)
        cores[2].wait_recv()
        g.sy[0] = chip(qy, low)
        y0 = rcopy(g.sy.at[0], g.ly.at[0], ypeer)
        return x1, y1, x0, y0

    def reduce_third(cps):
        g = sets[3]
        x1, y1, x0, y0 = cps
        x1.wait_recv()
        g.ty[...] = (b.sum[qy, top, :] + g.l1[qy, top, :].astype(F32) + g.lx[1].astype(F32)).astype(BF16)
        c1 = rcopy(g.ty, g.my, ypeer)
        y1.wait_recv()
        g.tx[...] = (b.sum[qx, low, :] + g.l1[qx, low, :].astype(F32) + g.ly[1].astype(F32)).astype(BF16)
        c2 = rcopy(g.tx, g.mx, xpeer)
        return x0, y0, c1, c2

    def reduce_end(cores, cps, out):
        g = sets[3]
        cores[3].wait_recv()
        arrive(cps)
        for rows, near, far_ref in ((top, g.lx, g.my), (low, g.ly, g.mx)):
            out[rows, :] = (
                b.sum[q0, rows, :]
                + g.l1[q0, rows, :].astype(F32)
                + near[0].astype(F32)
                + far_ref[...].astype(F32)
            ).astype(BF16)

    def weight_grad(w, lhs, rhs, gained):
        grad = tn(lhs[...].reshape(count, cols), rhs[...].reshape(count, width))
        b.gws[w] = (grad * b.gl[...] if gained else grad).astype(BF16).reshape(depth, hl, width)
        return grad

    def gain_grad(w, grad):
        return jnp.sum(grad * b.wt[w].reshape(cols, width).astype(F32), axis=0, keepdims=True)

    def weight_send(w, at):
        return z_scatter(
            lambda q: b.gws.at[w, q, at], lambda k: b.gwl.at[w, k, at], b.gwx.at[w, at]
        )

    def weight_sum(w, st, at):
        gout[w, y, at, :] = z_sum(st, b.gws[w, f, at, :].astype(F32)).astype(BF16)
        return same(gout.at[w, y, at], ypeer)

    every = pl.ds(0, hl)

    weight_grad(2, b.go, b.db, False)
    zgo = z_direct(weight_send(2, every))
    grad = weight_grad(1, b.dg, b.nb, True)
    zgg = z_direct(weight_send(1, every))
    b.vv[...] = gain_grad(1, grad)
    bone = reduce_begin(lambda pick: nn(pick(b.go), b.wt[2].reshape(cols, width)), False)

    def backward_pair(j, carry):
        k = SLOT // 2 - 1 - j
        ats = [pl.ds(2 * k + i, 8, stride=SLOT) for i in range(2)]
        size = [[b.dt[e, at, :] for e in range(2)] for at in ats]
        conv = [[b.xc[e, at, :] for e in range(2)] for at in ats]
        dmix = [[b.dm[e, at, :] for e in range(2)] for at in ats]
        push = [jnp.concatenate([size[i][e] * conv[i][e] for i in range(2)], axis=0).astype(BF16) for e in range(2)]
        dlow = [jnp.concatenate([dmix[i][e] for i in range(2)], axis=0).astype(BF16) for e in range(2)]
        rate_sum = [[zero, zero], [zero, zero]]
        weighted = [[zero, zero], [zero, zero]]
        new = []
        for n in range(STATE):
            inm = [b.bc[2 * k + i, n] for i in range(2)]
            outm = [b.bc[2 * k + i, STATE + n] for i in range(2)]
            dins, douts = [], []
            for e in range(2):
                rate = b.rate[n, e]
                here = b.sall[k + 1, n, e]
                before = [b.sall[k, n, e].astype(F32)[8:16], here.astype(F32)[0:8]]
                back = carry[2 * n + e]
                lams = [None, None]
                acc = b.ga[n, e]
                for i in (1, 0):
                    lam = outm[i] * dmix[i][e] + back
                    back = jnp.exp2(size[i][e] * rate) * lam
                    grad = back * before[i]
                    rate_sum[i][e] = rate_sum[i][e] + grad * rate
                    weighted[i][e] = weighted[i][e] + lam * inm[i]
                    acc = acc + grad * size[i][e]
                    lams[i] = lam
                b.ga[n, e] = acc
                new.append(back)
                dins.append(jnp.concatenate(lams, axis=0).astype(BF16) * push[e])
                douts.append(dlow[e] * here)
            b.sall[k + 1, n, 0] = dins[0] + dins[1]
            b.sall[k + 1, n, 1] = douts[0] + douts[1]
        for i in range(2):
            for e in range(2):
                b.ys[e, ats[i], :] = rate_sum[i][e] * LN2 + conv[i][e] * weighted[i][e]
                b.xc[e, ats[i], :] = size[i][e] * weighted[i][e]
        return tuple(new)

    carry = tuple(zero for _ in range(2 * STATE))
    carry = lax.fori_loop(0, SLOT // 8, backward_pair, carry)
    z_absorb(zgo)
    btwo = reduce_second(bone)
    carry = lax.fori_loop(SLOT // 8, 3 * SLOT // 8, backward_pair, carry)
    z_absorb(zgg)
    bthree = reduce_third(btwo)
    carry = lax.fori_loop(3 * SLOT // 8, SLOT // 2, backward_pair, carry)

    parts = [b.sall[1:, n, k].reshape(count, 128) for k in range(2) for n in range(STATE)]
    b.tm[...] = nt(jnp.concatenate(parts, axis=1), b.sel[0:128, :])

    b.t1[...] = nn(b.slow[...], b.wst[...])

    @pl.loop(0, 8)
    def _(j):
        at = slot_rows(j)
        dpre = pair(b.ys, at) * sigmoid(b.t1[at, :] + sbias)
        b.sg[BIAS_ROW : BIAS_ROW + 1, :] += jnp.sum(dpre, axis=0, keepdims=True)
        b.dsl[j] = dpre.astype(BF16)

    b.pp[...] = nt(b.dsl[...].reshape(count, cols), b.wst[...]).reshape(4, 2, SLOT, 128)

    @pl.loop(0, 4)
    def _(q):
        for cc in range(2):
            b.pp[q, cc] += b.tm[pl.ds(2 * q + cc, SLOT, stride=8), :]

    hold = [None, None]
    gate_dot = lambda pick: nn(pick(b.dg), b.ws[1])

    def pump_second(stage):
        if stage == 0:
            grad = tn(b.slow[...], b.dsl[...].reshape(count, cols))
            b.sg[STEP_ROW:LOG_ROW, :] = grad[:RANK]
        if stage == 1:
            reduce_end(bone, bthree, bsum)
            for n in range(STATE):
                parts = [jnp.sum(b.ga[n, e] * b.rate[n, e], axis=0, keepdims=True) for e in range(2)]
                b.sg[LOG_ROW + n : LOG_ROW + n + 1, :] = jnp.concatenate(parts, axis=1) * LN2

            @pl.loop(0, 8)
            def _(j):
                at = slot_rows(j)
                cpre = convolved(j)
                sig = sigmoid(cpre)
                b.t2[at, :] = sig * (1.0 + cpre * (1.0 - sig))
                unpair(b.dm, at, pair(b.xc, at) + pair(b.dm, at) * skip)

        if stage == 2:
            hold[0] = weight_sum(2, zgo, every)
            settle([*bone, *btwo, *bthree[2:]])
            sets[3].s1[...] = gate_dot(lambda ref: ref[:, oc].reshape(4 * SLOT, cols)).astype(BF16).reshape(4, SLOT, width)
            b.sum[...] = gate_dot(lambda ref: ref[:, c].reshape(4 * SLOT, cols)).reshape(4, SLOT, width)
        if stage == 3:
            hold[1] = weight_sum(1, zgg, every)

    all_reduce(2, pump_second)

    @pl.loop(0, 4)
    def _(q):
        for cc, src in ((c, sets[2].own), (oc, sets[2].oth)):
            b.dpj[slot_rows(2 * q + cc), :] = src[q].astype(BF16)

    b.t1[...] = nn(b.dpj[...], b.wpt[...])

    @pl.loop(0, 4)
    def _(q):
        for cc in range(2):
            j = 2 * q + cc
            at = slot_rows(j)
            dpre = (pair(b.dm, at) + b.t1[at, :]) * b.t2[at, :]
            b.dcp[0:SLOT, :] = dpre
            sums = [jnp.sum(dpre * b.ip[j, 5 + k : 5 + k + SLOT, :], axis=0, keepdims=True) for k in range(CONV)]
            sums.append(jnp.sum(dpre, axis=0, keepdims=True))
            b.sg[TAP_ROW : CONV_ROW + 1, :] += jnp.concatenate(sums, axis=0)
            dinner = taps[CONV - 1] * dpre
            for k in range(CONV - 1):
                dinner = dinner + taps[k] * b.dcp[CONV - 1 - k : CONV - 1 - k + SLOT, :]
            b.di[q, cc] = dinner.astype(BF16)

    grad = weight_grad(0, b.di, b.nb, True)
    first, second = pl.ds(0, hl // 2), pl.ds(hl // 2, hl // 2)
    zgi = [weight_send(0, first), weight_send(0, second)]
    for st in zgi:
        z_direct(st)
    total = b.vv[...] + gain_grad(0, grad)
    for i in range(8):
        b.vs[0, i : i + 1, :] = total[:, i * 128 : i * 128 + 128]
    v1 = rcopy(b.vs.at[0], b.vl.at[0], xpeer)
    done = reduce_begin(lambda pick: nn(pick(b.di), b.ws[0]), True)
    v1.wait_recv()
    b.vs[1] = b.vs[0] + b.vl[0]
    v2 = rcopy(b.vs.at[1], b.vl.at[1], ypeer)
    dtwo = reduce_second(done)
    z_absorb(zgi[0])
    z_absorb(zgi[1])
    grad = tn(b.dpj[...], b.cl[...].reshape(count, cols))
    b.sg[0:PROJ, :] = grad[:PROJ]
    for i in range(depth):
        b.sgs[i] = folded(b.sg[:, i * hl : (i + 1) * hl], hl)
    zgs = z_direct(z_scatter(lambda q: b.sgs.at[q], lambda k: b.sgl.at[k], b.sgx))
    v2.wait_recv()
    b.vs[2] = b.vs[1] + b.vl[1]
    v3 = rcopy(b.vs.at[2], b.vl.at[2], core)
    dthree = reduce_third(dtwo)
    v3.wait_recv()
    b.vz[f] = b.vs[2] + b.vl[2]
    v4 = z_gather(lambda q: b.vz.at[q])
    yin = [weight_sum(0, zgi[0], first)]
    z_absorb(zgs)
    yin.append(weight_sum(0, zgi[1], second))
    sout[y] = z_sum(zgs, b.sgs[f].astype(F32)).astype(BF16)
    ysmall = same(sout.at[y], ypeer)
    z_relay(v4)
    reduce_end(done, dthree, dsc)
    z_arrive(v4)
    total = b.vz[0]
    for k in range(1, depth):
        total = total + b.vz[k]
    vout[...] = total
    arrive(hold + yin + [ysmall])
    for cp in started:
        cp.wait_send()


def last_kernel(hl, piece, tok, cot, lens, bsum, dsc, gout, sout, vout, *outs):
    (out, dtok, ggain, ginner, ggate, gconv, gcb, gproj, gstep, gsb, glog, gskip, gwout) = outs
    s = lax.axis_index("shard")
    t32 = tok[...].astype(F32)
    rowid = lax.broadcasted_iota(jnp.int32, (SLOT, 1), 0)
    out[...] = (t32 + jnp.where(rowid < lens[0], bsum[...].astype(F32), 0.0)).astype(BF16)
    inv = lax.rsqrt(jnp.mean(t32 * t32, axis=1, keepdims=True) + EPS)
    ds = dsc[...].astype(F32)
    mean = jnp.mean(ds * t32, axis=1, keepdims=True)
    dtok[...] = cot[...].astype(F32) + inv * ds - t32 * (inv * inv * inv * mean)
    width = tok.shape[1]
    el = 2 * hl
    ginner[...] = gout[0].reshape(el, width).T.astype(F32)
    ggate[...] = gout[1].reshape(el, width).T.astype(F32)
    gwout[...] = gout[2].reshape(el, width).astype(F32)
    small = sout[...].astype(F32)
    halves = [jnp.concatenate([small[k][:, :hl], small[k][:, hl:el]], axis=0) for k in range(2)]
    both = jnp.concatenate(halves, axis=1)
    gproj[...] = both[:PROJ]
    gstep[...] = both[STEP_ROW:LOG_ROW]
    glog[...] = both[LOG_ROW:TAP_ROW]
    gconv[...] = both[TAP_ROW:CONV_ROW]
    gcb[...] = both[CONV_ROW : CONV_ROW + 1].reshape(el)
    gsb[...] = both[BIAS_ROW : BIAS_ROW + 1].reshape(el)
    gskip[...] = both[SKIP_ROW : SKIP_ROW + 1].reshape(el)
    per = 128 // piece
    vec = vout[...]
    rows = lax.broadcasted_iota(jnp.int32, (8, 128), 0)
    row = jnp.sum(jnp.where(rows == s // per, vec, 0.0), axis=0, keepdims=True)
    pick = jnp.zeros((1, piece), F32)
    for i in range(per):
        pick = jnp.where(lax.rem(s, per) == i, row[:, i * piece : (i + 1) * piece], pick)
    ggain[...] = pick.reshape(piece)


def make_local(replicas, shards):
    depth = shards // 4

    def local(
        tokens, norm_gain, w_inner, w_gate, conv_weight, conv_bias, w_proj, w_step, step_bias, a_log, skip_gain,
        w_out, cotangent, lengths,
    ):
        width = tokens.shape[1]
        el = w_inner.shape[1]
        hl = el // 2
        piece = norm_gain.shape[0]
        spec = buffers(depth, hl, width, shards, piece)
        nsem = 96 + 16 * depth
        vm = pl.BlockSpec(memory_space=pltpu.VMEM)
        sm = pl.BlockSpec(memory_space=pltpu.SMEM)
        sds = jax.ShapeDtypeStruct
        mid = pl.pallas_call(
            functools.partial(main_kernel, [tuple(group) for group in spec], depth, hl, piece, nsem),
            out_shape=(
                pltpu.VMEM((SLOT, width), BF16),
                pltpu.VMEM((SLOT, width), BF16),
                pltpu.VMEM((3, 2, hl, width), BF16),
                pltpu.VMEM((2, PACK // 2, 128), BF16),
                pltpu.VMEM((8, 128), F32),
            ),
            in_specs=[vm] * 13 + [sm],
            out_specs=(vm,) * 5,
            scratch_shapes=[pltpu.VMEM(shape, kind) for group in spec for shape, kind in group.values()]
            + [pltpu.SemaphoreType.DMA((nsem,)), pltpu.SemaphoreType.DMA((nsem,))],
            compiler_params=pltpu.CompilerParams(
                collective_id=0, has_side_effects=True, vmem_limit_bytes=61 << 20
            ),
            name="layer",
        )(
            tokens, cotangent, w_inner, w_gate, w_out, w_proj.T, w_step, a_log, conv_weight, conv_bias, step_bias,
            skip_gain, norm_gain, lengths,
        )
        bsum, dsc, gout, sout, vout = mid
        if replicas > 2:
            groups = [[r for r in range(replicas) if r % 2 == k] for k in range(2)]
            gout, sout, vout = (
                lax.psum(v.astype(F32), "replica", axis_index_groups=groups) for v in (gout, sout, vout)
            )
        outs = pl.pallas_call(
            functools.partial(last_kernel, hl, piece),
            out_shape=(
                sds((SLOT, width), BF16),
                sds((SLOT, width), F32),
                sds((piece,), F32),
                sds((width, el), F32),
                sds((width, el), F32),
                sds((CONV, el), F32),
                sds((el,), F32),
                sds((PROJ, el), F32),
                sds((RANK, el), F32),
                sds((el,), F32),
                sds((STATE, el), F32),
                sds((el,), F32),
                sds((el, width), F32),
            ),
            in_specs=[vm, vm, sm] + [vm] * 5,
            out_specs=(vm,) * 13,
            compiler_params=pltpu.CompilerParams(vmem_limit_bytes=16 << 20),
            name="results",
        )(tokens, cotangent, lengths, bsum, dsc, gout, sout, vout)
        return outs[:7] + (outs[7].T,) + outs[8:]

    return local


def solution(mesh):
    return jax.shard_map(
        make_local(mesh.shape["replica"], mesh.shape["shard"]),
        mesh=mesh,
        in_specs=(
            P(("replica", "shard"), None),
            P("shard"),
            P(None, "shard"),
            P(None, "shard"),
            P(None, "shard"),
            P("shard"),
            P("shard", None),
            P(None, "shard"),
            P("shard"),
            P(None, "shard"),
            P("shard"),
            P("shard", None),
            P(("replica", "shard"), None),
            P(("replica", "shard")),
        ),
        out_specs=(
            P(("replica", "shard"), None),
            P(("replica", "shard"), None),
            P("shard"),
            P(None, "shard"),
            P(None, "shard"),
            P(None, "shard"),
            P("shard"),
            P("shard", None),
            P(None, "shard"),
            P("shard"),
            P(None, "shard"),
            P("shard"),
            P("shard", None),
        ),
        check_vma=False,
    )
```

```python
import functools
import math
from types import SimpleNamespace

import jax
import jax.numpy as jnp
from jax import lax
from jax.experimental import pallas as pl
from jax.experimental.pallas import tpu as pltpu
from jax.sharding import PartitionSpec as P

RANK = 64
STATE = 16
CONV = 4
SLOT = 128
EPS = 1e-05
LN2 = math.log(2.0)
PROJ = RANK + 2 * STATE
PACK = 192
STEP_ROW = PROJ
LOG_ROW = STEP_ROW + RANK
TAP_ROW = LOG_ROW + STATE
CONV_ROW = TAP_ROW + CONV
BIAS_ROW = CONV_ROW + 1
SKIP_ROW = BIAS_ROW + 1
GAIN_ROW = SKIP_ROW + 1
MESH = pl.DeviceIdType.MESH
F32 = jnp.float32
BF16 = jnp.bfloat16


def sigmoid(value):
    return 0.5 * jnp.tanh(0.5 * value) + 0.5


def nt(left, right):
    return lax.dot_general(left, right, (((1,), (1,)), ((), ())), preferred_element_type=F32)


def nn(left, right):
    return lax.dot_general(left, right, (((1,), (0,)), ((), ())), preferred_element_type=F32)


def tn(left, right):
    return lax.dot_general(left, right, (((0,), (0,)), ((), ())), preferred_element_type=F32)


def buffers(depth, hl, width, shards, piece):
    cols = depth * hl
    rows = 8 * SLOT
    def reduce_small(part):
        low, full = ((4, part, 128), BF16), ((4, part, 128), F32)
        return dict(s1=low, l1=low, s2=low, l2=low, s3=low, l3=low, own=full, oth=full)

    reduce_large = dict(
        s1=((4, SLOT, width), BF16),
        l1=((4, SLOT, width), BF16),
        sx=((2, SLOT // 2, width), BF16),
        sy=((2, SLOT // 2, width), BF16),
        lx=((2, SLOT // 2, width), BF16),
        ly=((2, SLOT // 2, width), BF16),
        tx=((SLOT // 2, width), BF16),
        ty=((SLOT // 2, width), BF16),
        mx=((SLOT // 2, width), BF16),
        my=((SLOT // 2, width), BF16),
    )
    shapes = dict(
        wt=((3, depth, hl, width), BF16),
        ws=((2, cols, width), BF16),
        pka=((depth, PACK // 2, 128), BF16),
        wpt=((128, cols), BF16),
        gb=((2, 2, 8, cols), F32),
        t1=((rows, cols), F32),
        t2=((rows, cols), F32),
        gl=((1, width), F32),
        nb=((4, 2, SLOT, width), BF16),
        db=((4, 2, SLOT, width), BF16),
        pkl=((PACK, cols), F32),
        wst=((128, cols), BF16),
        rate=((STATE, 2, 8, 128), F32),
        ip=((8, SLOT + 8, cols), F32),
        dcp=((8, SLOT + 8, cols), F32),
        gacc=((cols, width), F32),
        tm=((rows, 128), F32),
        sel=((256, 2 * STATE * 128), BF16),
        bc=((SLOT, 2 * STATE, 8, 128), F32),
        sall=((SLOT // 2 + 1, STATE, 2, 16, 128), BF16),
        cl=((8, SLOT, cols), BF16),
        xc=((2, rows, 128), F32),
        pp=((4, 2, SLOT, 128), F32),
        slow=((8, SLOT, 128), BF16),
        dpj=((8, SLOT, 128), BF16),
        dt=((2, rows, 128), F32),
        ys=((2, rows, 128), F32),
        dm=((2, rows, 128), F32),
        ga=((STATE, 2, 8, 128), F32),
        carried=((STATE, 2, 8, 128), F32),
        go=((4, 2, SLOT, cols), BF16),
        dg=((4, 2, SLOT, cols), BF16),
        di=((4, 2, SLOT, cols), BF16),
        dsl=((8, SLOT, cols), BF16),
        gws=((3, depth, hl, width), BF16),
        gwl=((3, depth - 1, hl, width), BF16),
        gwx=((3, hl, width), BF16),
        sg=((PACK, cols), F32),
        sgs=((depth, PACK // 2, 128), BF16),
        sgl=((depth - 1, PACK // 2, 128), BF16),
        sgx=((PACK // 2, 128), BF16),
        vv=((1, width), F32),
        sum=((4, SLOT, width), F32),
        vs=((4, 8, 128), F32),
        vl=((3, 8, 128), F32),
        vz=((depth, 8, 128), F32),
    )
    return [shapes, reduce_small(SLOT), reduce_small(SLOT // 2), reduce_large, reduce_small(SLOT // 2)]


def main_kernel(names, depth, hl, piece, nsem, *refs):
    (tok, cot, win, wg, wo, wproj, wstep, alog, convw, convb, stepb, skipg, gain, lens) = refs[:14]
    (bsum, dsc, gout, sout, vout) = refs[14:19]
    send_sems, recv_sems = refs[-2:]
    sets, at = [], 19
    for group in names:
        sets.append(SimpleNamespace(**dict(zip(group, refs[at:]))))
        at += len(group)
    b = sets[0]
    width = tok.shape[1]
    cols = depth * hl
    el = 2 * hl
    count = 8 * SLOT
    half = SLOT // 2

    r = lax.axis_index("replica")
    s = lax.axis_index("shard")
    y = lax.rem(r, 2)
    f = s // 4
    x = lax.rem(s // 2, 2)
    c = lax.rem(s, 2)
    core = (r, s + 1 - 2 * c)
    xpeer = (r, s + 2 - 4 * x)
    ypeer = (r + 1 - 2 * y, s)
    zpos = [lax.rem(f + k, depth) for k in range(1, depth)]
    zpeers = [(r, s + 4 * (q - f)) for q in zpos]
    q0 = y * 2 + x
    qx = y * 2 + 1 - x
    qy = (1 - y) * 2 + x
    qd = (1 - y) * 2 + 1 - x
    oc = 1 - c
    top, low = slice(0, half), slice(half, SLOT)

    counter = [0]
    started = []
    line = depth == 4
    ends = (f == 0) | (f == 3)
    inner = (f == 1) | (f == 2)

    def ticket():
        counter[0] += 1
        assert counter[0] <= nsem
        return counter[0] - 1

    def remote(src, dst, dev, send, recv):
        return pltpu.make_async_remote_copy(
            src_ref=src,
            dst_ref=dst,
            send_sem=send_sems.at[send],
            recv_sem=recv_sems.at[recv],
            device_id=dev,
            device_id_type=MESH,
        )

    def rcopy(src, dst, dev):
        i = ticket()
        cp = remote(src, dst, dev, i, i)
        cp.start()
        started.append(cp)
        return cp

    def same(ref, dev):
        return rcopy(ref, ref, dev)

    def settle(cps):
        for cp in cps:
            cp.wait_send()
            started[:] = [other for other in started if other is not cp]

    def arrive(cps):
        for cp in cps:
            cp.wait_recv()

    def only(when, cp):
        @pl.when(when)
        def _():
            cp.start()

        def wait_send():
            @pl.when(when)
            def _():
                cp.wait_send()

        started.append(SimpleNamespace(wait_send=wait_send))

    def far(k):
        return ((f == 0) & (k == 3)) | ((f == 3) & (k == 1))

    def far_from(k):
        return ((f == 0) & (k == 1)) | ((f == 3) & (k == 3))

    def z_gather(piece):
        ids = [ticket() for _ in range(depth)]
        cps = {}
        for k in sorted(range(1, depth), key=lambda k: k != 2):
            cps[k] = remote(piece(f), piece(f), zpeers[k - 1], ids[k], ids[k])
            if line and k != 2:
                only(jnp.logical_not(far(k)), cps[k])
            else:
                cps[k].start()
                started.append(cps[k])
        return SimpleNamespace(piece=piece, ids=ids, cps=cps)

    def z_relay(st):
        if line:
            st.cps[2].wait_recv()
            q = 3 * (2 - jnp.where(inner, f, 1))
            near = jnp.where(inner, 2 * f - 1, 1)
            only(inner, remote(st.piece(q), st.piece(q), (r, s + 4 * (3 - q - f)), st.ids[0], st.ids[1] + near - 1))

    def z_arrive(st):
        for k in range(1, depth):
            if not (line and k == 2):
                st.cps[k].wait_recv()

    def z_scatter(send, land, extra):
        ids = [ticket() for _ in range(depth)]
        cps = {k: remote(send(zpos[k - 1]), land(k - 1), zpeers[k - 1], ids[k], ids[k]) for k in range(1, depth)}
        st = SimpleNamespace(send=send, land=land, extra=extra, cps=cps)
        if not line:
            for cp in cps.values():
                cp.start()
                started.append(cp)
            return st
        st.cross = remote(send(3 - f), extra, (r, s + 4 - 8 * (f // 3)), ids[0], ids[0])
        only(ends, st.cross)
        return st

    def z_direct(st):
        if line:
            only(ends, st.cps[2])
            for k in (1, 3):
                only(jnp.logical_not(far(k)), st.cps[k])
        return st

    def z_absorb(st):
        if line:

            @pl.when(inner)
            def _():
                st.cross.wait_recv()
                target = st.send(zpos[1])
                target[...] = (target[...].astype(F32) + st.extra[...].astype(F32)).astype(BF16)

            only(inner, st.cps[2])

    def z_sum(st, own):
        total = own
        for k in range(1, depth):
            if line and k != 2:

                @pl.when(jnp.logical_not(far_from(k)))
                def _():
                    st.cps[k].wait_recv()

            else:
                st.cps[k].wait_recv()
        for k in range(1, depth):
            value = st.land(k - 1)[...].astype(F32)
            total = total + (jnp.where(far_from(k), 0.0, value) if line and k != 2 else value)
        return total

    barrier = pltpu.get_barrier_semaphore()
    reach = [core, xpeer, ypeer]
    for dev in reach:
        pl.semaphore_signal(barrier, inc=1, device_id=dev, device_id_type=MESH)
    for k in range(1, depth):

        def hello():
            pl.semaphore_signal(barrier, inc=1, device_id=zpeers[k - 1], device_id_type=MESH)

        if line and k != 2:
            pl.when(jnp.logical_not(far(k)))(hello)
        else:
            hello()

    def lanes(value, n):
        value = value.astype(F32)
        if value.shape[1] == n:
            return value
        return jnp.concatenate([value, jnp.zeros((value.shape[0], n - value.shape[1]), F32)], axis=1)

    def folded(value, n):
        both = jnp.concatenate([value[: PACK // 2], value[PACK // 2 :]], axis=1)
        return lanes(both, 128).astype(BF16)

    def unfolded(value, n):
        return jnp.concatenate([value[:, :n], value[:, n : 2 * n]], axis=0)

    rows = [wproj[...], wstep[...], alog[...], convw[...]]
    rows += [v[...].reshape(1, el) for v in (convb, stepb, skipg)]
    rows = [v.astype(F32) for v in rows]
    rows.append(jnp.zeros((PACK - GAIN_ROW, el), F32))
    pack = jnp.concatenate(rows, axis=0)
    mine = jnp.where(y == 0, pack[:, :hl], pack[:, hl:])
    own_gain = gain[...].reshape(1, piece).astype(F32)
    rowid = lax.broadcasted_iota(jnp.int32, (PACK, 1), 0)
    b.pka[f] = folded(jnp.where(rowid == GAIN_ROW, own_gain, mine), hl)
    wint = win[...].T
    b.wt[0, f] = jnp.where(y == 0, wint[:hl], wint[hl:])
    t32 = tok[...].astype(F32)
    inv = lax.rsqrt(jnp.mean(t32 * t32, axis=1, keepdims=True) + EPS)
    b.nb[q0, c] = (t32 * inv).astype(BF16)

    if line:
        for w in range(3):
            for k in (1, 3):

                @pl.when(far_from(k))
                def _():
                    b.gwl[w, k - 1] = jnp.zeros((hl, width), BF16)

        for k in (1, 3):

            @pl.when(far_from(k))
            def _():
                b.sgl[k - 1] = jnp.zeros((PACK // 2, 128), BF16)

        pl.semaphore_wait(barrier, jnp.where(ends, 5, 6))
    else:
        pl.semaphore_wait(barrier, 2 + depth)

    def plane_start(buf):
        upper, lower = buf.at[q0, c, pl.ds(0, half)], buf.at[q0, c, pl.ds(half, half)]
        ax = same(upper, xpeer)
        by = same(lower, ypeer)
        bx = same(lower, xpeer)
        ay = same(upper, ypeer)
        oo = same(buf.at[q0, c], core)
        return ax, by, bx, ay, oo

    def plane_forward(buf, cps):
        ax, by, bx, ay, oo = cps
        ax.wait_recv()
        fa = same(buf.at[qx, c, pl.ds(0, half)], ypeer)
        by.wait_recv()
        fb = same(buf.at[qy, c, pl.ds(half, half)], xpeer)
        return bx, ay, oo, fa, fb

    def plane_core(buf, cps):
        bx, ay, oo, fa, fb = cps
        bx.wait_recv()
        ox = same(buf.at[qx, c], core)
        ay.wait_recv()
        oy = same(buf.at[qy, c], core)
        return oo, ox, oy, fa, fb

    def plane_last(buf, cps):
        oo, ox, oy, fa, fb = cps
        arrive([fa, fb])
        return oo, ox, oy, same(buf.at[qd, c], core)

    zsmall = z_gather(lambda q: b.pka.at[q])
    zin = z_gather(lambda q: b.wt.at[0, q])
    nstate = plane_start(b.nb)

    wgt = wg[...].T
    b.wt[1, f] = jnp.where(y == 0, wgt[:hl], wgt[hl:])
    b.wt[2, f] = wo[pl.ds(y * hl, hl), :]
    rowid = lax.broadcasted_iota(jnp.int32, (SLOT, 1), 0)
    b.db[q0, c] = jnp.where(rowid < lens[0], cot[...].astype(F32), 0.0).astype(BF16)
    z_relay(zsmall)
    nstate = plane_forward(b.nb, nstate)
    z_relay(zin)
    z_arrive(zsmall)
    locs = [unfolded(b.pka[i].astype(F32), hl) for i in range(depth)]
    pkl = jnp.concatenate(locs, axis=1)
    b.pkl[...] = pkl
    b.gb[c, x] = jnp.broadcast_to(pkl[GAIN_ROW : GAIN_ROW + 1], (8, cols))
    gx = same(b.gb.at[c, x], xpeer)
    dstate = plane_start(b.db)
    b.wst[...] = jnp.concatenate(
        [pkl[STEP_ROW:LOG_ROW], jnp.zeros((128 - RANK, cols), F32)], axis=0
    ).astype(BF16)
    b.wpt[...] = jnp.concatenate([pkl[:PROJ], jnp.zeros((128 - PROJ, cols), F32)], axis=0).astype(BF16)
    for n in range(STATE):
        row = -jnp.exp(pkl[LOG_ROW + n : LOG_ROW + n + 1]) * (1.0 / LN2)
        for et in range(2):
            b.rate[n, et] = jnp.broadcast_to(row[:, et * 128 : et * 128 + 128], (8, 128))
    nstate = plane_core(b.nb, nstate)
    b.ip[:, 0:8, :] = jnp.zeros((8, 8, cols), F32)
    b.dcp[:, SLOT : SLOT + 8, :] = jnp.zeros((8, 8, cols), F32)
    b.ga[...] = jnp.zeros((STATE, 2, 8, 128), F32)
    b.sall[0] = jnp.zeros((STATE, 2, 16, 128), BF16)
    b.sg[...] = jnp.zeros((PACK, cols), F32)
    source = lax.broadcasted_iota(jnp.int32, (256, 2 * STATE * 128), 0)
    target = lax.broadcasted_iota(jnp.int32, (256, 2 * STATE * 128), 1)
    b.sel[...] = jnp.where(lax.rem(source, 128) == RANK + target // 128, 1.0, 0.0).astype(BF16)
    gx.wait_recv()
    gc = same(b.gb.at[c], core)
    gc.wait_recv()
    pieces = []
    for i in range(depth):
        for j in range(2):
            for k in range(2):
                pieces.append(b.gb[k, j, 0:1, i * piece : (i + 1) * piece])
    b.gl[...] = jnp.concatenate(pieces, axis=1)

    z_arrive(zin)
    zgate = z_gather(lambda q: b.wt.at[1, q])
    zout = z_gather(lambda q: b.wt.at[2, q])

    def scaled(w):
        full = b.wt[w].reshape(cols, width).astype(F32)
        b.ws[w] = (full * b.gl[...]).astype(BF16)

    scaled(0)
    arrive(plane_last(b.nb, nstate))

    def row_of(i):
        return b.pkl[i : i + 1, :]

    taps = [row_of(TAP_ROW + k) for k in range(CONV)]
    cbias = row_of(CONV_ROW)
    sbias = row_of(BIAS_ROW)
    skip = row_of(SKIP_ROW)

    def slot_rows(j):
        return pl.ds(pl.multiple_of(j * SLOT, SLOT), SLOT)

    def pair(ref, at):
        return jnp.concatenate([ref[0, at, :], ref[1, at, :]], axis=1)

    def unpair(ref, at, value):
        ref[0, at, :] = value[:, :128]
        ref[1, at, :] = value[:, 128:]

    def convolved(j, begin, size):
        acc = jnp.broadcast_to(cbias, (size, cols))
        for k in range(CONV):
            acc = acc + taps[k] * b.ip[j, 5 + k + begin : 5 + k + begin + size, :]
        return acc

    b.ip[:, 8 : 8 + SLOT, :] = nt(b.nb[...].reshape(count, width), b.ws[0]).reshape(8, SLOT, cols)

    @pl.loop(0, 8)
    def _(j):
        acc = convolved(j, 0, SLOT)
        out = acc * sigmoid(acc)
        unpair(b.xc, slot_rows(j), out)
        b.cl[j] = out.astype(BF16)

    b.pp[...] = nt(b.cl[...].reshape(count, cols), b.wpt[...]).reshape(4, 2, SLOT, 128)

    def all_reduce(which, rows):
        g = sets[which]
        flight = []

        def first():
            g.s1[...] = b.pp[:, oc, rows, :].astype(BF16)
            flight[:] = [rcopy(g.s1, g.l1, core)]

        def second():
            arrive(flight)
            total = b.pp[:, c, rows, :] + g.l1[...].astype(F32)
            g.s2[...] = total.astype(BF16)
            flight[:] = [
                rcopy(g.s2.at[pl.ds(0, 2)], g.l2.at[pl.ds(0, 2)], xpeer),
                rcopy(g.s2.at[pl.ds(2, 2)], g.l2.at[pl.ds(2, 2)], ypeer),
            ]
            g.own[...] = total

        def third():
            arrive(flight)
            total = g.own[...] + g.l2[...].astype(F32)
            g.s3[...] = total.astype(BF16)
            flight[:] = [
                rcopy(g.s3.at[pl.ds(0, 2)], g.l3.at[pl.ds(0, 2)], ypeer),
                rcopy(g.s3.at[pl.ds(2, 2)], g.l3.at[pl.ds(2, 2)], xpeer),
            ]
            g.own[...] = total

        def fourth():
            arrive(flight)
            g.own[...] = g.own[...] + g.l3[...].astype(F32)
            flight[:] = [rcopy(g.own, g.oth, core)]

        return [first, second, third, fourth, lambda: arrive(flight)]

    summed = all_reduce(1, slice(0, SLOT))
    summed[0]()
    summed[1]()
    summed[2]()
    dstate = plane_forward(b.db, dstate)
    z_relay(zgate)
    summed[3]()
    dstate = plane_core(b.db, dstate)
    summed[4]()

    @pl.loop(0, 4)
    def _(q):
        for cc, src in ((c, sets[1].own), (oc, sets[1].oth)):
            j = 2 * q + cc
            proj = src[q]
            b.tm[pl.ds(j, SLOT, stride=8), :] = proj
            b.slow[j] = proj.astype(BF16)

    b.t1[...] = nn(b.slow[...].reshape(count, 128), b.wst[...])

    @pl.loop(0, 8)
    def _(j):
        at = slot_rows(j)
        pre = b.t1[at, :] + sbias
        unpair(b.dt, at, jnp.maximum(pre, 0.0) + jnp.log1p(jnp.exp(-jnp.abs(pre))))

    tm = b.tm[...]
    high = tm.astype(BF16)
    spread = jnp.concatenate([high, (tm - high.astype(F32)).astype(BF16)], axis=1)
    both = nn(spread, b.sel[...])
    for i in range(2 * STATE):
        b.bc[:, i] = both[:, i * 128 : i * 128 + 128].reshape(SLOT, 8, 128)

    z_relay(zout)
    dstate = plane_last(b.db, dstate)
    zero = jnp.zeros((8, 128), F32)

    steps = 4

    def forward_steps(j, carry):
        base = steps * j
        ats = [pl.ds(base + i, 8, stride=SLOT) for i in range(steps)]
        size = [[b.dt[e, at, :] for e in range(2)] for at in ats]
        push = [[size[i][e] * b.xc[e, ats[i], :] for e in range(2)] for i in range(steps)]
        out = [[zero, zero] for _ in range(steps)]
        for n in range(STATE):
            for e in range(2):
                rate = b.rate[n, e]
                state = b.carried[n, e]
                kept = []
                for i in range(steps):
                    state = jnp.exp2(size[i][e] * rate) * state + push[i][e] * b.bc[base + i, n]
                    out[i][e] = out[i][e] + b.bc[base + i, STATE + n] * state
                    kept.append(state)
                b.carried[n, e] = state
                for p in range(steps // 2):
                    both_states = jnp.concatenate(kept[2 * p : 2 * p + 2], axis=0)
                    b.sall[(steps // 2) * j + p + 1, n, e] = both_states.astype(BF16)
        for i in range(steps):
            for e in range(2):
                b.ys[e, ats[i], :] = out[i][e]
        return carry

    b.carried[...] = jnp.zeros((STATE, 2, 8, 128), F32)
    lax.fori_loop(0, SLOT // steps, forward_steps, 0)

    arrive(dstate)
    z_arrive(zgate)
    scaled(1)
    b.t1[...] = nt(b.nb[...].reshape(count, width), b.ws[1])
    z_arrive(zout)
    b.t2[...] = nt(b.db[...].reshape(count, width), b.wt[2].reshape(cols, width))

    @pl.loop(0, 4)
    def _(q):
        for cc in range(2):
            at = slot_rows(2 * q + cc)
            gpre = b.t1[at, :]
            dgat = b.t2[at, :]
            conv = pair(b.xc, at)
            mixed = pair(b.ys, at) + skip * conv
            sig = sigmoid(gpre)
            act = gpre * sig
            b.go[q, cc] = (mixed * act).astype(BF16)
            dmix = dgat * act
            unpair(b.dm, at, dmix)
            slope = sig * (1.0 + gpre * (1.0 - sig))
            b.dg[q, cc] = (dgat * mixed * slope).astype(BF16)
            b.sg[SKIP_ROW : SKIP_ROW + 1, :] += jnp.sum(dmix * conv, axis=0, keepdims=True)

    def reduce_begin(dots, more):
        g = sets[3]

        def low_of(value, q):
            return (value + g.s1[q].astype(F32) if more else value).astype(BF16)

        g.s1[qd] = low_of(dots(lambda ref: ref[qd, oc]), qd)
        cores = [rcopy(g.s1.at[qd], g.l1.at[qd], core)]
        others = (qx, qy, q0)
        rest = dots(lambda ref: jnp.concatenate([ref[q, oc] for q in others], axis=0))
        for k, q in enumerate(others):
            g.s1[q] = low_of(rest[k * SLOT : (k + 1) * SLOT], q)
            cores.append(rcopy(g.s1.at[q], g.l1.at[q], core))
        mine = dots(lambda ref: ref[:, c].reshape(4 * SLOT, cols)).reshape(4, SLOT, width)
        b.sum[...] = b.sum[...] + mine if more else mine
        return cores

    def reduce_second(cores):
        g = sets[3]

        def chip(q, rows):
            return (b.sum[q, rows, :] + g.l1[q, rows, :].astype(F32)).astype(BF16)

        cores[0].wait_recv()
        g.sx[1] = chip(qd, top)
        x1 = rcopy(g.sx.at[1], g.lx.at[1], xpeer)
        g.sy[1] = chip(qd, low)
        y1 = rcopy(g.sy.at[1], g.ly.at[1], ypeer)
        cores[1].wait_recv()
        g.sx[0] = chip(qx, top)
        x0 = rcopy(g.sx.at[0], g.lx.at[0], xpeer)
        cores[2].wait_recv()
        g.sy[0] = chip(qy, low)
        y0 = rcopy(g.sy.at[0], g.ly.at[0], ypeer)
        return x1, y1, x0, y0

    def reduce_third(cps):
        g = sets[3]
        x1, y1, x0, y0 = cps
        x1.wait_recv()
        g.ty[...] = (b.sum[qy, top, :] + g.l1[qy, top, :].astype(F32) + g.lx[1].astype(F32)).astype(BF16)
        c1 = rcopy(g.ty, g.my, ypeer)
        y1.wait_recv()
        g.tx[...] = (b.sum[qx, low, :] + g.l1[qx, low, :].astype(F32) + g.ly[1].astype(F32)).astype(BF16)
        c2 = rcopy(g.tx, g.mx, xpeer)
        return x0, y0, c1, c2

    def reduce_end(cores, cps, out):
        g = sets[3]
        cores[3].wait_recv()
        arrive(cps)
        for rows, near, far_ref in ((top, g.lx, g.my), (low, g.ly, g.mx)):
            out[rows, :] = (
                b.sum[q0, rows, :]
                + g.l1[q0, rows, :].astype(F32)
                + near[0].astype(F32)
                + far_ref[...].astype(F32)
            ).astype(BF16)

    def weight_grad(w, grad, gained):
        b.gws[w] = (grad * b.gl[...] if gained else grad).astype(BF16).reshape(depth, hl, width)
        return grad

    def rows_grad(lhs, rhs):
        return tn(lhs[...].reshape(count, cols), rhs[...].reshape(count, width))

    def gain_grad(w, grad):
        return jnp.sum(grad * b.wt[w].reshape(cols, width).astype(F32), axis=0, keepdims=True)

    def weight_send(w, at):
        return z_scatter(
            lambda q: b.gws.at[w, q, at], lambda k: b.gwl.at[w, k, at], b.gwx.at[w, at]
        )

    def weight_sum(w, st, at):
        gout[w, y, at, :] = z_sum(st, b.gws[w, f, at, :].astype(F32)).astype(BF16)
        return same(gout.at[w, y, at], ypeer)

    every = pl.ds(0, hl)

    weight_grad(2, rows_grad(b.go, b.db), False)
    zgo = z_direct(weight_send(2, every))
    grad = weight_grad(1, rows_grad(b.dg, b.nb), True)
    zgg = z_direct(weight_send(1, every))
    b.vv[...] = gain_grad(1, grad)
    bone = reduce_begin(lambda pick: nn(pick(b.go), b.wt[2].reshape(cols, width)), False)

    def backward_pair(j, carry):
        k = SLOT // 2 - 1 - j
        ats = [pl.ds(2 * k + i, 8, stride=SLOT) for i in range(2)]
        size = [[b.dt[e, at, :] for e in range(2)] for at in ats]
        conv = [[b.xc[e, at, :] for e in range(2)] for at in ats]
        dmix = [[b.dm[e, at, :] for e in range(2)] for at in ats]
        push = [jnp.concatenate([size[i][e] * conv[i][e] for i in range(2)], axis=0).astype(BF16) for e in range(2)]
        dlow = [jnp.concatenate([dmix[i][e] for i in range(2)], axis=0).astype(BF16) for e in range(2)]
        rate_sum = [[zero, zero], [zero, zero]]
        weighted = [[zero, zero], [zero, zero]]
        new = []
        for n in range(STATE):
            inm = [b.bc[2 * k + i, n] for i in range(2)]
            outm = [b.bc[2 * k + i, STATE + n] for i in range(2)]
            dins, douts = [], []
            for e in range(2):
                rate = b.rate[n, e]
                here = b.sall[k + 1, n, e]
                before = [b.sall[k, n, e].astype(F32)[8:16], here.astype(F32)[0:8]]
                back = carry[2 * n + e]
                lams = [None, None]
                acc = b.ga[n, e]
                for i in (1, 0):
                    lam = outm[i] * dmix[i][e] + back
                    back = jnp.exp2(size[i][e] * rate) * lam
                    grad = back * before[i]
                    rate_sum[i][e] = rate_sum[i][e] + grad * rate
                    weighted[i][e] = weighted[i][e] + lam * inm[i]
                    acc = acc + grad * size[i][e]
                    lams[i] = lam
                b.ga[n, e] = acc
                new.append(back)
                dins.append(jnp.concatenate(lams, axis=0).astype(BF16) * push[e])
                douts.append(dlow[e] * here)
            b.sall[k + 1, n, 0] = dins[0] + dins[1]
            b.sall[k + 1, n, 1] = douts[0] + douts[1]
        for i in range(2):
            for e in range(2):
                b.ys[e, ats[i], :] = rate_sum[i][e] * LN2 + conv[i][e] * weighted[i][e]
                b.xc[e, ats[i], :] = size[i][e] * weighted[i][e]
        return tuple(new)

    carry = tuple(zero for _ in range(2 * STATE))
    carry = lax.fori_loop(0, SLOT // 16, backward_pair, carry)
    btwo = reduce_second(bone)
    carry = lax.fori_loop(SLOT // 16, 3 * SLOT // 16, backward_pair, carry)
    z_absorb(zgo)
    bthree = reduce_third(btwo)
    carry = lax.fori_loop(3 * SLOT // 16, SLOT // 4, backward_pair, carry)

    def cut_of(h):
        return slice(h * half, h * half + half)

    def half_rows(j, h):
        return pl.ds(pl.multiple_of(j * SLOT + h * half, half), half)

    def packed_rows(j, h):
        return pl.ds(pl.multiple_of(h * 8 * half + j * half, half), half)

    def map_sums(h):
        begin = 1 + h * half // 2
        parts = [
            b.sall[begin : begin + half // 2, n, k].reshape(8 * half, 128) for k in range(2) for n in range(STATE)
        ]
        b.tm[h * 8 * half : (h + 1) * 8 * half, :] = nt(jnp.concatenate(parts, axis=1), b.sel[0:128, :])

    def rank_part(h):
        span = slice(h * 8 * half, (h + 1) * 8 * half)
        b.t1[span, :] = nn(b.slow[:, cut_of(h), :].reshape(8 * half, 128), b.wst[...])

        @pl.loop(0, 8)
        def _(j):
            dpre = pair(b.ys, half_rows(j, h)) * sigmoid(b.t1[packed_rows(j, h), :] + sbias)
            b.sg[BIAS_ROW : BIAS_ROW + 1, :] += jnp.sum(dpre, axis=0, keepdims=True)
            b.dsl[j, cut_of(h), :] = dpre.astype(BF16)

        rank = nt(b.dsl[:, cut_of(h), :].reshape(8 * half, cols), b.wst[...])
        for j in range(8):
            maps = b.tm[pl.ds(h * 8 * half + j, half, stride=8), :]
            b.pp[j // 2, j % 2, cut_of(h), :] = rank[j * half : (j + 1) * half] + maps

    def slopes(h):
        @pl.loop(0, 8)
        def _(j):
            at = half_rows(j, h)
            cpre = convolved(j, h * half, half)
            sig = sigmoid(cpre)
            b.t2[at, :] = sig * (1.0 + cpre * (1.0 - sig))
            unpair(b.dm, at, pair(b.xc, at) + pair(b.dm, at) * skip)

    def inner_part(which, h):
        @pl.loop(0, 4)
        def _(q):
            for cc, src in ((c, sets[which].own), (oc, sets[which].oth)):
                b.dpj[2 * q + cc, cut_of(h), :] = src[q].astype(BF16)

        span = slice(h * 8 * half, (h + 1) * 8 * half)
        b.t1[span, :] = nn(b.dpj[:, cut_of(h), :].reshape(8 * half, 128), b.wpt[...])

        @pl.loop(0, 4)
        def _(q):
            for cc in range(2):
                j = 2 * q + cc
                at = half_rows(j, h)
                dpre = (pair(b.dm, at) + b.t1[packed_rows(j, h), :]) * b.t2[at, :]
                b.dcp[j, cut_of(h), :] = dpre
                sums = []
                for k in range(CONV):
                    begin = 5 + k + h * half
                    sums.append(jnp.sum(dpre * b.ip[j, begin : begin + half, :], axis=0, keepdims=True))
                sums.append(jnp.sum(dpre, axis=0, keepdims=True))
                b.sg[TAP_ROW : CONV_ROW + 1, :] += jnp.concatenate(sums, axis=0)
                dinner = taps[CONV - 1] * dpre
                for k in range(CONV - 1):
                    begin = CONV - 1 - k + h * half
                    dinner = dinner + taps[k] * b.dcp[j, begin : begin + half, :]
                b.di[q, cc, cut_of(h), :] = dinner.astype(BF16)

    def inner_grad(h):
        return tn(
            b.di[:, :, cut_of(h), :].reshape(8 * half, cols), b.nb[:, :, cut_of(h), :].reshape(8 * half, width)
        )

    map_sums(1)
    rank_part(1)
    later = all_reduce(2, cut_of(1))
    later[0]()
    marks = [SLOT // 4 + v for v in (0, 8, 24, SLOT // 4)]
    for k in range(3):
        carry = lax.fori_loop(marks[k], marks[k + 1], backward_pair, carry)
        if k < 2:
            later[k + 1]()
    z_absorb(zgg)
    map_sums(0)
    later[3]()
    rank_part(0)
    sooner = all_reduce(4, cut_of(0))
    sooner[0]()
    later[4]()
    slopes(1)
    sooner[1]()
    inner_part(2, 1)
    reduce_end(bone, bthree, bsum)
    for n in range(STATE):
        parts = [jnp.sum(b.ga[n, e] * b.rate[n, e], axis=0, keepdims=True) for e in range(2)]
        b.sg[LOG_ROW + n : LOG_ROW + n + 1, :] = jnp.concatenate(parts, axis=1) * LN2
    slopes(0)
    sooner[2]()
    hold = [weight_sum(2, zgo, every)]
    b.gacc[...] = inner_grad(1)
    settle([*bone, *btwo, *bthree[2:]])
    gate_dot = lambda ref: nn(ref.reshape(4 * SLOT, cols), b.ws[1]).reshape(4, SLOT, width)
    sets[3].s1[...] = gate_dot(b.dg[:, oc]).astype(BF16)
    b.sum[...] = gate_dot(b.dg[:, c])
    sooner[3]()
    hold.append(weight_sum(1, zgg, every))
    sooner[4]()
    inner_part(4, 0)

    grad = weight_grad(0, b.gacc[...] + inner_grad(0), True)
    first, second = pl.ds(0, hl // 2), pl.ds(hl // 2, hl // 2)
    zgi = [weight_send(0, first), weight_send(0, second)]
    for st in zgi:
        z_direct(st)
    total = b.vv[...] + gain_grad(0, grad)
    for i in range(8):
        b.vs[0, i : i + 1, :] = total[:, i * 128 : i * 128 + 128]
    v1 = rcopy(b.vs.at[0], b.vl.at[0], xpeer)
    done = reduce_begin(lambda pick: nn(pick(b.di), b.ws[0]), True)
    v1.wait_recv()
    b.vs[1] = b.vs[0] + b.vl[0]
    v2 = rcopy(b.vs.at[1], b.vl.at[1], ypeer)
    dtwo = reduce_second(done)
    z_absorb(zgi[0])
    z_absorb(zgi[1])
    grad = tn(b.dpj[...].reshape(count, 128), b.cl[...].reshape(count, cols))
    b.sg[0:PROJ, :] = grad[:PROJ]
    grad = tn(b.slow[...].reshape(count, 128), b.dsl[...].reshape(count, cols))
    b.sg[STEP_ROW:LOG_ROW, :] = grad[:RANK]
    for i in range(depth):
        b.sgs[i] = folded(b.sg[:, i * hl : (i + 1) * hl], hl)
    zgs = z_direct(z_scatter(lambda q: b.sgs.at[q], lambda k: b.sgl.at[k], b.sgx))
    v2.wait_recv()
    b.vs[2] = b.vs[1] + b.vl[1]
    v3 = rcopy(b.vs.at[2], b.vl.at[2], core)
    dthree = reduce_third(dtwo)
    v3.wait_recv()
    b.vz[f] = b.vs[2] + b.vl[2]
    v4 = z_gather(lambda q: b.vz.at[q])
    yin = [weight_sum(0, zgi[0], first)]
    z_absorb(zgs)
    yin.append(weight_sum(0, zgi[1], second))
    sout[y] = z_sum(zgs, b.sgs[f].astype(F32)).astype(BF16)
    ysmall = same(sout.at[y], ypeer)
    z_relay(v4)
    reduce_end(done, dthree, dsc)
    z_arrive(v4)
    total = b.vz[0]
    for k in range(1, depth):
        total = total + b.vz[k]
    vout[...] = total
    arrive(hold + yin + [ysmall])
    for cp in started:
        cp.wait_send()


def last_kernel(hl, piece, tok, cot, lens, bsum, dsc, gout, sout, vout, *outs):
    (out, dtok, ggain, ginner, ggate, gconv, gcb, gproj, gstep, gsb, glog, gskip, gwout) = outs
    s = lax.axis_index("shard")
    t32 = tok[...].astype(F32)
    rowid = lax.broadcasted_iota(jnp.int32, (SLOT, 1), 0)
    out[...] = (t32 + jnp.where(rowid < lens[0], bsum[...].astype(F32), 0.0)).astype(BF16)
    inv = lax.rsqrt(jnp.mean(t32 * t32, axis=1, keepdims=True) + EPS)
    ds = dsc[...].astype(F32)
    mean = jnp.mean(ds * t32, axis=1, keepdims=True)
    dtok[...] = cot[...].astype(F32) + inv * ds - t32 * (inv * inv * inv * mean)
    width = tok.shape[1]
    el = 2 * hl
    ginner[...] = gout[0].reshape(el, width).T.astype(F32)
    ggate[...] = gout[1].reshape(el, width).T.astype(F32)
    gwout[...] = gout[2].reshape(el, width).astype(F32)
    small = sout[...].astype(F32)
    halves = [jnp.concatenate([small[k][:, :hl], small[k][:, hl:el]], axis=0) for k in range(2)]
    both = jnp.concatenate(halves, axis=1)
    gproj[...] = both[:PROJ]
    gstep[...] = both[STEP_ROW:LOG_ROW]
    glog[...] = both[LOG_ROW:TAP_ROW]
    gconv[...] = both[TAP_ROW:CONV_ROW]
    gcb[...] = both[CONV_ROW : CONV_ROW + 1].reshape(el)
    gsb[...] = both[BIAS_ROW : BIAS_ROW + 1].reshape(el)
    gskip[...] = both[SKIP_ROW : SKIP_ROW + 1].reshape(el)
    per = 128 // piece
    vec = vout[...]
    rows = lax.broadcasted_iota(jnp.int32, (8, 128), 0)
    row = jnp.sum(jnp.where(rows == s // per, vec, 0.0), axis=0, keepdims=True)
    pick = jnp.zeros((1, piece), F32)
    for i in range(per):
        pick = jnp.where(lax.rem(s, per) == i, row[:, i * piece : (i + 1) * piece], pick)
    ggain[...] = pick.reshape(piece)


def make_local(replicas, shards):
    depth = shards // 4

    def local(
        tokens, norm_gain, w_inner, w_gate, conv_weight, conv_bias, w_proj, w_step, step_bias, a_log, skip_gain,
        w_out, cotangent, lengths,
    ):
        width = tokens.shape[1]
        el = w_inner.shape[1]
        hl = el // 2
        piece = norm_gain.shape[0]
        spec = buffers(depth, hl, width, shards, piece)
        nsem = 96 + 16 * depth
        vm = pl.BlockSpec(memory_space=pltpu.VMEM)
        sm = pl.BlockSpec(memory_space=pltpu.SMEM)
        sds = jax.ShapeDtypeStruct
        mid = pl.pallas_call(
            functools.partial(main_kernel, [tuple(group) for group in spec], depth, hl, piece, nsem),
            out_shape=(
                pltpu.VMEM((SLOT, width), BF16),
                pltpu.VMEM((SLOT, width), BF16),
                pltpu.VMEM((3, 2, hl, width), BF16),
                pltpu.VMEM((2, PACK // 2, 128), BF16),
                pltpu.VMEM((8, 128), F32),
            ),
            in_specs=[vm] * 13 + [sm],
            out_specs=(vm,) * 5,
            scratch_shapes=[pltpu.VMEM(shape, kind) for group in spec for shape, kind in group.values()]
            + [pltpu.SemaphoreType.DMA((nsem,)), pltpu.SemaphoreType.DMA((nsem,))],
            compiler_params=pltpu.CompilerParams(
                collective_id=0, has_side_effects=True, vmem_limit_bytes=61 << 20
            ),
            name="layer",
        )(
            tokens, cotangent, w_inner, w_gate, w_out, w_proj.T, w_step, a_log, conv_weight, conv_bias, step_bias,
            skip_gain, norm_gain, lengths,
        )
        bsum, dsc, gout, sout, vout = mid
        if replicas > 2:
            groups = [[r for r in range(replicas) if r % 2 == k] for k in range(2)]
            gout, sout, vout = (
                lax.psum(v.astype(F32), "replica", axis_index_groups=groups) for v in (gout, sout, vout)
            )
        outs = pl.pallas_call(
            functools.partial(last_kernel, hl, piece),
            out_shape=(
                sds((SLOT, width), BF16),
                sds((SLOT, width), F32),
                sds((piece,), F32),
                sds((width, el), F32),
                sds((width, el), F32),
                sds((CONV, el), F32),
                sds((el,), F32),
                sds((PROJ, el), F32),
                sds((RANK, el), F32),
                sds((el,), F32),
                sds((STATE, el), F32),
                sds((el,), F32),
                sds((el, width), F32),
            ),
            in_specs=[vm, vm, sm] + [vm] * 5,
            out_specs=(vm,) * 13,
            compiler_params=pltpu.CompilerParams(vmem_limit_bytes=16 << 20),
            name="results",
        )(tokens, cotangent, lengths, bsum, dsc, gout, sout, vout)
        return outs[:7] + (outs[7].T,) + outs[8:]

    return local


def solution(mesh):
    return jax.shard_map(
        make_local(mesh.shape["replica"], mesh.shape["shard"]),
        mesh=mesh,
        in_specs=(
            P(("replica", "shard"), None),
            P("shard"),
            P(None, "shard"),
            P(None, "shard"),
            P(None, "shard"),
            P("shard"),
            P("shard", None),
            P(None, "shard"),
            P("shard"),
            P(None, "shard"),
            P("shard"),
            P("shard", None),
            P(("replica", "shard"), None),
            P(("replica", "shard")),
        ),
        out_specs=(
            P(("replica", "shard"), None),
            P(("replica", "shard"), None),
            P("shard"),
            P(None, "shard"),
            P(None, "shard"),
            P(None, "shard"),
            P("shard"),
            P("shard", None),
            P(None, "shard"),
            P("shard"),
            P(None, "shard"),
            P("shard"),
            P("shard", None),
        ),
        check_vma=False,
    )
```

```python
import functools
import math
from types import SimpleNamespace

import jax
import jax.numpy as jnp
from jax import lax
from jax.experimental import pallas as pl
from jax.experimental.pallas import tpu as pltpu
from jax.sharding import PartitionSpec as P

RANK = 64
STATE = 16
CONV = 4
SLOT = 128
EPS = 1e-05
LN2 = math.log(2.0)
PROJ = RANK + 2 * STATE
PACK = 192
STEP_ROW = PROJ
LOG_ROW = STEP_ROW + RANK
TAP_ROW = LOG_ROW + STATE
CONV_ROW = TAP_ROW + CONV
BIAS_ROW = CONV_ROW + 1
SKIP_ROW = BIAS_ROW + 1
GAIN_ROW = SKIP_ROW + 1
MESH = pl.DeviceIdType.MESH
F32 = jnp.float32
BF16 = jnp.bfloat16


def sigmoid(value):
    return 0.5 * jnp.tanh(0.5 * value) + 0.5


def nt(left, right):
    return lax.dot_general(left, right, (((1,), (1,)), ((), ())), preferred_element_type=F32)


def nn(left, right):
    return lax.dot_general(left, right, (((1,), (0,)), ((), ())), preferred_element_type=F32)


def tn(left, right):
    return lax.dot_general(left, right, (((0,), (0,)), ((), ())), preferred_element_type=F32)


def buffers(depth, hl, width, shards, piece):
    cols = depth * hl
    rows = 8 * SLOT
    def reduce_small(part):
        low, full = ((4, part, 128), BF16), ((4, part, 128), F32)
        return dict(s1=low, l1=low, s2=low, l2=low, s3=low, l3=low, own=full, oth=full)

    reduce_large = dict(
        s1=((4, SLOT, width), BF16),
        l1=((4, SLOT, width), BF16),
        sx=((2, SLOT // 2, width), BF16),
        sy=((2, SLOT // 2, width), BF16),
        lx=((2, SLOT // 2, width), BF16),
        ly=((2, SLOT // 2, width), BF16),
        tx=((SLOT // 2, width), BF16),
        ty=((SLOT // 2, width), BF16),
        mx=((SLOT // 2, width), BF16),
        my=((SLOT // 2, width), BF16),
    )
    shapes = dict(
        wt=((3, depth, hl, width), BF16),
        ws=((2, cols, width), BF16),
        pka=((depth, PACK // 2, 128), BF16),
        wpt=((128, cols), BF16),
        gb=((2, 2, 8, cols), F32),
        t1=((rows, cols), F32),
        t2=((rows, cols), F32),
        gl=((1, width), F32),
        nb=((4, 2, SLOT, width), BF16),
        db=((4, 2, SLOT, width), BF16),
        pkl=((PACK, cols), F32),
        wst=((128, cols), BF16),
        rate=((STATE, 2, 8, 128), F32),
        ip=((8, SLOT + 8, cols), F32),
        dcp=((8, SLOT + 8, cols), F32),
        gacc=((cols, width), F32),
        tm=((rows, 128), F32),
        sel=((256, 2 * STATE * 128), BF16),
        bc=((SLOT, 2 * STATE, 8, 128), F32),
        sall=((SLOT // 2 + 1, STATE, 2, 16, 128), BF16),
        cl=((8, SLOT, cols), BF16),
        xc=((2, rows, 128), F32),
        pp=((4, 2, SLOT, 128), F32),
        slow=((8, SLOT, 128), BF16),
        dpj=((8, SLOT, 128), BF16),
        dt=((2, rows, 128), F32),
        ys=((2, rows, 128), F32),
        dm=((2, rows, 128), F32),
        ga=((STATE, 2, 8, 128), F32),
        carried=((STATE, 2, 8, 128), F32),
        go=((4, 2, SLOT, cols), BF16),
        dg=((4, 2, SLOT, cols), BF16),
        di=((4, 2, SLOT, cols), BF16),
        dsl=((8, SLOT, cols), BF16),
        gws=((3, depth, hl, width), BF16),
        gwl=((3, depth - 1, hl, width), BF16),
        gwx=((3, hl, width), BF16),
        sg=((PACK, cols), F32),
        sgs=((depth, PACK // 2, 128), BF16),
        sgl=((depth - 1, PACK // 2, 128), BF16),
        sgx=((PACK // 2, 128), BF16),
        vv=((1, width), F32),
        sum=((4, SLOT, width), F32),
        vs=((4, 8, 128), F32),
        vl=((3, 8, 128), F32),
        vz=((depth, 8, 128), F32),
    )
    part = reduce_small(SLOT // 2)
    return [shapes, part, part, reduce_large, part, part]


def main_kernel(names, depth, hl, piece, nsem, *refs):
    (tok, cot, win, wg, wo, wproj, wstep, alog, convw, convb, stepb, skipg, gain, lens) = refs[:14]
    (bsum, dsc, gout, sout, vout) = refs[14:19]
    send_sems, recv_sems = refs[-2:]
    sets, at = [], 19
    for group in names:
        sets.append(SimpleNamespace(**dict(zip(group, refs[at:]))))
        at += len(group)
    b = sets[0]
    width = tok.shape[1]
    cols = depth * hl
    el = 2 * hl
    count = 8 * SLOT
    half = SLOT // 2

    r = lax.axis_index("replica")
    s = lax.axis_index("shard")
    y = lax.rem(r, 2)
    f = s // 4
    x = lax.rem(s // 2, 2)
    c = lax.rem(s, 2)
    core = (r, s + 1 - 2 * c)
    xpeer = (r, s + 2 - 4 * x)
    ypeer = (r + 1 - 2 * y, s)
    zpos = [lax.rem(f + k, depth) for k in range(1, depth)]
    zpeers = [(r, s + 4 * (q - f)) for q in zpos]
    q0 = y * 2 + x
    qx = y * 2 + 1 - x
    qy = (1 - y) * 2 + x
    qd = (1 - y) * 2 + 1 - x
    oc = 1 - c
    top, low = slice(0, half), slice(half, SLOT)

    counter = [0]
    started = []
    line = depth == 4
    ends = (f == 0) | (f == 3)
    inner = (f == 1) | (f == 2)

    def ticket():
        counter[0] += 1
        assert counter[0] <= nsem
        return counter[0] - 1

    def remote(src, dst, dev, send, recv):
        return pltpu.make_async_remote_copy(
            src_ref=src,
            dst_ref=dst,
            send_sem=send_sems.at[send],
            recv_sem=recv_sems.at[recv],
            device_id=dev,
            device_id_type=MESH,
        )

    def rcopy(src, dst, dev):
        i = ticket()
        cp = remote(src, dst, dev, i, i)
        cp.start()
        started.append(cp)
        return cp

    def same(ref, dev):
        return rcopy(ref, ref, dev)

    def settle(cps):
        for cp in cps:
            cp.wait_send()
            started[:] = [other for other in started if other is not cp]

    def arrive(cps):
        for cp in cps:
            cp.wait_recv()

    def only(when, cp):
        @pl.when(when)
        def _():
            cp.start()

        def wait_send():
            @pl.when(when)
            def _():
                cp.wait_send()

        started.append(SimpleNamespace(wait_send=wait_send))

    def far(k):
        return ((f == 0) & (k == 3)) | ((f == 3) & (k == 1))

    def far_from(k):
        return ((f == 0) & (k == 1)) | ((f == 3) & (k == 3))

    def z_gather(piece):
        ids = [ticket() for _ in range(depth)]
        cps = {}
        for k in sorted(range(1, depth), key=lambda k: k != 2):
            cps[k] = remote(piece(f), piece(f), zpeers[k - 1], ids[k], ids[k])
            if line and k != 2:
                only(jnp.logical_not(far(k)), cps[k])
            else:
                cps[k].start()
                started.append(cps[k])
        return SimpleNamespace(piece=piece, ids=ids, cps=cps)

    def z_relay(st):
        if line:
            st.cps[2].wait_recv()
            q = 3 * (2 - jnp.where(inner, f, 1))
            near = jnp.where(inner, 2 * f - 1, 1)
            only(inner, remote(st.piece(q), st.piece(q), (r, s + 4 * (3 - q - f)), st.ids[0], st.ids[1] + near - 1))

    def z_arrive(st):
        for k in range(1, depth):
            if not (line and k == 2):
                st.cps[k].wait_recv()

    def z_scatter(send, land, extra):
        ids = [ticket() for _ in range(depth)]
        cps = {k: remote(send(zpos[k - 1]), land(k - 1), zpeers[k - 1], ids[k], ids[k]) for k in range(1, depth)}
        st = SimpleNamespace(send=send, land=land, extra=extra, cps=cps)
        if not line:
            for cp in cps.values():
                cp.start()
                started.append(cp)
            return st
        st.cross = remote(send(3 - f), extra, (r, s + 4 - 8 * (f // 3)), ids[0], ids[0])
        only(ends, st.cross)
        return st

    def z_direct(st):
        if line:
            only(ends, st.cps[2])
            for k in (1, 3):
                only(jnp.logical_not(far(k)), st.cps[k])
        return st

    def z_absorb(st):
        if line:

            @pl.when(inner)
            def _():
                st.cross.wait_recv()
                target = st.send(zpos[1])
                target[...] = (target[...].astype(F32) + st.extra[...].astype(F32)).astype(BF16)

            only(inner, st.cps[2])

    def z_sum(st, own):
        total = own
        for k in range(1, depth):
            if line and k != 2:

                @pl.when(jnp.logical_not(far_from(k)))
                def _():
                    st.cps[k].wait_recv()

            else:
                st.cps[k].wait_recv()
        for k in range(1, depth):
            value = st.land(k - 1)[...].astype(F32)
            total = total + (jnp.where(far_from(k), 0.0, value) if line and k != 2 else value)
        return total

    barrier = pltpu.get_barrier_semaphore()
    reach = [core, xpeer, ypeer]
    for dev in reach:
        pl.semaphore_signal(barrier, inc=1, device_id=dev, device_id_type=MESH)
    for k in range(1, depth):

        def hello():
            pl.semaphore_signal(barrier, inc=1, device_id=zpeers[k - 1], device_id_type=MESH)

        if line and k != 2:
            pl.when(jnp.logical_not(far(k)))(hello)
        else:
            hello()

    def lanes(value, n):
        value = value.astype(F32)
        if value.shape[1] == n:
            return value
        return jnp.concatenate([value, jnp.zeros((value.shape[0], n - value.shape[1]), F32)], axis=1)

    def folded(value, n):
        both = jnp.concatenate([value[: PACK // 2], value[PACK // 2 :]], axis=1)
        return lanes(both, 128).astype(BF16)

    def unfolded(value, n):
        return jnp.concatenate([value[:, :n], value[:, n : 2 * n]], axis=0)

    rows = [wproj[...], wstep[...], alog[...], convw[...]]
    rows += [v[...].reshape(1, el) for v in (convb, stepb, skipg)]
    rows = [v.astype(F32) for v in rows]
    rows.append(jnp.zeros((PACK - GAIN_ROW, el), F32))
    pack = jnp.concatenate(rows, axis=0)
    mine = jnp.where(y == 0, pack[:, :hl], pack[:, hl:])
    own_gain = gain[...].reshape(1, piece).astype(F32)
    rowid = lax.broadcasted_iota(jnp.int32, (PACK, 1), 0)
    b.pka[f] = folded(jnp.where(rowid == GAIN_ROW, own_gain, mine), hl)
    wint = win[...].T
    b.wt[0, f] = jnp.where(y == 0, wint[:hl], wint[hl:])
    t32 = tok[...].astype(F32)
    inv = lax.rsqrt(jnp.mean(t32 * t32, axis=1, keepdims=True) + EPS)
    b.nb[q0, c] = (t32 * inv).astype(BF16)

    if line:
        for w in range(3):
            for k in (1, 3):

                @pl.when(far_from(k))
                def _():
                    b.gwl[w, k - 1] = jnp.zeros((hl, width), BF16)

        for k in (1, 3):

            @pl.when(far_from(k))
            def _():
                b.sgl[k - 1] = jnp.zeros((PACK // 2, 128), BF16)

        pl.semaphore_wait(barrier, jnp.where(ends, 5, 6))
    else:
        pl.semaphore_wait(barrier, 2 + depth)

    def plane_start(buf):
        upper, lower = buf.at[q0, c, pl.ds(0, half)], buf.at[q0, c, pl.ds(half, half)]
        ax = same(upper, xpeer)
        by = same(lower, ypeer)
        bx = same(lower, xpeer)
        ay = same(upper, ypeer)
        oo = same(buf.at[q0, c], core)
        return ax, by, bx, ay, oo

    def plane_forward(buf, cps):
        ax, by, bx, ay, oo = cps
        ax.wait_recv()
        fa = same(buf.at[qx, c, pl.ds(0, half)], ypeer)
        by.wait_recv()
        fb = same(buf.at[qy, c, pl.ds(half, half)], xpeer)
        return bx, ay, oo, fa, fb

    def plane_core(buf, cps):
        bx, ay, oo, fa, fb = cps
        bx.wait_recv()
        ox = same(buf.at[qx, c], core)
        ay.wait_recv()
        oy = same(buf.at[qy, c], core)
        return oo, ox, oy, fa, fb

    def plane_last(buf, cps):
        oo, ox, oy, fa, fb = cps
        arrive([fa, fb])
        return oo, ox, oy, same(buf.at[qd, c], core)

    zsmall = z_gather(lambda q: b.pka.at[q])
    zin = z_gather(lambda q: b.wt.at[0, q])
    nstate = plane_start(b.nb)

    wgt = wg[...].T
    b.wt[1, f] = jnp.where(y == 0, wgt[:hl], wgt[hl:])
    b.wt[2, f] = wo[pl.ds(y * hl, hl), :]
    rowid = lax.broadcasted_iota(jnp.int32, (SLOT, 1), 0)
    b.db[q0, c] = jnp.where(rowid < lens[0], cot[...].astype(F32), 0.0).astype(BF16)
    z_relay(zsmall)
    nstate = plane_forward(b.nb, nstate)
    z_relay(zin)
    z_arrive(zsmall)
    locs = [unfolded(b.pka[i].astype(F32), hl) for i in range(depth)]
    pkl = jnp.concatenate(locs, axis=1)
    b.pkl[...] = pkl
    b.gb[c, x] = jnp.broadcast_to(pkl[GAIN_ROW : GAIN_ROW + 1], (8, cols))
    gx = same(b.gb.at[c, x], xpeer)
    dstate = plane_start(b.db)
    b.wst[...] = jnp.concatenate(
        [pkl[STEP_ROW:LOG_ROW], jnp.zeros((128 - RANK, cols), F32)], axis=0
    ).astype(BF16)
    b.wpt[...] = jnp.concatenate([pkl[:PROJ], jnp.zeros((128 - PROJ, cols), F32)], axis=0).astype(BF16)
    for n in range(STATE):
        row = -jnp.exp(pkl[LOG_ROW + n : LOG_ROW + n + 1]) * (1.0 / LN2)
        for et in range(2):
            b.rate[n, et] = jnp.broadcast_to(row[:, et * 128 : et * 128 + 128], (8, 128))
    nstate = plane_core(b.nb, nstate)
    b.ip[:, 0:8, :] = jnp.zeros((8, 8, cols), F32)
    b.dcp[:, SLOT : SLOT + 8, :] = jnp.zeros((8, 8, cols), F32)
    b.ga[...] = jnp.zeros((STATE, 2, 8, 128), F32)
    b.sall[0] = jnp.zeros((STATE, 2, 16, 128), BF16)
    b.sg[...] = jnp.zeros((PACK, cols), F32)
    source = lax.broadcasted_iota(jnp.int32, (256, 2 * STATE * 128), 0)
    target = lax.broadcasted_iota(jnp.int32, (256, 2 * STATE * 128), 1)
    b.sel[...] = jnp.where(lax.rem(source, 128) == RANK + target // 128, 1.0, 0.0).astype(BF16)
    gx.wait_recv()
    gc = same(b.gb.at[c], core)
    gc.wait_recv()
    pieces = []
    for i in range(depth):
        for j in range(2):
            for k in range(2):
                pieces.append(b.gb[k, j, 0:1, i * piece : (i + 1) * piece])
    b.gl[...] = jnp.concatenate(pieces, axis=1)

    z_arrive(zin)
    zgate = z_gather(lambda q: b.wt.at[1, q])
    zout = z_gather(lambda q: b.wt.at[2, q])

    def scaled(w):
        full = b.wt[w].reshape(cols, width).astype(F32)
        b.ws[w] = (full * b.gl[...]).astype(BF16)

    scaled(0)
    arrive(plane_last(b.nb, nstate))

    def row_of(i):
        return b.pkl[i : i + 1, :]

    taps = [row_of(TAP_ROW + k) for k in range(CONV)]
    cbias = row_of(CONV_ROW)
    sbias = row_of(BIAS_ROW)
    skip = row_of(SKIP_ROW)

    def slot_rows(j):
        return pl.ds(pl.multiple_of(j * SLOT, SLOT), SLOT)

    def pair(ref, at):
        return jnp.concatenate([ref[0, at, :], ref[1, at, :]], axis=1)

    def unpair(ref, at, value):
        ref[0, at, :] = value[:, :128]
        ref[1, at, :] = value[:, 128:]

    def convolved(j, begin, size):
        acc = jnp.broadcast_to(cbias, (size, cols))
        for k in range(CONV):
            acc = acc + taps[k] * b.ip[j, 5 + k + begin : 5 + k + begin + size, :]
        return acc

    b.ip[:, 8 : 8 + SLOT, :] = nt(b.nb[...].reshape(count, width), b.ws[0]).reshape(8, SLOT, cols)

    @pl.loop(0, 8)
    def _(j):
        acc = convolved(j, 0, SLOT)
        out = acc * sigmoid(acc)
        unpair(b.xc, slot_rows(j), out)
        b.cl[j] = out.astype(BF16)

    b.pp[...] = nt(b.cl[...].reshape(count, cols), b.wpt[...]).reshape(4, 2, SLOT, 128)

    def all_reduce(which, rows):
        g = sets[which]
        flight = []

        def first():
            g.s1[...] = b.pp[:, oc, rows, :].astype(BF16)
            flight[:] = [rcopy(g.s1, g.l1, core)]

        def second():
            arrive(flight)
            total = b.pp[:, c, rows, :] + g.l1[...].astype(F32)
            g.s2[...] = total.astype(BF16)
            flight[:] = [
                rcopy(g.s2.at[pl.ds(0, 2)], g.l2.at[pl.ds(0, 2)], xpeer),
                rcopy(g.s2.at[pl.ds(2, 2)], g.l2.at[pl.ds(2, 2)], ypeer),
            ]
            g.own[...] = total

        def third():
            arrive(flight)
            total = g.own[...] + g.l2[...].astype(F32)
            g.s3[...] = total.astype(BF16)
            flight[:] = [
                rcopy(g.s3.at[pl.ds(0, 2)], g.l3.at[pl.ds(0, 2)], ypeer),
                rcopy(g.s3.at[pl.ds(2, 2)], g.l3.at[pl.ds(2, 2)], xpeer),
            ]
            g.own[...] = total

        def fourth():
            arrive(flight)
            g.own[...] = g.own[...] + g.l3[...].astype(F32)
            flight[:] = [rcopy(g.own, g.oth, core)]

        return [first, second, third, fourth, lambda: arrive(flight)]

    def cut_of(h):
        return slice(h * half, h * half + half)

    def half_rows(j, h):
        return pl.ds(pl.multiple_of(j * SLOT + h * half, half), half)

    def packed_rows(j, h):
        return pl.ds(pl.multiple_of(h * 8 * half + j * half, half), half)

    front = all_reduce(1, cut_of(0))
    back = all_reduce(5, cut_of(1))
    for k in range(3):
        front[k]()
        back[k]()
    dstate = plane_forward(b.db, dstate)
    z_relay(zgate)
    front[3]()
    back[3]()
    dstate = plane_core(b.db, dstate)
    front[4]()

    def scan_inputs(which, h):
        @pl.loop(0, 4)
        def _(q):
            for cc, src in ((c, sets[which].own), (oc, sets[which].oth)):
                j = 2 * q + cc
                proj = src[q]
                b.tm[pl.ds(h * 8 * half + j, half, stride=8), :] = proj
                b.slow[j, cut_of(h), :] = proj.astype(BF16)

        span = slice(h * 8 * half, (h + 1) * 8 * half)
        b.t1[span, :] = nn(b.slow[:, cut_of(h), :].reshape(8 * half, 128), b.wst[...])

        @pl.loop(0, 8)
        def _(j):
            pre = b.t1[packed_rows(j, h), :] + sbias
            unpair(b.dt, half_rows(j, h), jnp.maximum(pre, 0.0) + jnp.log1p(jnp.exp(-jnp.abs(pre))))

        tm = b.tm[span, :]
        high = tm.astype(BF16)
        spread = jnp.concatenate([high, (tm - high.astype(F32)).astype(BF16)], axis=1)
        both = nn(spread, b.sel[...])
        for i in range(2 * STATE):
            b.bc[cut_of(h), i] = both[:, i * 128 : i * 128 + 128].reshape(half, 8, 128)

    zero = jnp.zeros((8, 128), F32)

    steps = 4

    def forward_steps(j, carry):
        base = steps * j
        ats = [pl.ds(base + i, 8, stride=SLOT) for i in range(steps)]
        size = [[b.dt[e, at, :] for e in range(2)] for at in ats]
        push = [[size[i][e] * b.xc[e, ats[i], :] for e in range(2)] for i in range(steps)]
        out = [[zero, zero] for _ in range(steps)]
        for n in range(STATE):
            for e in range(2):
                rate = b.rate[n, e]
                state = b.carried[n, e]
                kept = []
                for i in range(steps):
                    state = jnp.exp2(size[i][e] * rate) * state + push[i][e] * b.bc[base + i, n]
                    out[i][e] = out[i][e] + b.bc[base + i, STATE + n] * state
                    kept.append(state)
                b.carried[n, e] = state
                for p in range(steps // 2):
                    both_states = jnp.concatenate(kept[2 * p : 2 * p + 2], axis=0)
                    b.sall[(steps // 2) * j + p + 1, n, e] = both_states.astype(BF16)
        for i in range(steps):
            for e in range(2):
                b.ys[e, ats[i], :] = out[i][e]
        return carry

    b.carried[...] = jnp.zeros((STATE, 2, 8, 128), F32)
    scan_inputs(1, 0)
    lax.fori_loop(0, half // steps, forward_steps, 0)
    z_relay(zout)
    back[4]()
    scan_inputs(5, 1)
    dstate = plane_last(b.db, dstate)
    lax.fori_loop(half // steps, SLOT // steps, forward_steps, 0)

    arrive(dstate)
    z_arrive(zgate)
    scaled(1)
    b.t1[...] = nt(b.nb[...].reshape(count, width), b.ws[1])
    z_arrive(zout)
    b.t2[...] = nt(b.db[...].reshape(count, width), b.wt[2].reshape(cols, width))

    @pl.loop(0, 4)
    def _(q):
        for cc in range(2):
            at = slot_rows(2 * q + cc)
            gpre = b.t1[at, :]
            dgat = b.t2[at, :]
            conv = pair(b.xc, at)
            mixed = pair(b.ys, at) + skip * conv
            sig = sigmoid(gpre)
            act = gpre * sig
            b.go[q, cc] = (mixed * act).astype(BF16)
            dmix = dgat * act
            unpair(b.dm, at, dmix)
            slope = sig * (1.0 + gpre * (1.0 - sig))
            b.dg[q, cc] = (dgat * mixed * slope).astype(BF16)
            b.sg[SKIP_ROW : SKIP_ROW + 1, :] += jnp.sum(dmix * conv, axis=0, keepdims=True)

    def reduce_begin(dots, more):
        g = sets[3]

        def low_of(value, q):
            return (value + g.s1[q].astype(F32) if more else value).astype(BF16)

        g.s1[qd] = low_of(dots(lambda ref: ref[qd, oc]), qd)
        cores = [rcopy(g.s1.at[qd], g.l1.at[qd], core)]
        others = (qx, qy, q0)
        rest = dots(lambda ref: jnp.concatenate([ref[q, oc] for q in others], axis=0))
        for k, q in enumerate(others):
            g.s1[q] = low_of(rest[k * SLOT : (k + 1) * SLOT], q)
            cores.append(rcopy(g.s1.at[q], g.l1.at[q], core))
        mine = dots(lambda ref: ref[:, c].reshape(4 * SLOT, cols)).reshape(4, SLOT, width)
        b.sum[...] = b.sum[...] + mine if more else mine
        return cores

    def reduce_second(cores):
        g = sets[3]

        def chip(q, rows):
            return (b.sum[q, rows, :] + g.l1[q, rows, :].astype(F32)).astype(BF16)

        cores[0].wait_recv()
        g.sx[1] = chip(qd, top)
        x1 = rcopy(g.sx.at[1], g.lx.at[1], xpeer)
        g.sy[1] = chip(qd, low)
        y1 = rcopy(g.sy.at[1], g.ly.at[1], ypeer)
        cores[1].wait_recv()
        g.sx[0] = chip(qx, top)
        x0 = rcopy(g.sx.at[0], g.lx.at[0], xpeer)
        cores[2].wait_recv()
        g.sy[0] = chip(qy, low)
        y0 = rcopy(g.sy.at[0], g.ly.at[0], ypeer)
        return x1, y1, x0, y0

    def reduce_third(cps):
        g = sets[3]
        x1, y1, x0, y0 = cps
        x1.wait_recv()
        g.ty[...] = (b.sum[qy, top, :] + g.l1[qy, top, :].astype(F32) + g.lx[1].astype(F32)).astype(BF16)
        c1 = rcopy(g.ty, g.my, ypeer)
        y1.wait_recv()
        g.tx[...] = (b.sum[qx, low, :] + g.l1[qx, low, :].astype(F32) + g.ly[1].astype(F32)).astype(BF16)
        c2 = rcopy(g.tx, g.mx, xpeer)
        return x0, y0, c1, c2

    def reduce_end(cores, cps, out):
        g = sets[3]
        cores[3].wait_recv()
        arrive(cps)
        for rows, near, far_ref in ((top, g.lx, g.my), (low, g.ly, g.mx)):
            out[rows, :] = (
                b.sum[q0, rows, :]
                + g.l1[q0, rows, :].astype(F32)
                + near[0].astype(F32)
                + far_ref[...].astype(F32)
            ).astype(BF16)

    def weight_grad(w, grad, gained):
        b.gws[w] = (grad * b.gl[...] if gained else grad).astype(BF16).reshape(depth, hl, width)
        return grad

    def rows_grad(lhs, rhs):
        return tn(lhs[...].reshape(count, cols), rhs[...].reshape(count, width))

    def gain_grad(w, grad):
        return jnp.sum(grad * b.wt[w].reshape(cols, width).astype(F32), axis=0, keepdims=True)

    def weight_send(w, at):
        return z_scatter(
            lambda q: b.gws.at[w, q, at], lambda k: b.gwl.at[w, k, at], b.gwx.at[w, at]
        )

    def weight_sum(w, st, at):
        gout[w, y, at, :] = z_sum(st, b.gws[w, f, at, :].astype(F32)).astype(BF16)
        return same(gout.at[w, y, at], ypeer)

    every = pl.ds(0, hl)

    weight_grad(2, rows_grad(b.go, b.db), False)
    zgo = z_direct(weight_send(2, every))
    grad = weight_grad(1, rows_grad(b.dg, b.nb), True)
    zgg = z_direct(weight_send(1, every))
    b.vv[...] = gain_grad(1, grad)
    bone = reduce_begin(lambda pick: nn(pick(b.go), b.wt[2].reshape(cols, width)), False)

    def backward_pair(j, carry):
        k = SLOT // 2 - 1 - j
        ats = [pl.ds(2 * k + i, 8, stride=SLOT) for i in range(2)]
        size = [[b.dt[e, at, :] for e in range(2)] for at in ats]
        conv = [[b.xc[e, at, :] for e in range(2)] for at in ats]
        dmix = [[b.dm[e, at, :] for e in range(2)] for at in ats]
        push = [jnp.concatenate([size[i][e] * conv[i][e] for i in range(2)], axis=0).astype(BF16) for e in range(2)]
        dlow = [jnp.concatenate([dmix[i][e] for i in range(2)], axis=0).astype(BF16) for e in range(2)]
        rate_sum = [[zero, zero], [zero, zero]]
        weighted = [[zero, zero], [zero, zero]]
        new = []
        for n in range(STATE):
            inm = [b.bc[2 * k + i, n] for i in range(2)]
            outm = [b.bc[2 * k + i, STATE + n] for i in range(2)]
            dins, douts = [], []
            for e in range(2):
                rate = b.rate[n, e]
                here = b.sall[k + 1, n, e]
                before = [b.sall[k, n, e].astype(F32)[8:16], here.astype(F32)[0:8]]
                back = carry[2 * n + e]
                lams = [None, None]
                acc = b.ga[n, e]
                for i in (1, 0):
                    lam = outm[i] * dmix[i][e] + back
                    back = jnp.exp2(size[i][e] * rate) * lam
                    grad = back * before[i]
                    rate_sum[i][e] = rate_sum[i][e] + grad * rate
                    weighted[i][e] = weighted[i][e] + lam * inm[i]
                    acc = acc + grad * size[i][e]
                    lams[i] = lam
                b.ga[n, e] = acc
                new.append(back)
                dins.append(jnp.concatenate(lams, axis=0).astype(BF16) * push[e])
                douts.append(dlow[e] * here)
            b.sall[k + 1, n, 0] = dins[0] + dins[1]
            b.sall[k + 1, n, 1] = douts[0] + douts[1]
        for i in range(2):
            for e in range(2):
                b.ys[e, ats[i], :] = rate_sum[i][e] * LN2 + conv[i][e] * weighted[i][e]
                b.xc[e, ats[i], :] = size[i][e] * weighted[i][e]
        return tuple(new)

    carry = tuple(zero for _ in range(2 * STATE))
    carry = lax.fori_loop(0, SLOT // 16, backward_pair, carry, unroll=2)
    btwo = reduce_second(bone)
    carry = lax.fori_loop(SLOT // 16, 3 * SLOT // 16, backward_pair, carry, unroll=2)
    z_absorb(zgo)
    bthree = reduce_third(btwo)
    carry = lax.fori_loop(3 * SLOT // 16, SLOT // 4, backward_pair, carry, unroll=2)

    def map_sums(h):
        begin = 1 + h * half // 2
        parts = [
            b.sall[begin : begin + half // 2, n, k].reshape(8 * half, 128) for k in range(2) for n in range(STATE)
        ]
        b.tm[h * 8 * half : (h + 1) * 8 * half, :] = nt(jnp.concatenate(parts, axis=1), b.sel[0:128, :])

    def rank_part(h):
        span = slice(h * 8 * half, (h + 1) * 8 * half)
        b.t1[span, :] = nn(b.slow[:, cut_of(h), :].reshape(8 * half, 128), b.wst[...])

        @pl.loop(0, 8)
        def _(j):
            dpre = pair(b.ys, half_rows(j, h)) * sigmoid(b.t1[packed_rows(j, h), :] + sbias)
            b.sg[BIAS_ROW : BIAS_ROW + 1, :] += jnp.sum(dpre, axis=0, keepdims=True)
            b.dsl[j, cut_of(h), :] = dpre.astype(BF16)

        rank = nt(b.dsl[:, cut_of(h), :].reshape(8 * half, cols), b.wst[...])
        for j in range(8):
            maps = b.tm[pl.ds(h * 8 * half + j, half, stride=8), :]
            b.pp[j // 2, j % 2, cut_of(h), :] = rank[j * half : (j + 1) * half] + maps

    def slopes(h):
        @pl.loop(0, 8)
        def _(j):
            at = half_rows(j, h)
            cpre = convolved(j, h * half, half)
            sig = sigmoid(cpre)
            b.t2[at, :] = sig * (1.0 + cpre * (1.0 - sig))
            unpair(b.dm, at, pair(b.xc, at) + pair(b.dm, at) * skip)

    def inner_part(which, h):
        @pl.loop(0, 4)
        def _(q):
            for cc, src in ((c, sets[which].own), (oc, sets[which].oth)):
                b.dpj[2 * q + cc, cut_of(h), :] = src[q].astype(BF16)

        span = slice(h * 8 * half, (h + 1) * 8 * half)
        b.t1[span, :] = nn(b.dpj[:, cut_of(h), :].reshape(8 * half, 128), b.wpt[...])

        @pl.loop(0, 4)
        def _(q):
            for cc in range(2):
                j = 2 * q + cc
                at = half_rows(j, h)
                dpre = (pair(b.dm, at) + b.t1[packed_rows(j, h), :]) * b.t2[at, :]
                b.dcp[j, cut_of(h), :] = dpre
                sums = []
                for k in range(CONV):
                    begin = 5 + k + h * half
                    sums.append(jnp.sum(dpre * b.ip[j, begin : begin + half, :], axis=0, keepdims=True))
                sums.append(jnp.sum(dpre, axis=0, keepdims=True))
                b.sg[TAP_ROW : CONV_ROW + 1, :] += jnp.concatenate(sums, axis=0)
                dinner = taps[CONV - 1] * dpre
                for k in range(CONV - 1):
                    begin = CONV - 1 - k + h * half
                    dinner = dinner + taps[k] * b.dcp[j, begin : begin + half, :]
                b.di[q, cc, cut_of(h), :] = dinner.astype(BF16)

    def inner_grad(h):
        return tn(
            b.di[:, :, cut_of(h), :].reshape(8 * half, cols), b.nb[:, :, cut_of(h), :].reshape(8 * half, width)
        )

    map_sums(1)
    rank_part(1)
    later = all_reduce(2, cut_of(1))
    later[0]()
    marks = [SLOT // 4 + v for v in (0, 8, 26, SLOT // 4)]
    for k in range(3):
        carry = lax.fori_loop(marks[k], marks[k + 1], backward_pair, carry, unroll=2)
        if k < 2:
            later[k + 1]()
    z_absorb(zgg)
    map_sums(0)
    rank_part(0)
    later[3]()
    sooner = all_reduce(4, cut_of(0))
    sooner[0]()
    later[4]()
    slopes(1)
    sooner[1]()
    inner_part(2, 1)
    reduce_end(bone, bthree, bsum)
    for n in range(STATE):
        parts = [jnp.sum(b.ga[n, e] * b.rate[n, e], axis=0, keepdims=True) for e in range(2)]
        b.sg[LOG_ROW + n : LOG_ROW + n + 1, :] = jnp.concatenate(parts, axis=1) * LN2
    slopes(0)
    sooner[2]()
    hold = [weight_sum(2, zgo, every)]
    b.gacc[...] = inner_grad(1)
    settle([*bone, *btwo, *bthree[2:]])
    gate_dot = lambda ref: nn(ref.reshape(4 * SLOT, cols), b.ws[1]).reshape(4, SLOT, width)
    sets[3].s1[...] = gate_dot(b.dg[:, oc]).astype(BF16)
    b.sum[...] = gate_dot(b.dg[:, c])
    sooner[3]()
    hold.append(weight_sum(1, zgg, every))
    sooner[4]()
    inner_part(4, 0)

    grad = weight_grad(0, b.gacc[...] + inner_grad(0), True)
    first, second = pl.ds(0, hl // 2), pl.ds(hl // 2, hl // 2)
    zgi = [weight_send(0, first), weight_send(0, second)]
    for st in zgi:
        z_direct(st)
    total = b.vv[...] + gain_grad(0, grad)
    for i in range(8):
        b.vs[0, i : i + 1, :] = total[:, i * 128 : i * 128 + 128]
    v1 = rcopy(b.vs.at[0], b.vl.at[0], xpeer)
    done = reduce_begin(lambda pick: nn(pick(b.di), b.ws[0]), True)
    v1.wait_recv()
    b.vs[1] = b.vs[0] + b.vl[0]
    v2 = rcopy(b.vs.at[1], b.vl.at[1], ypeer)
    dtwo = reduce_second(done)
    z_absorb(zgi[0])
    z_absorb(zgi[1])
    grad = tn(b.dpj[...].reshape(count, 128), b.cl[...].reshape(count, cols))
    b.sg[0:PROJ, :] = grad[:PROJ]
    grad = tn(b.slow[...].reshape(count, 128), b.dsl[...].reshape(count, cols))
    b.sg[STEP_ROW:LOG_ROW, :] = grad[:RANK]
    for i in range(depth):
        b.sgs[i] = folded(b.sg[:, i * hl : (i + 1) * hl], hl)
    zgs = z_direct(z_scatter(lambda q: b.sgs.at[q], lambda k: b.sgl.at[k], b.sgx))
    v2.wait_recv()
    b.vs[2] = b.vs[1] + b.vl[1]
    v3 = rcopy(b.vs.at[2], b.vl.at[2], core)
    dthree = reduce_third(dtwo)
    v3.wait_recv()
    b.vz[f] = b.vs[2] + b.vl[2]
    v4 = z_gather(lambda q: b.vz.at[q])
    yin = [weight_sum(0, zgi[0], first)]
    z_absorb(zgs)
    yin.append(weight_sum(0, zgi[1], second))
    sout[y] = z_sum(zgs, b.sgs[f].astype(F32)).astype(BF16)
    ysmall = same(sout.at[y], ypeer)
    z_relay(v4)
    reduce_end(done, dthree, dsc)
    z_arrive(v4)
    total = b.vz[0]
    for k in range(1, depth):
        total = total + b.vz[k]
    vout[...] = total
    arrive(hold + yin + [ysmall])
    for cp in started:
        cp.wait_send()


def last_kernel(hl, piece, tok, cot, lens, bsum, dsc, gout, sout, vout, *outs):
    (out, dtok, ggain, ginner, ggate, gconv, gcb, gproj, gstep, gsb, glog, gskip, gwout) = outs
    s = lax.axis_index("shard")
    t32 = tok[...].astype(F32)
    rowid = lax.broadcasted_iota(jnp.int32, (SLOT, 1), 0)
    out[...] = (t32 + jnp.where(rowid < lens[0], bsum[...].astype(F32), 0.0)).astype(BF16)
    inv = lax.rsqrt(jnp.mean(t32 * t32, axis=1, keepdims=True) + EPS)
    ds = dsc[...].astype(F32)
    mean = jnp.mean(ds * t32, axis=1, keepdims=True)
    dtok[...] = cot[...].astype(F32) + inv * ds - t32 * (inv * inv * inv * mean)
    width = tok.shape[1]
    el = 2 * hl
    ginner[...] = gout[0].reshape(el, width).T.astype(F32)
    ggate[...] = gout[1].reshape(el, width).T.astype(F32)
    gwout[...] = gout[2].reshape(el, width).astype(F32)
    small = sout[...].astype(F32)
    halves = [jnp.concatenate([small[k][:, :hl], small[k][:, hl:el]], axis=0) for k in range(2)]
    both = jnp.concatenate(halves, axis=1)
    gproj[...] = both[:PROJ]
    gstep[...] = both[STEP_ROW:LOG_ROW]
    glog[...] = both[LOG_ROW:TAP_ROW]
    gconv[...] = both[TAP_ROW:CONV_ROW]
    gcb[...] = both[CONV_ROW : CONV_ROW + 1].reshape(el)
    gsb[...] = both[BIAS_ROW : BIAS_ROW + 1].reshape(el)
    gskip[...] = both[SKIP_ROW : SKIP_ROW + 1].reshape(el)
    per = 128 // piece
    vec = vout[...]
    rows = lax.broadcasted_iota(jnp.int32, (8, 128), 0)
    row = jnp.sum(jnp.where(rows == s // per, vec, 0.0), axis=0, keepdims=True)
    pick = jnp.zeros((1, piece), F32)
    for i in range(per):
        pick = jnp.where(lax.rem(s, per) == i, row[:, i * piece : (i + 1) * piece], pick)
    ggain[...] = pick.reshape(piece)


def make_local(replicas, shards):
    depth = shards // 4

    def local(
        tokens, norm_gain, w_inner, w_gate, conv_weight, conv_bias, w_proj, w_step, step_bias, a_log, skip_gain,
        w_out, cotangent, lengths,
    ):
        width = tokens.shape[1]
        el = w_inner.shape[1]
        hl = el // 2
        piece = norm_gain.shape[0]
        spec = buffers(depth, hl, width, shards, piece)
        nsem = 96 + 16 * depth
        vm = pl.BlockSpec(memory_space=pltpu.VMEM)
        sm = pl.BlockSpec(memory_space=pltpu.SMEM)
        sds = jax.ShapeDtypeStruct
        mid = pl.pallas_call(
            functools.partial(main_kernel, [tuple(group) for group in spec], depth, hl, piece, nsem),
            out_shape=(
                pltpu.VMEM((SLOT, width), BF16),
                pltpu.VMEM((SLOT, width), BF16),
                pltpu.VMEM((3, 2, hl, width), BF16),
                pltpu.VMEM((2, PACK // 2, 128), BF16),
                pltpu.VMEM((8, 128), F32),
            ),
            in_specs=[vm] * 13 + [sm],
            out_specs=(vm,) * 5,
            scratch_shapes=[pltpu.VMEM(shape, kind) for group in spec for shape, kind in group.values()]
            + [pltpu.SemaphoreType.DMA((nsem,)), pltpu.SemaphoreType.DMA((nsem,))],
            compiler_params=pltpu.CompilerParams(
                collective_id=0, has_side_effects=True, vmem_limit_bytes=61 << 20
            ),
            name="layer",
        )(
            tokens, cotangent, w_inner, w_gate, w_out, w_proj.T, w_step, a_log, conv_weight, conv_bias, step_bias,
            skip_gain, norm_gain, lengths,
        )
        bsum, dsc, gout, sout, vout = mid
        if replicas > 2:
            groups = [[r for r in range(replicas) if r % 2 == k] for k in range(2)]
            gout, sout, vout = (
                lax.psum(v.astype(F32), "replica", axis_index_groups=groups) for v in (gout, sout, vout)
            )
        outs = pl.pallas_call(
            functools.partial(last_kernel, hl, piece),
            out_shape=(
                sds((SLOT, width), BF16),
                sds((SLOT, width), F32),
                sds((piece,), F32),
                sds((width, el), F32),
                sds((width, el), F32),
                sds((CONV, el), F32),
                sds((el,), F32),
                sds((PROJ, el), F32),
                sds((RANK, el), F32),
                sds((el,), F32),
                sds((STATE, el), F32),
                sds((el,), F32),
                sds((el, width), F32),
            ),
            in_specs=[vm, vm, sm] + [vm] * 5,
            out_specs=(vm,) * 13,
            compiler_params=pltpu.CompilerParams(vmem_limit_bytes=16 << 20),
            name="results",
        )(tokens, cotangent, lengths, bsum, dsc, gout, sout, vout)
        return outs[:7] + (outs[7].T,) + outs[8:]

    return local


def solution(mesh):
    return jax.shard_map(
        make_local(mesh.shape["replica"], mesh.shape["shard"]),
        mesh=mesh,
        in_specs=(
            P(("replica", "shard"), None),
            P("shard"),
            P(None, "shard"),
            P(None, "shard"),
            P(None, "shard"),
            P("shard"),
            P("shard", None),
            P(None, "shard"),
            P("shard"),
            P(None, "shard"),
            P("shard"),
            P("shard", None),
            P(("replica", "shard"), None),
            P(("replica", "shard")),
        ),
        out_specs=(
            P(("replica", "shard"), None),
            P(("replica", "shard"), None),
            P("shard"),
            P(None, "shard"),
            P(None, "shard"),
            P(None, "shard"),
            P("shard"),
            P("shard", None),
            P(None, "shard"),
            P("shard"),
            P(None, "shard"),
            P("shard"),
            P("shard", None),
        ),
        check_vma=False,
    )
```

```python
import functools
import math
from types import SimpleNamespace

import jax
import jax.numpy as jnp
from jax import lax
from jax.experimental import pallas as pl
from jax.experimental.pallas import tpu as pltpu
from jax.sharding import PartitionSpec as P

RANK = 64
STATE = 16
CONV = 4
SLOT = 128
EPS = 1e-05
LN2 = math.log(2.0)
PROJ = RANK + 2 * STATE
PACK = 192
STEP_ROW = PROJ
LOG_ROW = STEP_ROW + RANK
TAP_ROW = LOG_ROW + STATE
CONV_ROW = TAP_ROW + CONV
BIAS_ROW = CONV_ROW + 1
SKIP_ROW = BIAS_ROW + 1
GAIN_ROW = SKIP_ROW + 1
MESH = pl.DeviceIdType.MESH
F32 = jnp.float32
BF16 = jnp.bfloat16


def sigmoid(value):
    return 0.5 * jnp.tanh(0.5 * value) + 0.5


def nt(left, right):
    return lax.dot_general(left, right, (((1,), (1,)), ((), ())), preferred_element_type=F32)


def nn(left, right):
    return lax.dot_general(left, right, (((1,), (0,)), ((), ())), preferred_element_type=F32)


def tn(left, right):
    return lax.dot_general(left, right, (((0,), (0,)), ((), ())), preferred_element_type=F32)


def buffers(depth, hl, width, shards, piece):
    cols = depth * hl
    rows = 8 * SLOT
    def reduce_small(part):
        low, full = ((4, part, 128), BF16), ((4, part, 128), F32)
        return dict(s1=low, l1=low, s2=low, l2=low, s3=low, l3=low, own=full, oth=full)

    reduce_large = dict(
        s1=((4, SLOT, width), BF16),
        l1=((4, SLOT, width), BF16),
        sx=((2, SLOT // 2, width), BF16),
        sy=((2, SLOT // 2, width), BF16),
        lx=((2, SLOT // 2, width), BF16),
        ly=((2, SLOT // 2, width), BF16),
        tx=((SLOT // 2, width), BF16),
        ty=((SLOT // 2, width), BF16),
        mx=((SLOT // 2, width), BF16),
        my=((SLOT // 2, width), BF16),
    )
    shapes = dict(
        wt=((3, depth, hl, width), BF16),
        ws=((2, cols, width), BF16),
        pka=((depth, PACK // 2, 128), BF16),
        wpt=((128, cols), BF16),
        gb=((2, 2, 8, cols), F32),
        t1=((rows, cols), F32),
        t2=((rows, cols), F32),
        gl=((1, width), F32),
        nb=((4, 2, SLOT, width), BF16),
        db=((4, 2, SLOT, width), BF16),
        pkl=((PACK, cols), F32),
        wst=((128, cols), BF16),
        rate=((STATE, 2, 8, 128), F32),
        ip=((8, SLOT + 8, cols), F32),
        dcp=((8, SLOT + 8, cols), F32),
        gacc=((cols, width), F32),
        tm=((rows, 128), F32),
        sel=((256, 2 * STATE * 128), BF16),
        bc=((SLOT, 2 * STATE, 8, 128), F32),
        sall=((SLOT // 2 + 1, STATE, 2, 16, 128), BF16),
        cl=((8, SLOT, cols), BF16),
        xc=((2, rows, 128), F32),
        pp=((4, 2, SLOT, 128), F32),
        slow=((8, SLOT, 128), BF16),
        dpj=((8, SLOT, 128), BF16),
        dt=((2, rows, 128), F32),
        ys=((2, rows, 128), F32),
        dm=((2, rows, 128), F32),
        ga=((STATE, 2, 8, 128), F32),
        carried=((STATE, 2, 8, 128), F32),
        go=((4, 2, SLOT, cols), BF16),
        dg=((4, 2, SLOT, cols), BF16),
        di=((4, 2, SLOT, cols), BF16),
        dsl=((8, SLOT, cols), BF16),
        gws=((3, depth, hl, width), BF16),
        gwl=((3, depth - 1, hl, width), BF16),
        gwx=((3, hl, width), BF16),
        sg=((PACK, cols), F32),
        sgs=((depth, PACK // 2, 128), BF16),
        sgl=((depth - 1, PACK // 2, 128), BF16),
        sgx=((PACK // 2, 128), BF16),
        vv=((1, width), F32),
        sum=((4, SLOT, width), F32),
        vs=((4, 8, 128), F32),
        vl=((3, 8, 128), F32),
        vz=((depth, 8, 128), F32),
    )
    part = reduce_small(SLOT // 2)
    return [shapes, part, part, reduce_large, part, part]


def main_kernel(names, depth, hl, piece, nsem, *refs):
    (tok, cot, win, wg, wo, wproj, wstep, alog, convw, convb, stepb, skipg, gain, lens) = refs[:14]
    (bsum, dsc, gout, sout, vout) = refs[14:19]
    send_sems, recv_sems = refs[-2:]
    sets, at = [], 19
    for group in names:
        sets.append(SimpleNamespace(**dict(zip(group, refs[at:]))))
        at += len(group)
    b = sets[0]
    width = tok.shape[1]
    cols = depth * hl
    el = 2 * hl
    count = 8 * SLOT
    half = SLOT // 2

    r = lax.axis_index("replica")
    s = lax.axis_index("shard")
    y = lax.rem(r, 2)
    f = s // 4
    x = lax.rem(s // 2, 2)
    c = lax.rem(s, 2)
    core = (r, s + 1 - 2 * c)
    xpeer = (r, s + 2 - 4 * x)
    ypeer = (r + 1 - 2 * y, s)
    zpos = [lax.rem(f + k, depth) for k in range(1, depth)]
    zpeers = [(r, s + 4 * (q - f)) for q in zpos]
    q0 = y * 2 + x
    qx = y * 2 + 1 - x
    qy = (1 - y) * 2 + x
    qd = (1 - y) * 2 + 1 - x
    oc = 1 - c
    top, low = slice(0, half), slice(half, SLOT)

    counter = [0]
    started = []
    line = depth == 4
    ends = (f == 0) | (f == 3)
    inner = (f == 1) | (f == 2)

    def ticket():
        counter[0] += 1
        assert counter[0] <= nsem
        return counter[0] - 1

    def remote(src, dst, dev, send, recv):
        return pltpu.make_async_remote_copy(
            src_ref=src,
            dst_ref=dst,
            send_sem=send_sems.at[send],
            recv_sem=recv_sems.at[recv],
            device_id=dev,
            device_id_type=MESH,
        )

    def rcopy(src, dst, dev):
        i = ticket()
        cp = remote(src, dst, dev, i, i)
        cp.start()
        started.append(cp)
        return cp

    def same(ref, dev):
        return rcopy(ref, ref, dev)

    def settle(cps):
        for cp in cps:
            cp.wait_send()
            started[:] = [other for other in started if other is not cp]

    def arrive(cps):
        for cp in cps:
            cp.wait_recv()

    def only(when, cp):
        @pl.when(when)
        def _():
            cp.start()

        def wait_send():
            @pl.when(when)
            def _():
                cp.wait_send()

        started.append(SimpleNamespace(wait_send=wait_send))

    def far(k):
        return ((f == 0) & (k == 3)) | ((f == 3) & (k == 1))

    def far_from(k):
        return ((f == 0) & (k == 1)) | ((f == 3) & (k == 3))

    def z_gather(piece):
        ids = [ticket() for _ in range(depth)]
        cps = {}
        for k in sorted(range(1, depth), key=lambda k: k != 2):
            cps[k] = remote(piece(f), piece(f), zpeers[k - 1], ids[k], ids[k])
            if line and k != 2:
                only(jnp.logical_not(far(k)), cps[k])
            else:
                cps[k].start()
                started.append(cps[k])
        return SimpleNamespace(piece=piece, ids=ids, cps=cps)

    def z_relay(st):
        if line:
            st.cps[2].wait_recv()
            q = 3 * (2 - jnp.where(inner, f, 1))
            near = jnp.where(inner, 2 * f - 1, 1)
            only(inner, remote(st.piece(q), st.piece(q), (r, s + 4 * (3 - q - f)), st.ids[0], st.ids[1] + near - 1))

    def z_arrive(st):
        for k in range(1, depth):
            if not (line and k == 2):
                st.cps[k].wait_recv()

    def z_scatter(send, land, extra):
        ids = [ticket() for _ in range(depth)]
        cps = {k: remote(send(zpos[k - 1]), land(k - 1), zpeers[k - 1], ids[k], ids[k]) for k in range(1, depth)}
        st = SimpleNamespace(send=send, land=land, extra=extra, cps=cps)
        if not line:
            for cp in cps.values():
                cp.start()
                started.append(cp)
            return st
        st.cross = remote(send(3 - f), extra, (r, s + 4 - 8 * (f // 3)), ids[0], ids[0])
        only(ends, st.cross)
        return st

    def z_direct(st):
        if line:
            only(ends, st.cps[2])
            for k in (1, 3):
                only(jnp.logical_not(far(k)), st.cps[k])
        return st

    def z_absorb(st):
        if line:

            @pl.when(inner)
            def _():
                st.cross.wait_recv()
                target = st.send(zpos[1])
                target[...] = (target[...].astype(F32) + st.extra[...].astype(F32)).astype(BF16)

            only(inner, st.cps[2])

    def z_sum(st, own):
        total = own
        for k in range(1, depth):
            if line and k != 2:

                @pl.when(jnp.logical_not(far_from(k)))
                def _():
                    st.cps[k].wait_recv()

            else:
                st.cps[k].wait_recv()
        for k in range(1, depth):
            value = st.land(k - 1)[...].astype(F32)
            total = total + (jnp.where(far_from(k), 0.0, value) if line and k != 2 else value)
        return total

    barrier = pltpu.get_barrier_semaphore()
    reach = [core, xpeer, ypeer]
    for dev in reach:
        pl.semaphore_signal(barrier, inc=1, device_id=dev, device_id_type=MESH)
    for k in range(1, depth):

        def hello():
            pl.semaphore_signal(barrier, inc=1, device_id=zpeers[k - 1], device_id_type=MESH)

        if line and k != 2:
            pl.when(jnp.logical_not(far(k)))(hello)
        else:
            hello()

    def lanes(value, n):
        value = value.astype(F32)
        if value.shape[1] == n:
            return value
        return jnp.concatenate([value, jnp.zeros((value.shape[0], n - value.shape[1]), F32)], axis=1)

    def folded(value, n):
        both = jnp.concatenate([value[: PACK // 2], value[PACK // 2 :]], axis=1)
        return lanes(both, 128).astype(BF16)

    def unfolded(value, n):
        return jnp.concatenate([value[:, :n], value[:, n : 2 * n]], axis=0)

    rows = [wproj[...], wstep[...], alog[...], convw[...]]
    rows += [v[...].reshape(1, el) for v in (convb, stepb, skipg)]
    rows = [v.astype(F32) for v in rows]
    rows.append(jnp.zeros((PACK - GAIN_ROW, el), F32))
    pack = jnp.concatenate(rows, axis=0)
    mine = jnp.where(y == 0, pack[:, :hl], pack[:, hl:])
    own_gain = gain[...].reshape(1, piece).astype(F32)
    rowid = lax.broadcasted_iota(jnp.int32, (PACK, 1), 0)
    b.pka[f] = folded(jnp.where(rowid == GAIN_ROW, own_gain, mine), hl)
    wint = win[...].T
    b.wt[0, f] = jnp.where(y == 0, wint[:hl], wint[hl:])
    t32 = tok[...].astype(F32)
    inv = lax.rsqrt(jnp.mean(t32 * t32, axis=1, keepdims=True) + EPS)
    b.nb[q0, c] = (t32 * inv).astype(BF16)

    if line:
        for w in range(3):
            for k in (1, 3):

                @pl.when(far_from(k))
                def _():
                    b.gwl[w, k - 1] = jnp.zeros((hl, width), BF16)

        for k in (1, 3):

            @pl.when(far_from(k))
            def _():
                b.sgl[k - 1] = jnp.zeros((PACK // 2, 128), BF16)

        pl.semaphore_wait(barrier, jnp.where(ends, 5, 6))
    else:
        pl.semaphore_wait(barrier, 2 + depth)

    def plane_start(buf):
        upper, lower = buf.at[q0, c, pl.ds(0, half)], buf.at[q0, c, pl.ds(half, half)]
        ax = same(upper, xpeer)
        by = same(lower, ypeer)
        bx = same(lower, xpeer)
        ay = same(upper, ypeer)
        oo = same(buf.at[q0, c], core)
        return ax, by, bx, ay, oo

    def plane_forward(buf, cps):
        ax, by, bx, ay, oo = cps
        ax.wait_recv()
        fa = same(buf.at[qx, c, pl.ds(0, half)], ypeer)
        by.wait_recv()
        fb = same(buf.at[qy, c, pl.ds(half, half)], xpeer)
        return bx, ay, oo, fa, fb

    def plane_core(buf, cps):
        bx, ay, oo, fa, fb = cps
        bx.wait_recv()
        ox = same(buf.at[qx, c], core)
        ay.wait_recv()
        oy = same(buf.at[qy, c], core)
        return oo, ox, oy, fa, fb

    def plane_last(buf, cps):
        oo, ox, oy, fa, fb = cps
        arrive([fa, fb])
        return oo, ox, oy, same(buf.at[qd, c], core)

    zsmall = z_gather(lambda q: b.pka.at[q])
    zin = z_gather(lambda q: b.wt.at[0, q])
    nstate = plane_start(b.nb)

    wgt = wg[...].T
    b.wt[1, f] = jnp.where(y == 0, wgt[:hl], wgt[hl:])
    b.wt[2, f] = wo[pl.ds(y * hl, hl), :]
    rowid = lax.broadcasted_iota(jnp.int32, (SLOT, 1), 0)
    b.db[q0, c] = jnp.where(rowid < lens[0], cot[...].astype(F32), 0.0).astype(BF16)
    z_relay(zsmall)
    nstate = plane_forward(b.nb, nstate)
    z_relay(zin)
    z_arrive(zsmall)
    locs = [unfolded(b.pka[i].astype(F32), hl) for i in range(depth)]
    pkl = jnp.concatenate(locs, axis=1)
    b.pkl[...] = pkl
    b.gb[c, x] = jnp.broadcast_to(pkl[GAIN_ROW : GAIN_ROW + 1], (8, cols))
    gx = same(b.gb.at[c, x], xpeer)
    dstate = plane_start(b.db)
    b.wst[...] = jnp.concatenate(
        [pkl[STEP_ROW:LOG_ROW], jnp.zeros((128 - RANK, cols), F32)], axis=0
    ).astype(BF16)
    b.wpt[...] = jnp.concatenate([pkl[:PROJ], jnp.zeros((128 - PROJ, cols), F32)], axis=0).astype(BF16)
    for n in range(STATE):
        row = -jnp.exp(pkl[LOG_ROW + n : LOG_ROW + n + 1]) * (1.0 / LN2)
        for et in range(2):
            b.rate[n, et] = jnp.broadcast_to(row[:, et * 128 : et * 128 + 128], (8, 128))
    nstate = plane_core(b.nb, nstate)
    b.ip[:, 0:8, :] = jnp.zeros((8, 8, cols), F32)
    b.dcp[:, SLOT : SLOT + 8, :] = jnp.zeros((8, 8, cols), F32)
    b.ga[...] = jnp.zeros((STATE, 2, 8, 128), F32)
    b.sall[0] = jnp.zeros((STATE, 2, 16, 128), BF16)
    b.sg[...] = jnp.zeros((PACK, cols), F32)
    source = lax.broadcasted_iota(jnp.int32, (256, 2 * STATE * 128), 0)
    target = lax.broadcasted_iota(jnp.int32, (256, 2 * STATE * 128), 1)
    b.sel[...] = jnp.where(lax.rem(source, 128) == RANK + target // 128, 1.0, 0.0).astype(BF16)
    gx.wait_recv()
    gc = same(b.gb.at[c], core)
    gc.wait_recv()
    pieces = []
    for i in range(depth):
        for j in range(2):
            for k in range(2):
                pieces.append(b.gb[k, j, 0:1, i * piece : (i + 1) * piece])
    b.gl[...] = jnp.concatenate(pieces, axis=1)

    z_arrive(zin)
    zgate = z_gather(lambda q: b.wt.at[1, q])
    zout = z_gather(lambda q: b.wt.at[2, q])

    def scaled(w):
        full = b.wt[w].reshape(cols, width).astype(F32)
        b.ws[w] = (full * b.gl[...]).astype(BF16)

    scaled(0)
    arrive(plane_last(b.nb, nstate))

    def row_of(i):
        return b.pkl[i : i + 1, :]

    taps = [row_of(TAP_ROW + k) for k in range(CONV)]
    cbias = row_of(CONV_ROW)
    sbias = row_of(BIAS_ROW)
    skip = row_of(SKIP_ROW)

    def slot_rows(j):
        return pl.ds(pl.multiple_of(j * SLOT, SLOT), SLOT)

    def pair(ref, at):
        return jnp.concatenate([ref[0, at, :], ref[1, at, :]], axis=1)

    def unpair(ref, at, value):
        ref[0, at, :] = value[:, :128]
        ref[1, at, :] = value[:, 128:]

    def convolved(j, begin, size):
        acc = jnp.broadcast_to(cbias, (size, cols))
        for k in range(CONV):
            acc = acc + taps[k] * b.ip[j, 5 + k + begin : 5 + k + begin + size, :]
        return acc

    b.ip[:, 8 : 8 + SLOT, :] = nt(b.nb[...].reshape(count, width), b.ws[0]).reshape(8, SLOT, cols)

    @pl.loop(0, 8)
    def _(j):
        acc = convolved(j, 0, SLOT)
        out = acc * sigmoid(acc)
        unpair(b.xc, slot_rows(j), out)
        b.cl[j] = out.astype(BF16)

    b.pp[...] = nt(b.cl[...].reshape(count, cols), b.wpt[...]).reshape(4, 2, SLOT, 128)

    def all_reduce(which, rows):
        g = sets[which]
        flight = []

        def first():
            g.s1[...] = b.pp[:, oc, rows, :].astype(BF16)
            flight[:] = [rcopy(g.s1, g.l1, core)]

        def second():
            arrive(flight)
            total = b.pp[:, c, rows, :] + g.l1[...].astype(F32)
            g.s2[...] = total.astype(BF16)
            flight[:] = [
                rcopy(g.s2.at[pl.ds(0, 2)], g.l2.at[pl.ds(0, 2)], xpeer),
                rcopy(g.s2.at[pl.ds(2, 2)], g.l2.at[pl.ds(2, 2)], ypeer),
            ]
            g.own[...] = total

        def third():
            arrive(flight)
            total = g.own[...] + g.l2[...].astype(F32)
            g.s3[...] = total.astype(BF16)
            flight[:] = [
                rcopy(g.s3.at[pl.ds(0, 2)], g.l3.at[pl.ds(0, 2)], ypeer),
                rcopy(g.s3.at[pl.ds(2, 2)], g.l3.at[pl.ds(2, 2)], xpeer),
            ]
            g.own[...] = total

        def fourth():
            arrive(flight)
            g.own[...] = g.own[...] + g.l3[...].astype(F32)
            flight[:] = [rcopy(g.own, g.oth, core)]

        return [first, second, third, fourth, lambda: arrive(flight)]

    def cut_of(h):
        return slice(h * half, h * half + half)

    def half_rows(j, h):
        return pl.ds(pl.multiple_of(j * SLOT + h * half, half), half)

    def packed_rows(j, h):
        return pl.ds(pl.multiple_of(h * 8 * half + j * half, half), half)

    front = all_reduce(1, cut_of(0))
    back = all_reduce(5, cut_of(1))
    for k in range(3):
        front[k]()
        back[k]()
    dstate = plane_forward(b.db, dstate)
    z_relay(zgate)
    front[3]()
    back[3]()
    dstate = plane_core(b.db, dstate)
    front[4]()

    def scan_inputs(which, h):
        @pl.loop(0, 4)
        def _(q):
            for cc, src in ((c, sets[which].own), (oc, sets[which].oth)):
                j = 2 * q + cc
                proj = src[q]
                b.tm[pl.ds(h * 8 * half + j, half, stride=8), :] = proj
                b.slow[j, cut_of(h), :] = proj.astype(BF16)

        span = slice(h * 8 * half, (h + 1) * 8 * half)
        b.t1[span, :] = nn(b.slow[:, cut_of(h), :].reshape(8 * half, 128), b.wst[...])

        @pl.loop(0, 8)
        def _(j):
            pre = b.t1[packed_rows(j, h), :] + sbias
            unpair(b.dt, half_rows(j, h), jnp.maximum(pre, 0.0) + jnp.log1p(jnp.exp(-jnp.abs(pre))))

        tm = b.tm[span, :]
        high = tm.astype(BF16)
        spread = jnp.concatenate([high, (tm - high.astype(F32)).astype(BF16)], axis=1)
        both = nn(spread, b.sel[...])
        for i in range(2 * STATE):
            b.bc[cut_of(h), i] = both[:, i * 128 : i * 128 + 128].reshape(half, 8, 128)

    zero = jnp.zeros((8, 128), F32)

    steps = 4

    def forward_steps(j, carry):
        base = steps * j
        ats = [pl.ds(base + i, 8, stride=SLOT) for i in range(steps)]
        size = [[b.dt[e, at, :] for e in range(2)] for at in ats]
        push = [[size[i][e] * b.xc[e, ats[i], :] for e in range(2)] for i in range(steps)]
        out = [[zero, zero] for _ in range(steps)]
        for n in range(STATE):
            for e in range(2):
                rate = b.rate[n, e]
                state = b.carried[n, e]
                kept = []
                for i in range(steps):
                    state = jnp.exp2(size[i][e] * rate) * state + push[i][e] * b.bc[base + i, n]
                    out[i][e] = out[i][e] + b.bc[base + i, STATE + n] * state
                    kept.append(state)
                b.carried[n, e] = state
                for p in range(steps // 2):
                    both_states = jnp.concatenate(kept[2 * p : 2 * p + 2], axis=0)
                    b.sall[(steps // 2) * j + p + 1, n, e] = both_states.astype(BF16)
        for i in range(steps):
            for e in range(2):
                b.ys[e, ats[i], :] = out[i][e]
        return carry

    b.carried[...] = jnp.zeros((STATE, 2, 8, 128), F32)
    scan_inputs(1, 0)
    lax.fori_loop(0, half // steps, forward_steps, 0)
    z_relay(zout)
    back[4]()
    scan_inputs(5, 1)
    dstate = plane_last(b.db, dstate)
    lax.fori_loop(half // steps, SLOT // steps, forward_steps, 0)

    arrive(dstate)
    z_arrive(zgate)
    scaled(1)
    b.t1[...] = nt(b.nb[...].reshape(count, width), b.ws[1])
    z_arrive(zout)
    b.t2[...] = nt(b.db[...].reshape(count, width), b.wt[2].reshape(cols, width))

    @pl.loop(0, 4)
    def _(q):
        for cc in range(2):
            at = slot_rows(2 * q + cc)
            gpre = b.t1[at, :]
            dgat = b.t2[at, :]
            conv = pair(b.xc, at)
            mixed = pair(b.ys, at) + skip * conv
            sig = sigmoid(gpre)
            act = gpre * sig
            b.go[q, cc] = (mixed * act).astype(BF16)
            dmix = dgat * act
            unpair(b.dm, at, dmix)
            slope = sig * (1.0 + gpre * (1.0 - sig))
            b.dg[q, cc] = (dgat * mixed * slope).astype(BF16)
            b.sg[SKIP_ROW : SKIP_ROW + 1, :] += jnp.sum(dmix * conv, axis=0, keepdims=True)

    def reduce_begin(dots, more):
        g = sets[3]

        def low_of(value, q):
            return (value + g.s1[q].astype(F32) if more else value).astype(BF16)

        g.s1[qd] = low_of(dots(lambda ref: ref[qd, oc]), qd)
        cores = [rcopy(g.s1.at[qd], g.l1.at[qd], core)]
        others = (qx, qy, q0)
        rest = dots(lambda ref: jnp.concatenate([ref[q, oc] for q in others], axis=0))
        for k, q in enumerate(others):
            g.s1[q] = low_of(rest[k * SLOT : (k + 1) * SLOT], q)
            cores.append(rcopy(g.s1.at[q], g.l1.at[q], core))
        mine = dots(lambda ref: ref[:, c].reshape(4 * SLOT, cols)).reshape(4, SLOT, width)
        b.sum[...] = b.sum[...] + mine if more else mine
        return cores

    def reduce_second(cores):
        g = sets[3]

        def chip(q, rows):
            return (b.sum[q, rows, :] + g.l1[q, rows, :].astype(F32)).astype(BF16)

        cores[0].wait_recv()
        g.sx[1] = chip(qd, top)
        x1 = rcopy(g.sx.at[1], g.lx.at[1], xpeer)
        g.sy[1] = chip(qd, low)
        y1 = rcopy(g.sy.at[1], g.ly.at[1], ypeer)
        cores[1].wait_recv()
        g.sx[0] = chip(qx, top)
        x0 = rcopy(g.sx.at[0], g.lx.at[0], xpeer)
        cores[2].wait_recv()
        g.sy[0] = chip(qy, low)
        y0 = rcopy(g.sy.at[0], g.ly.at[0], ypeer)
        return x1, y1, x0, y0

    def reduce_third(cps):
        g = sets[3]
        x1, y1, x0, y0 = cps
        x1.wait_recv()
        g.ty[...] = (b.sum[qy, top, :] + g.l1[qy, top, :].astype(F32) + g.lx[1].astype(F32)).astype(BF16)
        c1 = rcopy(g.ty, g.my, ypeer)
        y1.wait_recv()
        g.tx[...] = (b.sum[qx, low, :] + g.l1[qx, low, :].astype(F32) + g.ly[1].astype(F32)).astype(BF16)
        c2 = rcopy(g.tx, g.mx, xpeer)
        return x0, y0, c1, c2

    def reduce_end(cores, cps, out):
        g = sets[3]
        cores[3].wait_recv()
        arrive(cps)
        for rows, near, far_ref in ((top, g.lx, g.my), (low, g.ly, g.mx)):
            out[rows, :] = (
                b.sum[q0, rows, :]
                + g.l1[q0, rows, :].astype(F32)
                + near[0].astype(F32)
                + far_ref[...].astype(F32)
            ).astype(BF16)

    def weight_grad(w, grad, gained):
        b.gws[w] = (grad * b.gl[...] if gained else grad).astype(BF16).reshape(depth, hl, width)
        return grad

    def rows_grad(lhs, rhs):
        return tn(lhs[...].reshape(count, cols), rhs[...].reshape(count, width))

    def gain_grad(w, grad):
        return jnp.sum(grad * b.wt[w].reshape(cols, width).astype(F32), axis=0, keepdims=True)

    def weight_send(w, at):
        return z_scatter(
            lambda q: b.gws.at[w, q, at], lambda k: b.gwl.at[w, k, at], b.gwx.at[w, at]
        )

    def weight_sum(w, st, at):
        gout[w, y, at, :] = z_sum(st, b.gws[w, f, at, :].astype(F32)).astype(BF16)
        return same(gout.at[w, y, at], ypeer)

    every = pl.ds(0, hl)

    weight_grad(2, rows_grad(b.go, b.db), False)
    zgo = z_direct(weight_send(2, every))
    grad = weight_grad(1, rows_grad(b.dg, b.nb), True)
    zgg = z_direct(weight_send(1, every))
    b.vv[...] = gain_grad(1, grad)
    bone = reduce_begin(lambda pick: nn(pick(b.go), b.wt[2].reshape(cols, width)), False)

    def backward_pair(j, carry):
        k = SLOT // 2 - 1 - j
        ats = [pl.ds(2 * k + i, 8, stride=SLOT) for i in range(2)]
        size = [[b.dt[e, at, :] for e in range(2)] for at in ats]
        conv = [[b.xc[e, at, :] for e in range(2)] for at in ats]
        dmix = [[b.dm[e, at, :] for e in range(2)] for at in ats]
        push = [jnp.concatenate([size[i][e] * conv[i][e] for i in range(2)], axis=0).astype(BF16) for e in range(2)]
        dlow = [jnp.concatenate([dmix[i][e] for i in range(2)], axis=0).astype(BF16) for e in range(2)]
        rate_sum = [[zero, zero], [zero, zero]]
        weighted = [[zero, zero], [zero, zero]]
        new = []
        for n in range(STATE):
            inm = [b.bc[2 * k + i, n] for i in range(2)]
            outm = [b.bc[2 * k + i, STATE + n] for i in range(2)]
            dins, douts = [], []
            for e in range(2):
                rate = b.rate[n, e]
                here = b.sall[k + 1, n, e]
                before = [b.sall[k, n, e].astype(F32)[8:16], here.astype(F32)[0:8]]
                back = carry[2 * n + e]
                lams = [None, None]
                acc = b.ga[n, e]
                for i in (1, 0):
                    lam = outm[i] * dmix[i][e] + back
                    back = jnp.exp2(size[i][e] * rate) * lam
                    grad = back * before[i]
                    rate_sum[i][e] = rate_sum[i][e] + grad * rate
                    weighted[i][e] = weighted[i][e] + lam * inm[i]
                    acc = acc + grad * size[i][e]
                    lams[i] = lam
                b.ga[n, e] = acc
                new.append(back)
                dins.append(jnp.concatenate(lams, axis=0).astype(BF16) * push[e])
                douts.append(dlow[e] * here)
            b.sall[k + 1, n, 0] = dins[0] + dins[1]
            b.sall[k + 1, n, 1] = douts[0] + douts[1]
        for i in range(2):
            for e in range(2):
                b.ys[e, ats[i], :] = rate_sum[i][e] * LN2 + conv[i][e] * weighted[i][e]
                b.xc[e, ats[i], :] = size[i][e] * weighted[i][e]
        return tuple(new)

    carry = tuple(zero for _ in range(2 * STATE))
    carry = lax.fori_loop(0, SLOT // 16, backward_pair, carry, unroll=2)
    btwo = reduce_second(bone)
    carry = lax.fori_loop(SLOT // 16, 3 * SLOT // 16, backward_pair, carry, unroll=2)
    z_absorb(zgo)
    bthree = reduce_third(btwo)
    carry = lax.fori_loop(3 * SLOT // 16, SLOT // 4, backward_pair, carry, unroll=2)

    def map_sums(h):
        begin = 1 + h * half // 2
        parts = [
            b.sall[begin : begin + half // 2, n, k].reshape(8 * half, 128) for k in range(2) for n in range(STATE)
        ]
        b.tm[h * 8 * half : (h + 1) * 8 * half, :] = nt(jnp.concatenate(parts, axis=1), b.sel[0:128, :])

    def rank_part(h):
        span = slice(h * 8 * half, (h + 1) * 8 * half)
        b.t1[span, :] = nn(b.slow[:, cut_of(h), :].reshape(8 * half, 128), b.wst[...])

        @pl.loop(0, 8)
        def _(j):
            dpre = pair(b.ys, half_rows(j, h)) * sigmoid(b.t1[packed_rows(j, h), :] + sbias)
            b.sg[BIAS_ROW : BIAS_ROW + 1, :] += jnp.sum(dpre, axis=0, keepdims=True)
            b.dsl[j, cut_of(h), :] = dpre.astype(BF16)

        rank = nt(b.dsl[:, cut_of(h), :].reshape(8 * half, cols), b.wst[...])
        for j in range(8):
            maps = b.tm[pl.ds(h * 8 * half + j, half, stride=8), :]
            b.pp[j // 2, j % 2, cut_of(h), :] = rank[j * half : (j + 1) * half] + maps

    def slopes(h):
        @pl.loop(0, 8)
        def _(j):
            at = half_rows(j, h)
            cpre = convolved(j, h * half, half)
            sig = sigmoid(cpre)
            b.t2[at, :] = sig * (1.0 + cpre * (1.0 - sig))
            unpair(b.dm, at, pair(b.xc, at) + pair(b.dm, at) * skip)

    def inner_part(which, h):
        @pl.loop(0, 4)
        def _(q):
            for cc, src in ((c, sets[which].own), (oc, sets[which].oth)):
                b.dpj[2 * q + cc, cut_of(h), :] = src[q].astype(BF16)

        span = slice(h * 8 * half, (h + 1) * 8 * half)
        b.t1[span, :] = nn(b.dpj[:, cut_of(h), :].reshape(8 * half, 128), b.wpt[...])

        @pl.loop(0, 4)
        def _(q):
            for cc in range(2):
                j = 2 * q + cc
                at = half_rows(j, h)
                dpre = (pair(b.dm, at) + b.t1[packed_rows(j, h), :]) * b.t2[at, :]
                b.dcp[j, cut_of(h), :] = dpre
                sums = []
                for k in range(CONV):
                    begin = 5 + k + h * half
                    sums.append(jnp.sum(dpre * b.ip[j, begin : begin + half, :], axis=0, keepdims=True))
                sums.append(jnp.sum(dpre, axis=0, keepdims=True))
                b.sg[TAP_ROW : CONV_ROW + 1, :] += jnp.concatenate(sums, axis=0)
                dinner = taps[CONV - 1] * dpre
                for k in range(CONV - 1):
                    begin = CONV - 1 - k + h * half
                    dinner = dinner + taps[k] * b.dcp[j, begin : begin + half, :]
                b.di[q, cc, cut_of(h), :] = dinner.astype(BF16)

    def inner_grad(h):
        return tn(
            b.di[:, :, cut_of(h), :].reshape(8 * half, cols), b.nb[:, :, cut_of(h), :].reshape(8 * half, width)
        )

    map_sums(1)
    rank_part(1)
    later = all_reduce(2, cut_of(1))
    later[0]()
    marks = [SLOT // 4 + v for v in (0, 8, 26, SLOT // 4)]
    for k in range(3):
        carry = lax.fori_loop(marks[k], marks[k + 1], backward_pair, carry, unroll=2)
        if k < 2:
            later[k + 1]()
    z_absorb(zgg)
    map_sums(0)
    rank_part(0)
    later[3]()
    sooner = all_reduce(4, cut_of(0))
    sooner[0]()
    later[4]()
    slopes(1)
    sooner[1]()
    inner_part(2, 1)
    reduce_end(bone, bthree, bsum)
    sooner[2]()
    hold = [weight_sum(2, zgo, every)]
    slopes(0)
    b.gacc[...] = inner_grad(1)
    settle([*bone, *btwo, *bthree[2:]])
    gate_dot = lambda ref: nn(ref.reshape(4 * SLOT, cols), b.ws[1]).reshape(4, SLOT, width)
    sets[3].s1[...] = gate_dot(b.dg[:, oc]).astype(BF16)
    b.sum[...] = gate_dot(b.dg[:, c])
    sooner[3]()
    hold.append(weight_sum(1, zgg, every))
    sooner[4]()
    inner_part(4, 0)

    grad = weight_grad(0, b.gacc[...] + inner_grad(0), True)
    first, second = pl.ds(0, hl // 2), pl.ds(hl // 2, hl // 2)
    zgi = [weight_send(0, first), weight_send(0, second)]
    for st in zgi:
        z_direct(st)
    total = b.vv[...] + gain_grad(0, grad)
    for i in range(8):
        b.vs[0, i : i + 1, :] = total[:, i * 128 : i * 128 + 128]
    v1 = rcopy(b.vs.at[0], b.vl.at[0], xpeer)
    done = reduce_begin(lambda pick: nn(pick(b.di), b.ws[0]), True)
    v1.wait_recv()
    b.vs[1] = b.vs[0] + b.vl[0]
    v2 = rcopy(b.vs.at[1], b.vl.at[1], ypeer)
    dtwo = reduce_second(done)
    z_absorb(zgi[0])
    z_absorb(zgi[1])
    for n in range(STATE):
        parts = [jnp.sum(b.ga[n, e] * b.rate[n, e], axis=0, keepdims=True) for e in range(2)]
        b.sg[LOG_ROW + n : LOG_ROW + n + 1, :] = jnp.concatenate(parts, axis=1) * LN2
    grad = tn(b.dpj[...].reshape(count, 128), b.cl[...].reshape(count, cols))
    b.sg[0:PROJ, :] = grad[:PROJ]
    grad = tn(b.slow[...].reshape(count, 128), b.dsl[...].reshape(count, cols))
    b.sg[STEP_ROW:LOG_ROW, :] = grad[:RANK]
    for i in range(depth):
        b.sgs[i] = folded(b.sg[:, i * hl : (i + 1) * hl], hl)
    zgs = z_direct(z_scatter(lambda q: b.sgs.at[q], lambda k: b.sgl.at[k], b.sgx))
    v2.wait_recv()
    b.vs[2] = b.vs[1] + b.vl[1]
    v3 = rcopy(b.vs.at[2], b.vl.at[2], core)
    dthree = reduce_third(dtwo)
    v3.wait_recv()
    b.vz[f] = b.vs[2] + b.vl[2]
    v4 = z_gather(lambda q: b.vz.at[q])
    yin = [weight_sum(0, zgi[0], first)]
    z_absorb(zgs)
    yin.append(weight_sum(0, zgi[1], second))
    sout[y] = z_sum(zgs, b.sgs[f].astype(F32)).astype(BF16)
    ysmall = same(sout.at[y], ypeer)
    z_relay(v4)
    reduce_end(done, dthree, dsc)
    z_arrive(v4)
    total = b.vz[0]
    for k in range(1, depth):
        total = total + b.vz[k]
    vout[...] = total
    arrive(hold + yin + [ysmall])
    for cp in started:
        cp.wait_send()


def last_kernel(hl, piece, tok, cot, lens, bsum, dsc, gout, sout, vout, *outs):
    (out, dtok, ggain, ginner, ggate, gconv, gcb, gproj, gstep, gsb, glog, gskip, gwout) = outs
    s = lax.axis_index("shard")
    t32 = tok[...].astype(F32)
    rowid = lax.broadcasted_iota(jnp.int32, (SLOT, 1), 0)
    out[...] = (t32 + jnp.where(rowid < lens[0], bsum[...].astype(F32), 0.0)).astype(BF16)
    inv = lax.rsqrt(jnp.mean(t32 * t32, axis=1, keepdims=True) + EPS)
    ds = dsc[...].astype(F32)
    mean = jnp.mean(ds * t32, axis=1, keepdims=True)
    dtok[...] = cot[...].astype(F32) + inv * ds - t32 * (inv * inv * inv * mean)
    width = tok.shape[1]
    el = 2 * hl
    ginner[...] = gout[0].reshape(el, width).T.astype(F32)
    ggate[...] = gout[1].reshape(el, width).T.astype(F32)
    gwout[...] = gout[2].reshape(el, width).astype(F32)
    small = sout[...].astype(F32)
    halves = [jnp.concatenate([small[k][:, :hl], small[k][:, hl:el]], axis=0) for k in range(2)]
    both = jnp.concatenate(halves, axis=1)
    gproj[...] = both[:PROJ]
    gstep[...] = both[STEP_ROW:LOG_ROW]
    glog[...] = both[LOG_ROW:TAP_ROW]
    gconv[...] = both[TAP_ROW:CONV_ROW]
    gcb[...] = both[CONV_ROW : CONV_ROW + 1].reshape(el)
    gsb[...] = both[BIAS_ROW : BIAS_ROW + 1].reshape(el)
    gskip[...] = both[SKIP_ROW : SKIP_ROW + 1].reshape(el)
    per = 128 // piece
    vec = vout[...]
    rows = lax.broadcasted_iota(jnp.int32, (8, 128), 0)
    row = jnp.sum(jnp.where(rows == s // per, vec, 0.0), axis=0, keepdims=True)
    pick = jnp.zeros((1, piece), F32)
    for i in range(per):
        pick = jnp.where(lax.rem(s, per) == i, row[:, i * piece : (i + 1) * piece], pick)
    ggain[...] = pick.reshape(piece)


def make_local(replicas, shards):
    depth = shards // 4

    def local(
        tokens, norm_gain, w_inner, w_gate, conv_weight, conv_bias, w_proj, w_step, step_bias, a_log, skip_gain,
        w_out, cotangent, lengths,
    ):
        width = tokens.shape[1]
        el = w_inner.shape[1]
        hl = el // 2
        piece = norm_gain.shape[0]
        spec = buffers(depth, hl, width, shards, piece)
        nsem = 96 + 16 * depth
        vm = pl.BlockSpec(memory_space=pltpu.VMEM)
        sm = pl.BlockSpec(memory_space=pltpu.SMEM)
        sds = jax.ShapeDtypeStruct
        mid = pl.pallas_call(
            functools.partial(main_kernel, [tuple(group) for group in spec], depth, hl, piece, nsem),
            out_shape=(
                pltpu.VMEM((SLOT, width), BF16),
                pltpu.VMEM((SLOT, width), BF16),
                pltpu.VMEM((3, 2, hl, width), BF16),
                pltpu.VMEM((2, PACK // 2, 128), BF16),
                pltpu.VMEM((8, 128), F32),
            ),
            in_specs=[vm] * 13 + [sm],
            out_specs=(vm,) * 5,
            scratch_shapes=[pltpu.VMEM(shape, kind) for group in spec for shape, kind in group.values()]
            + [pltpu.SemaphoreType.DMA((nsem,)), pltpu.SemaphoreType.DMA((nsem,))],
            compiler_params=pltpu.CompilerParams(
                collective_id=0, has_side_effects=True, vmem_limit_bytes=61 << 20
            ),
            name="layer",
        )(
            tokens, cotangent, w_inner, w_gate, w_out, w_proj.T, w_step, a_log, conv_weight, conv_bias, step_bias,
            skip_gain, norm_gain, lengths,
        )
        bsum, dsc, gout, sout, vout = mid
        if replicas > 2:
            groups = [[r for r in range(replicas) if r % 2 == k] for k in range(2)]
            gout, sout, vout = (
                lax.psum(v.astype(F32), "replica", axis_index_groups=groups) for v in (gout, sout, vout)
            )
        outs = pl.pallas_call(
            functools.partial(last_kernel, hl, piece),
            out_shape=(
                sds((SLOT, width), BF16),
                sds((SLOT, width), F32),
                sds((piece,), F32),
                sds((width, el), F32),
                sds((width, el), F32),
                sds((CONV, el), F32),
                sds((el,), F32),
                sds((PROJ, el), F32),
                sds((RANK, el), F32),
                sds((el,), F32),
                sds((STATE, el), F32),
                sds((el,), F32),
                sds((el, width), F32),
            ),
            in_specs=[vm, vm, sm] + [vm] * 5,
            out_specs=(vm,) * 13,
            compiler_params=pltpu.CompilerParams(vmem_limit_bytes=16 << 20),
            name="results",
        )(tokens, cotangent, lengths, bsum, dsc, gout, sout, vout)
        return outs[:7] + (outs[7].T,) + outs[8:]

    return local


def solution(mesh):
    return jax.shard_map(
        make_local(mesh.shape["replica"], mesh.shape["shard"]),
        mesh=mesh,
        in_specs=(
            P(("replica", "shard"), None),
            P("shard"),
            P(None, "shard"),
            P(None, "shard"),
            P(None, "shard"),
            P("shard"),
            P("shard", None),
            P(None, "shard"),
            P("shard"),
            P(None, "shard"),
            P("shard"),
            P("shard", None),
            P(("replica", "shard"), None),
            P(("replica", "shard")),
        ),
        out_specs=(
            P(("replica", "shard"), None),
            P(("replica", "shard"), None),
            P("shard"),
            P(None, "shard"),
            P(None, "shard"),
            P(None, "shard"),
            P("shard"),
            P("shard", None),
            P(None, "shard"),
            P("shard"),
            P(None, "shard"),
            P("shard"),
            P("shard", None),
        ),
        check_vma=False,
    )
```

```python
import functools
import math
from types import SimpleNamespace

import jax
import jax.numpy as jnp
from jax import lax
from jax.experimental import pallas as pl
from jax.experimental.pallas import tpu as pltpu
from jax.sharding import PartitionSpec as P

RANK = 64
STATE = 16
CONV = 4
SLOT = 128
EPS = 1e-05
LN2 = math.log(2.0)
PROJ = RANK + 2 * STATE
PACK = 192
STEP_ROW = PROJ
LOG_ROW = STEP_ROW + RANK
TAP_ROW = LOG_ROW + STATE
CONV_ROW = TAP_ROW + CONV
BIAS_ROW = CONV_ROW + 1
SKIP_ROW = BIAS_ROW + 1
GAIN_ROW = SKIP_ROW + 1
MESH = pl.DeviceIdType.MESH
F32 = jnp.float32
BF16 = jnp.bfloat16


def sigmoid(value):
    return 0.5 * jnp.tanh(0.5 * value) + 0.5


def nt(left, right):
    return lax.dot_general(left, right, (((1,), (1,)), ((), ())), preferred_element_type=F32)


def nn(left, right):
    return lax.dot_general(left, right, (((1,), (0,)), ((), ())), preferred_element_type=F32)


def tn(left, right):
    return lax.dot_general(left, right, (((0,), (0,)), ((), ())), preferred_element_type=F32)


def buffers(depth, hl, width, shards, piece):
    cols = depth * hl
    rows = 8 * SLOT
    def reduce_small(part):
        low, full = ((4, part, 128), BF16), ((4, part, 128), F32)
        return dict(s1=low, l1=low, s2=low, l2=low, s3=low, l3=low, own=full, oth=full)

    reduce_large = dict(
        s1=((4, SLOT, width), BF16),
        l1=((4, SLOT, width), BF16),
        sx=((2, SLOT // 2, width), BF16),
        sy=((2, SLOT // 2, width), BF16),
        lx=((2, SLOT // 2, width), BF16),
        ly=((2, SLOT // 2, width), BF16),
        tx=((SLOT // 2, width), BF16),
        ty=((SLOT // 2, width), BF16),
        mx=((SLOT // 2, width), BF16),
        my=((SLOT // 2, width), BF16),
    )
    shapes = dict(
        wt=((3, depth, hl, width), BF16),
        ws=((2, cols, width), BF16),
        pka=((depth, PACK // 2, 128), BF16),
        wpt=((128, cols), BF16),
        gb=((2, 2, 8, cols), F32),
        t1=((rows, cols), F32),
        t2=((rows, cols), F32),
        gl=((1, width), F32),
        nb=((4, 2, SLOT, width), BF16),
        db=((4, 2, SLOT, width), BF16),
        pkl=((PACK, cols), F32),
        wst=((128, cols), BF16),
        rate=((STATE, 2, 8, 128), F32),
        ip=((8, SLOT + 8, cols), F32),
        dcp=((8, SLOT + 8, cols), F32),
        gacc=((cols, width), F32),
        tm=((rows, 128), F32),
        sel=((256, 2 * STATE * 128), BF16),
        bc=((SLOT, 2 * STATE, 8, 128), F32),
        sall=((SLOT // 2 + 1, STATE, 2, 16, 128), BF16),
        cl=((8, SLOT, cols), BF16),
        xc=((2, rows, 128), F32),
        pp=((4, 2, SLOT, 128), F32),
        slow=((8, SLOT, 128), BF16),
        dpj=((8, SLOT, 128), BF16),
        dt=((2, rows, 128), F32),
        ys=((2, rows, 128), F32),
        dm=((2, rows, 128), F32),
        ga=((STATE, 2, 8, 128), F32),
        carried=((STATE, 2, 8, 128), F32),
        go=((4, 2, SLOT, cols), BF16),
        dg=((4, 2, SLOT, cols), BF16),
        di=((4, 2, SLOT, cols), BF16),
        dsl=((8, SLOT, cols), BF16),
        gws=((3, depth, hl, width), BF16),
        gwl=((3, depth - 1, hl, width), BF16),
        gwx=((3, hl, width), BF16),
        sg=((PACK, cols), F32),
        sgs=((depth, PACK // 2, 128), BF16),
        sgl=((depth - 1, PACK // 2, 128), BF16),
        sgx=((PACK // 2, 128), BF16),
        vv=((1, width), F32),
        sum=((4, SLOT, width), F32),
        vs=((4, 8, 128), F32),
        vl=((3, 8, 128), F32),
        vz=((depth, 8, 128), F32),
    )
    part = reduce_small(SLOT // 2)
    return [shapes, part, part, reduce_large, part, part]


def main_kernel(names, depth, hl, piece, nsem, *refs):
    (tok, cot, win, wg, wo, wproj, wstep, alog, convw, convb, stepb, skipg, gain, lens) = refs[:14]
    (bsum, dsc, gout, sout, vout) = refs[14:19]
    send_sems, recv_sems = refs[-2:]
    sets, at = [], 19
    for group in names:
        sets.append(SimpleNamespace(**dict(zip(group, refs[at:]))))
        at += len(group)
    b = sets[0]
    width = tok.shape[1]
    cols = depth * hl
    el = 2 * hl
    count = 8 * SLOT
    half = SLOT // 2

    r = lax.axis_index("replica")
    s = lax.axis_index("shard")
    y = lax.rem(r, 2)
    f = s // 4
    x = lax.rem(s // 2, 2)
    c = lax.rem(s, 2)
    core = (r, s + 1 - 2 * c)
    xpeer = (r, s + 2 - 4 * x)
    ypeer = (r + 1 - 2 * y, s)
    zpos = [lax.rem(f + k, depth) for k in range(1, depth)]
    zpeers = [(r, s + 4 * (q - f)) for q in zpos]
    q0 = y * 2 + x
    qx = y * 2 + 1 - x
    qy = (1 - y) * 2 + x
    qd = (1 - y) * 2 + 1 - x
    oc = 1 - c
    top, low = slice(0, half), slice(half, SLOT)

    counter = [0]
    started = []
    line = depth == 4
    ends = (f == 0) | (f == 3)
    inner = (f == 1) | (f == 2)

    def ticket():
        counter[0] += 1
        assert counter[0] <= nsem
        return counter[0] - 1

    def remote(src, dst, dev, send, recv):
        return pltpu.make_async_remote_copy(
            src_ref=src,
            dst_ref=dst,
            send_sem=send_sems.at[send],
            recv_sem=recv_sems.at[recv],
            device_id=dev,
            device_id_type=MESH,
        )

    def rcopy(src, dst, dev):
        i = ticket()
        cp = remote(src, dst, dev, i, i)
        cp.start()
        started.append(cp)
        return cp

    def same(ref, dev):
        return rcopy(ref, ref, dev)

    def settle(cps):
        for cp in cps:
            cp.wait_send()
            started[:] = [other for other in started if other is not cp]

    def arrive(cps):
        for cp in cps:
            cp.wait_recv()

    def only(when, cp):
        @pl.when(when)
        def _():
            cp.start()

        def wait_send():
            @pl.when(when)
            def _():
                cp.wait_send()

        started.append(SimpleNamespace(wait_send=wait_send))

    def far(k):
        return ((f == 0) & (k == 3)) | ((f == 3) & (k == 1))

    def far_from(k):
        return ((f == 0) & (k == 1)) | ((f == 3) & (k == 3))

    def z_gather(piece):
        ids = [ticket() for _ in range(depth)]
        cps = {}
        for k in sorted(range(1, depth), key=lambda k: k != 2):
            cps[k] = remote(piece(f), piece(f), zpeers[k - 1], ids[k], ids[k])
            if line and k != 2:
                only(jnp.logical_not(far(k)), cps[k])
            else:
                cps[k].start()
                started.append(cps[k])
        return SimpleNamespace(piece=piece, ids=ids, cps=cps)

    def z_relay(st):
        if line:
            st.cps[2].wait_recv()
            q = 3 * (2 - jnp.where(inner, f, 1))
            near = jnp.where(inner, 2 * f - 1, 1)
            only(inner, remote(st.piece(q), st.piece(q), (r, s + 4 * (3 - q - f)), st.ids[0], st.ids[1] + near - 1))

    def z_arrive(st):
        for k in range(1, depth):
            if not (line and k == 2):
                st.cps[k].wait_recv()

    def z_scatter(send, land, extra):
        ids = [ticket() for _ in range(depth)]
        cps = {k: remote(send(zpos[k - 1]), land(k - 1), zpeers[k - 1], ids[k], ids[k]) for k in range(1, depth)}
        st = SimpleNamespace(send=send, land=land, extra=extra, cps=cps)
        if not line:
            for cp in cps.values():
                cp.start()
                started.append(cp)
            return st
        st.cross = remote(send(3 - f), extra, (r, s + 4 - 8 * (f // 3)), ids[0], ids[0])
        only(ends, st.cross)
        return st

    def z_direct(st):
        if line:
            only(ends, st.cps[2])
            for k in (1, 3):
                only(jnp.logical_not(far(k)), st.cps[k])
        return st

    def z_absorb(st):
        if line:

            @pl.when(inner)
            def _():
                st.cross.wait_recv()
                target = st.send(zpos[1])
                target[...] = (target[...].astype(F32) + st.extra[...].astype(F32)).astype(BF16)

            only(inner, st.cps[2])

    def z_sum(st, own):
        total = own
        for k in range(1, depth):
            if line and k != 2:

                @pl.when(jnp.logical_not(far_from(k)))
                def _():
                    st.cps[k].wait_recv()

            else:
                st.cps[k].wait_recv()
        for k in range(1, depth):
            value = st.land(k - 1)[...].astype(F32)
            total = total + (jnp.where(far_from(k), 0.0, value) if line and k != 2 else value)
        return total

    barrier = pltpu.get_barrier_semaphore()
    reach = [core, xpeer, ypeer]
    for dev in reach:
        pl.semaphore_signal(barrier, inc=1, device_id=dev, device_id_type=MESH)
    for k in range(1, depth):

        def hello():
            pl.semaphore_signal(barrier, inc=1, device_id=zpeers[k - 1], device_id_type=MESH)

        if line and k != 2:
            pl.when(jnp.logical_not(far(k)))(hello)
        else:
            hello()

    def lanes(value, n):
        value = value.astype(F32)
        if value.shape[1] == n:
            return value
        return jnp.concatenate([value, jnp.zeros((value.shape[0], n - value.shape[1]), F32)], axis=1)

    def folded(value, n):
        both = jnp.concatenate([value[: PACK // 2], value[PACK // 2 :]], axis=1)
        return lanes(both, 128).astype(BF16)

    def unfolded(value, n):
        return jnp.concatenate([value[:, :n], value[:, n : 2 * n]], axis=0)

    rows = [wproj[...], wstep[...], alog[...], convw[...]]
    rows += [v[...].reshape(1, el) for v in (convb, stepb, skipg)]
    rows = [v.astype(F32) for v in rows]
    rows.append(jnp.zeros((PACK - GAIN_ROW, el), F32))
    pack = jnp.concatenate(rows, axis=0)
    mine = jnp.where(y == 0, pack[:, :hl], pack[:, hl:])
    own_gain = gain[...].reshape(1, piece).astype(F32)
    rowid = lax.broadcasted_iota(jnp.int32, (PACK, 1), 0)
    b.pka[f] = folded(jnp.where(rowid == GAIN_ROW, own_gain, mine), hl)
    wint = win[...].T
    b.wt[0, f] = jnp.where(y == 0, wint[:hl], wint[hl:])
    t32 = tok[...].astype(F32)
    inv = lax.rsqrt(jnp.mean(t32 * t32, axis=1, keepdims=True) + EPS)
    b.nb[q0, c] = (t32 * inv).astype(BF16)

    if line:
        for w in range(3):
            for k in (1, 3):

                @pl.when(far_from(k))
                def _():
                    b.gwl[w, k - 1] = jnp.zeros((hl, width), BF16)

        for k in (1, 3):

            @pl.when(far_from(k))
            def _():
                b.sgl[k - 1] = jnp.zeros((PACK // 2, 128), BF16)

        pl.semaphore_wait(barrier, jnp.where(ends, 5, 6))
    else:
        pl.semaphore_wait(barrier, 2 + depth)

    def plane_start(buf):
        upper, lower = buf.at[q0, c, pl.ds(0, half)], buf.at[q0, c, pl.ds(half, half)]
        ax = same(upper, xpeer)
        by = same(lower, ypeer)
        bx = same(lower, xpeer)
        ay = same(upper, ypeer)
        oo = same(buf.at[q0, c], core)
        return ax, by, bx, ay, oo

    def plane_forward(buf, cps):
        ax, by, bx, ay, oo = cps
        ax.wait_recv()
        fa = same(buf.at[qx, c, pl.ds(0, half)], ypeer)
        by.wait_recv()
        fb = same(buf.at[qy, c, pl.ds(half, half)], xpeer)
        return bx, ay, oo, fa, fb

    def plane_core(buf, cps):
        bx, ay, oo, fa, fb = cps
        bx.wait_recv()
        ox = same(buf.at[qx, c], core)
        ay.wait_recv()
        oy = same(buf.at[qy, c], core)
        return oo, ox, oy, fa, fb

    def plane_last(buf, cps):
        oo, ox, oy, fa, fb = cps
        arrive([fa, fb])
        return oo, ox, oy, same(buf.at[qd, c], core)

    zsmall = z_gather(lambda q: b.pka.at[q])
    zin = z_gather(lambda q: b.wt.at[0, q])
    nstate = plane_start(b.nb)

    wgt = wg[...].T
    b.wt[1, f] = jnp.where(y == 0, wgt[:hl], wgt[hl:])
    b.wt[2, f] = wo[pl.ds(y * hl, hl), :]
    rowid = lax.broadcasted_iota(jnp.int32, (SLOT, 1), 0)
    b.db[q0, c] = jnp.where(rowid < lens[0], cot[...].astype(F32), 0.0).astype(BF16)
    z_relay(zsmall)
    nstate = plane_forward(b.nb, nstate)
    z_relay(zin)
    z_arrive(zsmall)
    locs = [unfolded(b.pka[i].astype(F32), hl) for i in range(depth)]
    pkl = jnp.concatenate(locs, axis=1)
    b.pkl[...] = pkl
    b.gb[c, x] = jnp.broadcast_to(pkl[GAIN_ROW : GAIN_ROW + 1], (8, cols))
    gx = same(b.gb.at[c, x], xpeer)
    dstate = plane_start(b.db)
    b.wst[...] = jnp.concatenate(
        [pkl[STEP_ROW:LOG_ROW], jnp.zeros((128 - RANK, cols), F32)], axis=0
    ).astype(BF16)
    b.wpt[...] = jnp.concatenate([pkl[:PROJ], jnp.zeros((128 - PROJ, cols), F32)], axis=0).astype(BF16)
    for n in range(STATE):
        row = -jnp.exp(pkl[LOG_ROW + n : LOG_ROW + n + 1]) * (1.0 / LN2)
        for et in range(2):
            b.rate[n, et] = jnp.broadcast_to(row[:, et * 128 : et * 128 + 128], (8, 128))
    nstate = plane_core(b.nb, nstate)
    b.ip[:, 0:8, :] = jnp.zeros((8, 8, cols), F32)
    b.dcp[:, SLOT : SLOT + 8, :] = jnp.zeros((8, 8, cols), F32)
    b.ga[...] = jnp.zeros((STATE, 2, 8, 128), F32)
    b.sall[0] = jnp.zeros((STATE, 2, 16, 128), BF16)
    b.sg[...] = jnp.zeros((PACK, cols), F32)
    source = lax.broadcasted_iota(jnp.int32, (256, 2 * STATE * 128), 0)
    target = lax.broadcasted_iota(jnp.int32, (256, 2 * STATE * 128), 1)
    b.sel[...] = jnp.where(lax.rem(source, 128) == RANK + target // 128, 1.0, 0.0).astype(BF16)
    gx.wait_recv()
    gc = same(b.gb.at[c], core)
    gc.wait_recv()
    pieces = []
    for i in range(depth):
        for j in range(2):
            for k in range(2):
                pieces.append(b.gb[k, j, 0:1, i * piece : (i + 1) * piece])
    b.gl[...] = jnp.concatenate(pieces, axis=1)

    z_arrive(zin)
    zgate = z_gather(lambda q: b.wt.at[1, q])
    zout = z_gather(lambda q: b.wt.at[2, q])

    def scaled(w):
        full = b.wt[w].reshape(cols, width).astype(F32)
        b.ws[w] = (full * b.gl[...]).astype(BF16)

    scaled(0)
    arrive(plane_last(b.nb, nstate))

    def row_of(i):
        return b.pkl[i : i + 1, :]

    taps = [row_of(TAP_ROW + k) for k in range(CONV)]
    cbias = row_of(CONV_ROW)
    sbias = row_of(BIAS_ROW)
    skip = row_of(SKIP_ROW)

    def slot_rows(j):
        return pl.ds(pl.multiple_of(j * SLOT, SLOT), SLOT)

    def pair(ref, at):
        return jnp.concatenate([ref[0, at, :], ref[1, at, :]], axis=1)

    def unpair(ref, at, value):
        ref[0, at, :] = value[:, :128]
        ref[1, at, :] = value[:, 128:]

    def convolved(j, begin, size):
        acc = jnp.broadcast_to(cbias, (size, cols))
        for k in range(CONV):
            acc = acc + taps[k] * b.ip[j, 5 + k + begin : 5 + k + begin + size, :]
        return acc

    b.ip[:, 8 : 8 + SLOT, :] = nt(b.nb[...].reshape(count, width), b.ws[0]).reshape(8, SLOT, cols)

    @pl.loop(0, 8)
    def _(j):
        acc = convolved(j, 0, SLOT)
        out = acc * sigmoid(acc)
        unpair(b.xc, slot_rows(j), out)
        b.cl[j] = out.astype(BF16)

    b.pp[...] = nt(b.cl[...].reshape(count, cols), b.wpt[...]).reshape(4, 2, SLOT, 128)

    def all_reduce(which, rows):
        g = sets[which]
        flight = []

        def first():
            g.s1[...] = b.pp[:, oc, rows, :].astype(BF16)
            flight[:] = [rcopy(g.s1, g.l1, core)]

        def second():
            arrive(flight)
            total = b.pp[:, c, rows, :] + g.l1[...].astype(F32)
            g.s2[...] = total.astype(BF16)
            flight[:] = [
                rcopy(g.s2.at[pl.ds(0, 2)], g.l2.at[pl.ds(0, 2)], xpeer),
                rcopy(g.s2.at[pl.ds(2, 2)], g.l2.at[pl.ds(2, 2)], ypeer),
            ]
            g.own[...] = total

        def third():
            arrive(flight)
            total = g.own[...] + g.l2[...].astype(F32)
            g.s3[...] = total.astype(BF16)
            flight[:] = [
                rcopy(g.s3.at[pl.ds(0, 2)], g.l3.at[pl.ds(0, 2)], ypeer),
                rcopy(g.s3.at[pl.ds(2, 2)], g.l3.at[pl.ds(2, 2)], xpeer),
            ]
            g.own[...] = total

        def fourth():
            arrive(flight)
            g.own[...] = g.own[...] + g.l3[...].astype(F32)
            flight[:] = [rcopy(g.own, g.oth, core)]

        return [first, second, third, fourth, lambda: arrive(flight)]

    def cut_of(h):
        return slice(h * half, h * half + half)

    def half_rows(j, h):
        return pl.ds(pl.multiple_of(j * SLOT + h * half, half), half)

    def packed_rows(j, h):
        return pl.ds(pl.multiple_of(h * 8 * half + j * half, half), half)

    front = all_reduce(1, cut_of(0))
    back = all_reduce(5, cut_of(1))
    for k in range(3):
        front[k]()
        back[k]()
    dstate = plane_forward(b.db, dstate)
    z_relay(zgate)
    front[3]()
    back[3]()
    dstate = plane_core(b.db, dstate)
    front[4]()

    def scan_inputs(which, h):
        @pl.loop(0, 4)
        def _(q):
            for cc, src in ((c, sets[which].own), (oc, sets[which].oth)):
                j = 2 * q + cc
                proj = src[q]
                b.tm[pl.ds(h * 8 * half + j, half, stride=8), :] = proj
                b.slow[j, cut_of(h), :] = proj.astype(BF16)

        span = slice(h * 8 * half, (h + 1) * 8 * half)
        b.t1[span, :] = nn(b.slow[:, cut_of(h), :].reshape(8 * half, 128), b.wst[...])

        @pl.loop(0, 8)
        def _(j):
            pre = b.t1[packed_rows(j, h), :] + sbias
            unpair(b.dt, half_rows(j, h), jnp.maximum(pre, 0.0) + jnp.log1p(jnp.exp(-jnp.abs(pre))))

        tm = b.tm[span, :]
        high = tm.astype(BF16)
        spread = jnp.concatenate([high, (tm - high.astype(F32)).astype(BF16)], axis=1)
        both = nn(spread, b.sel[...])
        for i in range(2 * STATE):
            b.bc[cut_of(h), i] = both[:, i * 128 : i * 128 + 128].reshape(half, 8, 128)

    zero = jnp.zeros((8, 128), F32)

    steps = 4

    def forward_steps(j, carry):
        base = steps * j
        ats = [pl.ds(base + i, 8, stride=SLOT) for i in range(steps)]
        size = [[b.dt[e, at, :] for e in range(2)] for at in ats]
        push = [[size[i][e] * b.xc[e, ats[i], :] for e in range(2)] for i in range(steps)]
        out = [[zero, zero] for _ in range(steps)]
        for n in range(STATE):
            for e in range(2):
                rate = b.rate[n, e]
                state = b.carried[n, e]
                kept = []
                for i in range(steps):
                    state = jnp.exp2(size[i][e] * rate) * state + push[i][e] * b.bc[base + i, n]
                    out[i][e] = out[i][e] + b.bc[base + i, STATE + n] * state
                    kept.append(state)
                b.carried[n, e] = state
                for p in range(steps // 2):
                    both_states = jnp.concatenate(kept[2 * p : 2 * p + 2], axis=0)
                    b.sall[(steps // 2) * j + p + 1, n, e] = both_states.astype(BF16)
        for i in range(steps):
            for e in range(2):
                b.ys[e, ats[i], :] = out[i][e]
        return carry

    b.carried[...] = jnp.zeros((STATE, 2, 8, 128), F32)
    scan_inputs(1, 0)
    lax.fori_loop(0, half // steps, forward_steps, 0)
    z_relay(zout)
    back[4]()
    scan_inputs(5, 1)
    dstate = plane_last(b.db, dstate)
    lax.fori_loop(half // steps, SLOT // steps, forward_steps, 0)

    arrive(dstate)
    z_arrive(zgate)
    scaled(1)
    b.t1[...] = nt(b.nb[...].reshape(count, width), b.ws[1])
    z_arrive(zout)
    b.t2[...] = nt(b.db[...].reshape(count, width), b.wt[2].reshape(cols, width))

    @pl.loop(0, 4)
    def _(q):
        for cc in range(2):
            at = slot_rows(2 * q + cc)
            gpre = b.t1[at, :]
            dgat = b.t2[at, :]
            conv = pair(b.xc, at)
            mixed = pair(b.ys, at) + skip * conv
            sig = sigmoid(gpre)
            act = gpre * sig
            b.go[q, cc] = (mixed * act).astype(BF16)
            dmix = dgat * act
            unpair(b.dm, at, dmix)
            slope = sig * (1.0 + gpre * (1.0 - sig))
            b.dg[q, cc] = (dgat * mixed * slope).astype(BF16)
            b.sg[SKIP_ROW : SKIP_ROW + 1, :] += jnp.sum(dmix * conv, axis=0, keepdims=True)

    def reduce_begin(dots, more):
        g = sets[3]

        def low_of(value, q):
            return (value + g.s1[q].astype(F32) if more else value).astype(BF16)

        g.s1[qd] = low_of(dots(lambda ref: ref[qd, oc]), qd)
        cores = [rcopy(g.s1.at[qd], g.l1.at[qd], core)]
        others = (qx, qy, q0)
        rest = dots(lambda ref: jnp.concatenate([ref[q, oc] for q in others], axis=0))
        for k, q in enumerate(others):
            g.s1[q] = low_of(rest[k * SLOT : (k + 1) * SLOT], q)
            cores.append(rcopy(g.s1.at[q], g.l1.at[q], core))
        mine = dots(lambda ref: ref[:, c].reshape(4 * SLOT, cols)).reshape(4, SLOT, width)
        b.sum[...] = b.sum[...] + mine if more else mine
        return cores

    def reduce_second(cores):
        g = sets[3]

        def chip(q, rows):
            return (b.sum[q, rows, :] + g.l1[q, rows, :].astype(F32)).astype(BF16)

        cores[0].wait_recv()
        g.sx[1] = chip(qd, top)
        x1 = rcopy(g.sx.at[1], g.lx.at[1], xpeer)
        g.sy[1] = chip(qd, low)
        y1 = rcopy(g.sy.at[1], g.ly.at[1], ypeer)
        cores[1].wait_recv()
        g.sx[0] = chip(qx, top)
        x0 = rcopy(g.sx.at[0], g.lx.at[0], xpeer)
        cores[2].wait_recv()
        g.sy[0] = chip(qy, low)
        y0 = rcopy(g.sy.at[0], g.ly.at[0], ypeer)
        return x1, y1, x0, y0

    def reduce_third(cps):
        g = sets[3]
        x1, y1, x0, y0 = cps
        x1.wait_recv()
        g.ty[...] = (b.sum[qy, top, :] + g.l1[qy, top, :].astype(F32) + g.lx[1].astype(F32)).astype(BF16)
        c1 = rcopy(g.ty, g.my, ypeer)
        y1.wait_recv()
        g.tx[...] = (b.sum[qx, low, :] + g.l1[qx, low, :].astype(F32) + g.ly[1].astype(F32)).astype(BF16)
        c2 = rcopy(g.tx, g.mx, xpeer)
        return x0, y0, c1, c2

    def reduce_end(cores, cps, out):
        g = sets[3]
        cores[3].wait_recv()
        arrive(cps)
        for rows, near, far_ref in ((top, g.lx, g.my), (low, g.ly, g.mx)):
            out[rows, :] = (
                b.sum[q0, rows, :]
                + g.l1[q0, rows, :].astype(F32)
                + near[0].astype(F32)
                + far_ref[...].astype(F32)
            ).astype(BF16)

    def weight_grad(w, grad, gained):
        b.gws[w] = (grad * b.gl[...] if gained else grad).astype(BF16).reshape(depth, hl, width)
        return grad

    def rows_grad(lhs, rhs):
        return tn(lhs[...].reshape(count, cols), rhs[...].reshape(count, width))

    def gain_grad(w, grad):
        return jnp.sum(grad * b.wt[w].reshape(cols, width).astype(F32), axis=0, keepdims=True)

    def weight_send(w, at):
        return z_scatter(
            lambda q: b.gws.at[w, q, at], lambda k: b.gwl.at[w, k, at], b.gwx.at[w, at]
        )

    def weight_sum(w, st, at):
        gout[w, y, at, :] = z_sum(st, b.gws[w, f, at, :].astype(F32)).astype(BF16)
        return same(gout.at[w, y, at], ypeer)

    every = pl.ds(0, hl)

    weight_grad(2, rows_grad(b.go, b.db), False)
    zgo = z_direct(weight_send(2, every))
    grad = weight_grad(1, rows_grad(b.dg, b.nb), True)
    zgg = z_direct(weight_send(1, every))
    b.vv[...] = gain_grad(1, grad)
    bone = reduce_begin(lambda pick: nn(pick(b.go), b.wt[2].reshape(cols, width)), False)

    def backward_pair(j, carry):
        k = SLOT // 2 - 1 - j
        ats = [pl.ds(2 * k + i, 8, stride=SLOT) for i in range(2)]
        size = [[b.dt[e, at, :] for e in range(2)] for at in ats]
        conv = [[b.xc[e, at, :] for e in range(2)] for at in ats]
        dmix = [[b.dm[e, at, :] for e in range(2)] for at in ats]
        push = [jnp.concatenate([size[i][e] * conv[i][e] for i in range(2)], axis=0).astype(BF16) for e in range(2)]
        dlow = [jnp.concatenate([dmix[i][e] for i in range(2)], axis=0).astype(BF16) for e in range(2)]
        rate_sum = [[zero, zero], [zero, zero]]
        weighted = [[zero, zero], [zero, zero]]
        new = []
        for n in range(STATE):
            inm = [b.bc[2 * k + i, n] for i in range(2)]
            outm = [b.bc[2 * k + i, STATE + n] for i in range(2)]
            dins, douts = [], []
            for e in range(2):
                rate = b.rate[n, e]
                here = b.sall[k + 1, n, e]
                before = [b.sall[k, n, e].astype(F32)[8:16], here.astype(F32)[0:8]]
                back = carry[2 * n + e]
                lams = [None, None]
                acc = b.ga[n, e]
                for i in (1, 0):
                    lam = outm[i] * dmix[i][e] + back
                    back = jnp.exp2(size[i][e] * rate) * lam
                    grad = back * before[i]
                    rate_sum[i][e] = rate_sum[i][e] + grad * rate
                    weighted[i][e] = weighted[i][e] + lam * inm[i]
                    acc = acc + grad * size[i][e]
                    lams[i] = lam
                b.ga[n, e] = acc
                new.append(back)
                dins.append(jnp.concatenate(lams, axis=0).astype(BF16) * push[e])
                douts.append(dlow[e] * here)
            b.sall[k + 1, n, 0] = dins[0] + dins[1]
            b.sall[k + 1, n, 1] = douts[0] + douts[1]
        for i in range(2):
            for e in range(2):
                b.ys[e, ats[i], :] = rate_sum[i][e] * LN2 + conv[i][e] * weighted[i][e]
                b.xc[e, ats[i], :] = size[i][e] * weighted[i][e]
        return tuple(new)

    carry = tuple(zero for _ in range(2 * STATE))
    carry = lax.fori_loop(0, SLOT // 16, backward_pair, carry, unroll=2)
    btwo = reduce_second(bone)
    carry = lax.fori_loop(SLOT // 16, 3 * SLOT // 16, backward_pair, carry, unroll=2)
    z_absorb(zgo)
    bthree = reduce_third(btwo)
    carry = lax.fori_loop(3 * SLOT // 16, SLOT // 4, backward_pair, carry, unroll=2)

    def map_sums(h):
        begin = 1 + h * half // 2
        parts = [
            b.sall[begin : begin + half // 2, n, k].reshape(8 * half, 128) for k in range(2) for n in range(STATE)
        ]
        b.tm[h * 8 * half : (h + 1) * 8 * half, :] = nt(jnp.concatenate(parts, axis=1), b.sel[0:128, :])

    def rank_part(h):
        span = slice(h * 8 * half, (h + 1) * 8 * half)
        b.t1[span, :] = nn(b.slow[:, cut_of(h), :].reshape(8 * half, 128), b.wst[...])

        @pl.loop(0, 8)
        def _(j):
            dpre = pair(b.ys, half_rows(j, h)) * sigmoid(b.t1[packed_rows(j, h), :] + sbias)
            b.sg[BIAS_ROW : BIAS_ROW + 1, :] += jnp.sum(dpre, axis=0, keepdims=True)
            b.dsl[j, cut_of(h), :] = dpre.astype(BF16)

        rank = nt(b.dsl[:, cut_of(h), :].reshape(8 * half, cols), b.wst[...])
        for j in range(8):
            maps = b.tm[pl.ds(h * 8 * half + j, half, stride=8), :]
            b.pp[j // 2, j % 2, cut_of(h), :] = rank[j * half : (j + 1) * half] + maps

    def slopes(h):
        @pl.loop(0, 8)
        def _(j):
            at = half_rows(j, h)
            cpre = convolved(j, h * half, half)
            sig = sigmoid(cpre)
            b.t2[at, :] = sig * (1.0 + cpre * (1.0 - sig))
            unpair(b.dm, at, pair(b.xc, at) + pair(b.dm, at) * skip)

    def inner_part(which, h):
        @pl.loop(0, 4)
        def _(q):
            for cc, src in ((c, sets[which].own), (oc, sets[which].oth)):
                b.dpj[2 * q + cc, cut_of(h), :] = src[q].astype(BF16)

        span = slice(h * 8 * half, (h + 1) * 8 * half)
        b.t1[span, :] = nn(b.dpj[:, cut_of(h), :].reshape(8 * half, 128), b.wpt[...])

        @pl.loop(0, 4)
        def _(q):
            for cc in range(2):
                j = 2 * q + cc
                at = half_rows(j, h)
                dpre = (pair(b.dm, at) + b.t1[packed_rows(j, h), :]) * b.t2[at, :]
                b.dcp[j, cut_of(h), :] = dpre
                sums = []
                for k in range(CONV):
                    begin = 5 + k + h * half
                    sums.append(jnp.sum(dpre * b.ip[j, begin : begin + half, :], axis=0, keepdims=True))
                sums.append(jnp.sum(dpre, axis=0, keepdims=True))
                b.sg[TAP_ROW : CONV_ROW + 1, :] += jnp.concatenate(sums, axis=0)
                dinner = taps[CONV - 1] * dpre
                for k in range(CONV - 1):
                    begin = CONV - 1 - k + h * half
                    dinner = dinner + taps[k] * b.dcp[j, begin : begin + half, :]
                b.di[q, cc, cut_of(h), :] = dinner.astype(BF16)

    def inner_grad(h):
        return tn(
            b.di[:, :, cut_of(h), :].reshape(8 * half, cols), b.nb[:, :, cut_of(h), :].reshape(8 * half, width)
        )

    map_sums(1)
    rank_part(1)
    later = all_reduce(2, cut_of(1))
    later[0]()
    marks = [SLOT // 4 + v for v in (0, 8, 26, SLOT // 4)]
    for k in range(3):
        carry = lax.fori_loop(marks[k], marks[k + 1], backward_pair, carry, unroll=2)
        if k < 2:
            later[k + 1]()
    z_absorb(zgg)
    map_sums(0)
    rank_part(0)
    later[3]()
    sooner = all_reduce(4, cut_of(0))
    sooner[0]()
    later[4]()
    slopes(1)
    sooner[1]()
    inner_part(2, 1)
    reduce_end(bone, bthree, bsum)
    sooner[2]()
    hold = [weight_sum(2, zgo, every)]
    slopes(0)
    b.gacc[...] = inner_grad(1)
    settle([*bone, *btwo, *bthree[2:]])
    gate_dot = lambda ref: nn(ref.reshape(4 * SLOT, cols), b.ws[1]).reshape(4, SLOT, width)
    sets[3].s1[...] = gate_dot(b.dg[:, oc]).astype(BF16)
    b.sum[...] = gate_dot(b.dg[:, c])
    sooner[3]()
    hold.append(weight_sum(1, zgg, every))
    sooner[4]()
    inner_part(4, 0)

    grad = weight_grad(0, b.gacc[...] + inner_grad(0), True)
    first, second = pl.ds(0, hl // 2), pl.ds(hl // 2, hl // 2)
    zgi = [weight_send(0, first), weight_send(0, second)]
    for st in zgi:
        z_direct(st)
    total = b.vv[...] + gain_grad(0, grad)
    for i in range(8):
        b.vs[0, i : i + 1, :] = total[:, i * 128 : i * 128 + 128]
    v1 = rcopy(b.vs.at[0], b.vl.at[0], xpeer)
    done = reduce_begin(lambda pick: nn(pick(b.di), b.ws[0]), True)
    v1.wait_recv()
    b.vs[1] = b.vs[0] + b.vl[0]
    v2 = rcopy(b.vs.at[1], b.vl.at[1], ypeer)
    dtwo = reduce_second(done)
    z_absorb(zgi[0])
    for n in range(STATE):
        parts = [jnp.sum(b.ga[n, e] * b.rate[n, e], axis=0, keepdims=True) for e in range(2)]
        b.sg[LOG_ROW + n : LOG_ROW + n + 1, :] = jnp.concatenate(parts, axis=1) * LN2
    grad = tn(b.dpj[...].reshape(count, 128), b.cl[...].reshape(count, cols))
    b.sg[0:PROJ, :] = grad[:PROJ]
    grad = tn(b.slow[...].reshape(count, 128), b.dsl[...].reshape(count, cols))
    b.sg[STEP_ROW:LOG_ROW, :] = grad[:RANK]
    for i in range(depth):
        b.sgs[i] = folded(b.sg[:, i * hl : (i + 1) * hl], hl)
    z_absorb(zgi[1])
    zgs = z_direct(z_scatter(lambda q: b.sgs.at[q], lambda k: b.sgl.at[k], b.sgx))
    v2.wait_recv()
    b.vs[2] = b.vs[1] + b.vl[1]
    v3 = rcopy(b.vs.at[2], b.vl.at[2], core)
    dthree = reduce_third(dtwo)
    v3.wait_recv()
    b.vz[f] = b.vs[2] + b.vl[2]
    v4 = z_gather(lambda q: b.vz.at[q])
    yin = [weight_sum(0, zgi[0], first)]
    z_absorb(zgs)
    yin.append(weight_sum(0, zgi[1], second))
    sout[y] = z_sum(zgs, b.sgs[f].astype(F32)).astype(BF16)
    ysmall = same(sout.at[y], ypeer)
    z_relay(v4)
    reduce_end(done, dthree, dsc)
    z_arrive(v4)
    total = b.vz[0]
    for k in range(1, depth):
        total = total + b.vz[k]
    vout[...] = total
    arrive(hold + yin + [ysmall])
    for cp in started:
        cp.wait_send()


def last_kernel(hl, piece, tok, cot, lens, bsum, dsc, gout, sout, vout, *outs):
    (out, dtok, ggain, ginner, ggate, gconv, gcb, gproj, gstep, gsb, glog, gskip, gwout) = outs
    s = lax.axis_index("shard")
    t32 = tok[...].astype(F32)
    rowid = lax.broadcasted_iota(jnp.int32, (SLOT, 1), 0)
    out[...] = (t32 + jnp.where(rowid < lens[0], bsum[...].astype(F32), 0.0)).astype(BF16)
    inv = lax.rsqrt(jnp.mean(t32 * t32, axis=1, keepdims=True) + EPS)
    ds = dsc[...].astype(F32)
    mean = jnp.mean(ds * t32, axis=1, keepdims=True)
    dtok[...] = cot[...].astype(F32) + inv * ds - t32 * (inv * inv * inv * mean)
    width = tok.shape[1]
    el = 2 * hl
    ginner[...] = gout[0].reshape(el, width).T.astype(F32)
    ggate[...] = gout[1].reshape(el, width).T.astype(F32)
    gwout[...] = gout[2].reshape(el, width).astype(F32)
    small = sout[...].astype(F32)
    halves = [jnp.concatenate([small[k][:, :hl], small[k][:, hl:el]], axis=0) for k in range(2)]
    both = jnp.concatenate(halves, axis=1)
    gproj[...] = both[:PROJ]
    gstep[...] = both[STEP_ROW:LOG_ROW]
    glog[...] = both[LOG_ROW:TAP_ROW]
    gconv[...] = both[TAP_ROW:CONV_ROW]
    gcb[...] = both[CONV_ROW : CONV_ROW + 1].reshape(el)
    gsb[...] = both[BIAS_ROW : BIAS_ROW + 1].reshape(el)
    gskip[...] = both[SKIP_ROW : SKIP_ROW + 1].reshape(el)
    per = 128 // piece
    vec = vout[...]
    rows = lax.broadcasted_iota(jnp.int32, (8, 128), 0)
    row = jnp.sum(jnp.where(rows == s // per, vec, 0.0), axis=0, keepdims=True)
    pick = jnp.zeros((1, piece), F32)
    for i in range(per):
        pick = jnp.where(lax.rem(s, per) == i, row[:, i * piece : (i + 1) * piece], pick)
    ggain[...] = pick.reshape(piece)


def make_local(replicas, shards):
    depth = shards // 4

    def local(
        tokens, norm_gain, w_inner, w_gate, conv_weight, conv_bias, w_proj, w_step, step_bias, a_log, skip_gain,
        w_out, cotangent, lengths,
    ):
        width = tokens.shape[1]
        el = w_inner.shape[1]
        hl = el // 2
        piece = norm_gain.shape[0]
        spec = buffers(depth, hl, width, shards, piece)
        nsem = 96 + 16 * depth
        vm = pl.BlockSpec(memory_space=pltpu.VMEM)
        sm = pl.BlockSpec(memory_space=pltpu.SMEM)
        sds = jax.ShapeDtypeStruct
        mid = pl.pallas_call(
            functools.partial(main_kernel, [tuple(group) for group in spec], depth, hl, piece, nsem),
            out_shape=(
                pltpu.VMEM((SLOT, width), BF16),
                pltpu.VMEM((SLOT, width), BF16),
                pltpu.VMEM((3, 2, hl, width), BF16),
                pltpu.VMEM((2, PACK // 2, 128), BF16),
                pltpu.VMEM((8, 128), F32),
            ),
            in_specs=[vm] * 13 + [sm],
            out_specs=(vm,) * 5,
            scratch_shapes=[pltpu.VMEM(shape, kind) for group in spec for shape, kind in group.values()]
            + [pltpu.SemaphoreType.DMA((nsem,)), pltpu.SemaphoreType.DMA((nsem,))],
            compiler_params=pltpu.CompilerParams(
                collective_id=0, has_side_effects=True, vmem_limit_bytes=61 << 20
            ),
            name="layer",
        )(
            tokens, cotangent, w_inner, w_gate, w_out, w_proj.T, w_step, a_log, conv_weight, conv_bias, step_bias,
            skip_gain, norm_gain, lengths,
        )
        bsum, dsc, gout, sout, vout = mid
        if replicas > 2:
            groups = [[r for r in range(replicas) if r % 2 == k] for k in range(2)]
            gout, sout, vout = (
                lax.psum(v.astype(F32), "replica", axis_index_groups=groups) for v in (gout, sout, vout)
            )
        outs = pl.pallas_call(
            functools.partial(last_kernel, hl, piece),
            out_shape=(
                sds((SLOT, width), BF16),
                sds((SLOT, width), F32),
                sds((piece,), F32),
                sds((width, el), F32),
                sds((width, el), F32),
                sds((CONV, el), F32),
                sds((el,), F32),
                sds((PROJ, el), F32),
                sds((RANK, el), F32),
                sds((el,), F32),
                sds((STATE, el), F32),
                sds((el,), F32),
                sds((el, width), F32),
            ),
            in_specs=[vm, vm, sm] + [vm] * 5,
            out_specs=(vm,) * 13,
            compiler_params=pltpu.CompilerParams(vmem_limit_bytes=16 << 20),
            name="results",
        )(tokens, cotangent, lengths, bsum, dsc, gout, sout, vout)
        return outs[:7] + (outs[7].T,) + outs[8:]

    return local


def solution(mesh):
    return jax.shard_map(
        make_local(mesh.shape["replica"], mesh.shape["shard"]),
        mesh=mesh,
        in_specs=(
            P(("replica", "shard"), None),
            P("shard"),
            P(None, "shard"),
            P(None, "shard"),
            P(None, "shard"),
            P("shard"),
            P("shard", None),
            P(None, "shard"),
            P("shard"),
            P(None, "shard"),
            P("shard"),
            P("shard", None),
            P(("replica", "shard"), None),
            P(("replica", "shard")),
        ),
        out_specs=(
            P(("replica", "shard"), None),
            P(("replica", "shard"), None),
            P("shard"),
            P(None, "shard"),
            P(None, "shard"),
            P(None, "shard"),
            P("shard"),
            P("shard", None),
            P(None, "shard"),
            P("shard"),
            P(None, "shard"),
            P("shard"),
            P("shard", None),
        ),
        check_vma=False,
    )
```
